32 devices in a mesh: dp: 8 (over y, x, core), tensor: 4 (over z).
Axes of the slice: x: 2, y: 2, z: 4, core: 2. Of those that a mesh axis runs over, the one named last changes fastest.
Arguments:
- tokens: bfloat16 [16384, 1536], P(('dp', 'tensor')), may hold values from -6 to 6
- perm: int32 [16384], P('dp'), may hold values from 0 to 16383, as said below
- routes: int32 [16384, 4], P('dp'), may hold values from 0 to 7, all different within a row
- gates: bfloat16 [16384, 4], P(('dp', 'tensor')), may hold values from 0.049804688 to 0.5
- lengths: int32 [8, 4], P('dp'), may hold values from 1 to 1024, 2048 in all within a row
- cotangent: bfloat16 [16384, 1536], P(('dp', 'tensor')), may hold values from -6 to 6
- gain_attn: float32 [1536], replicated, may hold values from 0.5 to 1.5
- w_query: bfloat16 [1536, 1536], P(None, 'tensor'), may hold values from -0.15625 to 0.15625
- w_keyval: bfloat16 [1536, 512], replicated, may hold values from -0.15625 to 0.15625
- w_out: bfloat16 [1536, 1536], P('tensor'), may hold values from -1.5 to 1.5
- gain_moe: float32 [1536], replicated, may hold values from 0.5 to 1.5
- w_gate: bfloat16 [8, 1536, 768], P(None, None, 'tensor'), may hold values from -0.15625 to 0.15625
- w_up: bfloat16 [8, 1536, 768], P(None, None, 'tensor'), may hold values from -0.15625 to 0.15625
- w_down: bfloat16 [8, 768, 1536], P(None, 'tensor'), may hold values from -0.21875 to 0.21875
Outputs:
- outputs: bfloat16 [16384, 1536], P(('dp', 'tensor'))
- grad_tokens: bfloat16 [16384, 1536], P(('dp', 'tensor'))
- grad_gain_attn: float32 [1536], P('dp')
- grad_query: float32 [1536, 1536], P('dp', 'tensor')
- grad_keyval: float32 [1536, 512], P('dp')
- grad_out: float32 [1536, 1536], P('tensor', 'dp')
- grad_gain_moe: float32 [1536], P('dp')
- grad_gate: float32 [8, 1536, 768], P(None, 'dp', 'tensor')
- grad_up: float32 [8, 1536, 768], P(None, 'dp', 'tensor')
- grad_down: float32 [8, 768, 1536], P(None, 'tensor', 'dp')
The draws below stay inside these ranges and needn't reach their ends.
Inputs may be any that keep to these rules, and one draw needn't show every extreme that they name: `perm`: each value once. The 512 rows of aligned block b go to blocks b' with b' % 4 == b % 4, exactly 64 rows to each such block, where block b' holds rows b' * 512 to (b' + 1) * 512 - 1 of the dealt order.
All inputs are finite; a program needn't handle non-finite values.
Results may differ from the reference program's by a relative error of at most 0.02.
Values may be sent and summed in bfloat16 or wider, within the bound.
A program may use at most 448 MiB of HBM per device.

```python
import math
import jax
import jax.numpy as jnp
import numpy as np
from jax import lax

D = 1536
H = 12
KVH = 2
HD = 128
FF = 768
TOP = 4
E = 8
ROWS = 512
SEQS = 4
BQ = 512
TOK = 2048
SEQ_MAX = 1024
Q = 64
C = 1152
TOKENS = 16384
N_DP = 8
N_TENSOR = 4


def draw_perm(key, part):
    block_count = N_DP * N_TENSOR
    first_keys = jax.random.split(jax.random.fold_in(key, 11), block_count)
    second_keys = jax.random.split(jax.random.fold_in(key, 12), block_count)
    first_perm = jax.vmap(lambda one_key: jax.random.permutation(one_key, ROWS))(first_keys).reshape(N_DP, N_TENSOR, ROWS).astype(jnp.int32)
    second_perm = jax.vmap(lambda one_key: jax.random.permutation(one_key, ROWS))(second_keys).reshape(N_DP, N_TENSOR, ROWS).astype(jnp.int32)
    source_dp = jnp.arange(N_DP, dtype=jnp.int32)[:, None, None]
    quarter = jnp.arange(N_TENSOR, dtype=jnp.int32)[None, :, None] + jnp.zeros((N_DP, 1, ROWS), jnp.int32)
    dest_dp = (first_perm // Q).astype(jnp.int32)
    arrival = (source_dp * Q + first_perm % Q).astype(jnp.int32)
    local_row = second_perm[dest_dp, quarter, arrival].astype(jnp.int32)
    result = (dest_dp * N_TENSOR + quarter) * ROWS + local_row
    return result.reshape(-1).astype(jnp.int32)


def shard_levels(rng, extent, cuts, low, largest):
    factor_of, own = 1.0, jax.random.fold_in(rng, 6)
    for axis_at, parts in cuts:
        heights = jnp.exp(jax.random.uniform(jax.random.fold_in(own, axis_at), (parts,), jnp.float32, low / len(cuts), largest / len(cuts)))
        factor_of = factor_of * jnp.repeat(heights, extent[axis_at] // parts).reshape([-1 if axis == axis_at else 1 for axis in range(len(extent))])
    return factor_of


def distinct(key, rows, count, top, lift):
    sequence = jax.random.permutation(jax.random.fold_in(key, 1), count)
    boost = sequence
    for power in range(3):
        boost = boost * boost // count
    boost = boost * lift // count
    lots = jax.random.randint(jax.random.fold_in(key, 2), (rows, count), 0, 4096) + boost
    fixed_rows = jax.random.permutation(jax.random.fold_in(key, 3), rows)[jnp.arange(count) % rows]
    lots = jnp.where(jnp.arange(rows)[:, None] == fixed_rows[None, :], 1 << 14, lots)
    priority = lots * count + jnp.arange(count)
    return lax.top_k(priority.astype(jnp.int32), top)[1].astype(jnp.int32)


def profile(number_of, total, reach, lean):
    portions = [(1 << 20) // math.isqrt(grade ** lean) + 1 for grade in range(2, number_of + 1)]
    surplus, given = total - reach - (number_of - 1), [1] * (number_of - 1)
    while surplus > 0:
        movable = [i for i in range(number_of - 1) if given[i] < reach]
        pool, budget = sum([portions[i] for i in movable]), surplus
        for i in movable:
            addition = min(reach - given[i], max(1, budget * portions[i] // pool), surplus)
            given[i] = given[i] + addition
            surplus = surplus - addition
    return np.array([reach] + given)


def uneven_parts(own_key, amount, total, reach, skew):
    if amount == 2:
        one = jax.random.randint(own_key, (), max(1, total - reach), min(reach, total - 1) + 1)
        return jnp.stack([one, total - one])
    tallies = jnp.asarray(profile(amount, total, reach, skew), jnp.int32)
    couples = (amount - 1) // 2
    source_of, taker = tallies[1:1 + 2 * couples:2], tallies[2:2 + 2 * couples:2]
    margin = jnp.minimum(source_of - 1, reach - taker)
    shifted = jax.random.randint(jax.random.fold_in(own_key, 1), (couples,), 0, 1 << 20) % (margin + 1)
    tallies = tallies.at[1:1 + 2 * couples:2].set(source_of - shifted).at[2:2 + 2 * couples:2].set(taker + shifted)
    return tallies[jax.random.permutation(jax.random.fold_in(own_key, 2), amount)]


def gaussian(rng, extent, width, limit, shards=(), kind=jnp.bfloat16):
    values = jax.random.normal(rng, extent, jnp.float32) * width
    if len(shards) > 0:
        values = shard_levels(rng, extent, shards, -0.22, 0.18) * values
    return jnp.clip(values, min=-limit, max=limit).astype(kind)


def setup_inputs(seed: int = 0) -> dict:
    splits = jax.random.split(jax.random.key(seed), 15)
    return {
        "tokens": gaussian(splits[0], (TOKENS, D), 1.0, 6.0, ((0, 32),)),
        "perm": draw_perm(jax.random.fold_in(splits[14], 71), 0),
        "routes": distinct(splits[2], TOKENS, E, TOP, 4096),
        "gates": jnp.clip(0.049804688 + 0.4501953 * jax.random.uniform(splits[3], (TOKENS, TOP), jnp.float32) ** shard_levels(splits[3], (TOKENS, TOP), ((0, 32),), -0.2, 0.2), 0.049804688, 0.5).astype(jnp.bfloat16),
        "lengths": jax.vmap(lambda own: uneven_parts(own, SEQS, TOK, SEQ_MAX, 2))(jax.random.split(splits[4], N_DP)).reshape((N_DP, SEQS)).astype(jnp.int32),
        "cotangent": gaussian(splits[5], (TOKENS, D), 1.0, 6.0, ((0, 32),)),
        "gain_attn": jnp.clip(1.0 + 0.1 * jax.random.normal(splits[6], (D,), jnp.float32), 0.5, 1.5),
        "w_query": gaussian(splits[7], (D, H * HD), D ** -0.5, 0.15625, ((1, 4),)),
        "w_keyval": gaussian(splits[8], (D, 2 * KVH * HD), D ** -0.5, 0.15625),
        "w_out": gaussian(splits[9], (H * HD, D), (HD // 8) ** -0.5, 1.5, ((0, 4),)),
        "gain_moe": jnp.clip(1.0 + 0.1 * jax.random.normal(splits[10], (D,), jnp.float32), 0.5, 1.5),
        "w_gate": gaussian(splits[11], (E, D, FF), D ** -0.5, 0.15625, ((2, 4),)),
        "w_up": gaussian(splits[12], (E, D, FF), D ** -0.5, 0.15625, ((2, 4),)),
        "w_down": gaussian(splits[13], (E, FF, D), FF ** -0.5, 0.21875, ((1, 4),)),
    }


@jax.custom_vjp
def low(v):
    return lax.optimization_barrier(v.astype(jnp.bfloat16)).astype(jnp.float32)

@jax.custom_vjp
def low_back(v):
    return v

def low_keep(v):
    return (low(v), None)

def low_pass(kept, grad):
    return (grad,)

def back_keep(v):
    return (v, None)

def back_low(kept, grad):
    return (low(grad),)
low.defvjp(low_keep, low_pass)
low_back.defvjp(back_keep, back_low)
eps_norm = 1e-06
rope_base = 1000000.0
masked_score = -1e+30

def fine_dot(matrix_a, matrix_b):
    return jnp.dot(matrix_a, matrix_b, precision=lax.Precision.HIGHEST, preferred_element_type=jnp.float32)

def position_tables(seq_lengths, group_rows):
    row_ids = jnp.arange(group_rows, dtype=jnp.int32)
    seq_lengths = seq_lengths.astype(jnp.int32)
    seq_ends = jnp.cumsum(seq_lengths, dtype=jnp.int32).astype(jnp.int32)
    segment = lax.optimization_barrier(jnp.sum((row_ids[:, None] >= seq_ends[None, :]).astype(jnp.int32), axis=1, dtype=jnp.int32)).astype(jnp.int32)
    starts = (seq_ends - seq_lengths).astype(jnp.int32)
    seq_ids = jnp.arange(seq_lengths.shape[0], dtype=jnp.int32)
    first_row = lax.optimization_barrier(jnp.sum(jnp.where(segment[:, None] == seq_ids[None, :], starts[None, :], 0), axis=1, dtype=jnp.int32)).astype(jnp.int32)
    offset = (row_ids - first_row).astype(jnp.float32)
    half_dim = HD // 2
    frequency = rope_base ** (-2.0 * jnp.arange(half_dim, dtype=jnp.float32) / HD)
    angles = offset[:, None] * frequency[None, :]
    return (row_ids, segment, jnp.cos(angles)[:, None, :], jnp.sin(angles)[:, None, :])

def rotate(values, cosine_table, sine_table):
    half_dim = values.shape[-1] // 2
    first_half = values[..., :half_dim]
    second_half = values[..., half_dim:]
    return jnp.concatenate([first_half * cosine_table - second_half * sine_table, second_half * cosine_table + first_half * sine_table], axis=-1)

def group_forward(weights, inputs):
    gain_one, query_w, keyval_w, out_w, gain_two, gate_w, up_w, down_w = weights
    x_rows, route_rows, gate_rows, seq_lengths = inputs
    row_ids, segment, cosine_table, sine_table = position_tables(seq_lengths, TOK)
    score_scale = HD ** (-0.5)
    per_group = H // N_TENSOR
    inv_one = lax.rsqrt(lax.optimization_barrier(jnp.mean(x_rows * x_rows, axis=1, keepdims=True)) + eps_norm)
    normed_one = low(x_rows * inv_one * gain_one)
    queries = low(rotate(low_back(fine_dot(normed_one, query_w)).reshape(TOK, H, HD), cosine_table, sine_table))
    keyval = fine_dot(normed_one, keyval_w).reshape(TOK, 2, KVH, HD)
    key_list = []
    value_list = []
    for group_index in range(N_TENSOR):
        kv_head = group_index * per_group // (H // KVH)
        key_list.append(low(rotate(low_back(keyval[:, 0, kv_head:kv_head + 1]), cosine_table, sine_table))[:, 0])
        value_list.append(low(low_back(keyval[:, 1, kv_head])))
    keys_all = jnp.stack(key_list)
    values_all = jnp.stack(value_list)
    grouped = queries.reshape(TOK // BQ, BQ, N_TENSOR, per_group, HD)

    def attend(block_args):
        query_block, block_index = block_args
        block_start = (block_index * BQ).astype(jnp.int32)
        rows_q = block_start + jnp.arange(BQ, dtype=jnp.int32)
        seg_q = lax.dynamic_slice_in_dim(segment, block_start, BQ, 0)
        scores = jnp.einsum('qgpd,gkd->gpqk', query_block, keys_all, precision=lax.Precision.HIGHEST) * score_scale
        scores = low_back(scores)
        allowed = (seg_q[:, None] == segment[None, :]) & (row_ids[None, :] <= rows_q[:, None])
        scores = jnp.where(allowed, scores, masked_score)
        row_peak = lax.optimization_barrier(jnp.max(scores, axis=3, keepdims=True))
        exponent = jnp.exp(scores - row_peak)
        soft = exponent / lax.optimization_barrier(jnp.sum(exponent, axis=3, keepdims=True))
        mixed_rows = jnp.einsum('gpqk,gkd->qgpd', low(soft), values_all, precision=lax.Precision.HIGHEST)
        return low_back(low(mixed_rows)).reshape(BQ, H * HD)
    attended = lax.map(jax.checkpoint(attend), (grouped, jnp.arange(TOK // BQ, dtype=jnp.int32)))
    attended = attended.reshape(TOK, H * HD)
    hidden_state = x_rows + low_back(fine_dot(attended, out_w))
    inv_two = lax.rsqrt(lax.optimization_barrier(jnp.mean(hidden_state * hidden_state, axis=1, keepdims=True)) + eps_norm)
    normed_two = low(hidden_state * inv_two * gain_two)
    route_flat = route_rows.reshape(-1).astype(jnp.int32)
    onehot = (route_flat[:, None] == jnp.arange(E, dtype=jnp.int32)[None, :]).astype(jnp.int32)
    before = (jnp.cumsum(onehot, axis=0, dtype=jnp.int32) - onehot).astype(jnp.int32)
    position = lax.optimization_barrier(jnp.sum(before * onehot, axis=1, dtype=jnp.int32)).astype(jnp.int32)
    slot_of = jnp.where(position < C, route_flat * C + position, E * C).astype(jnp.int32)
    pair_token = (jnp.arange(TOK * TOP, dtype=jnp.int32) // TOP).astype(jnp.int32)
    slot_token = jnp.full((E * C + 1,), TOK, jnp.int32).at[slot_of].set(pair_token)[:E * C].astype(jnp.int32)
    padded_two = jnp.concatenate([normed_two, jnp.zeros((1, D), jnp.float32)], axis=0)
    slot_rows = padded_two[slot_token].reshape(E, C, D)
    gate_val = low_back(jnp.einsum('ecd,edf->ecf', slot_rows, gate_w, precision=lax.Precision.HIGHEST))
    up_val = low_back(jnp.einsum('ecd,edf->ecf', slot_rows, up_w, precision=lax.Precision.HIGHEST))
    hidden = low(jnp.square(jax.nn.relu(gate_val)) * up_val)
    expert_out = low_back(jnp.einsum('ecf,efd->ecd', hidden, down_w, precision=lax.Precision.HIGHEST))
    expert_pad = jnp.concatenate([expert_out.reshape(E * C, D), jnp.zeros((1, D), jnp.float32)], axis=0)
    picked = expert_pad[slot_of].reshape(TOK, TOP, D)
    mixture = lax.optimization_barrier(jnp.sum(picked * gate_rows[:, :, None], axis=1))
    return hidden_state + mixture

def reference(tokens, perm, routes, gates, lengths, cotangent, gain_attn, w_query, w_keyval, w_out, gain_moe, w_gate, w_up, w_down):
    perm = perm.astype(jnp.int32)
    source_row = jnp.zeros((TOKENS,), jnp.int32).at[perm].set(jnp.arange(TOKENS, dtype=jnp.int32)).astype(jnp.int32)
    x_dealt = tokens[source_row].astype(jnp.float32).reshape(N_DP, TOK, D)
    cot_dealt = cotangent[source_row].astype(jnp.float32).reshape(N_DP, TOK, D)
    route_dealt = routes[source_row].astype(jnp.int32).reshape(N_DP, TOK, TOP)
    gate_dealt = gates[source_row].astype(jnp.float32).reshape(N_DP, TOK, TOP)
    length_rows = lengths.astype(jnp.int32)
    weights = tuple((weight.astype(jnp.float32) for weight in (gain_attn, w_query, w_keyval, w_out, gain_moe, w_gate, w_up, w_down)))

    def forward(weight_set, x_groups):
        group_step = jax.checkpoint(lambda inputs: group_forward(weight_set, inputs))
        return lax.map(group_step, (x_groups, route_dealt, gate_dealt, length_rows))
    result, pullback = jax.vjp(forward, weights, x_dealt)
    weight_grads, x_grad = pullback(cot_dealt)
    outputs = result.reshape(TOKENS, D)[perm].astype(jnp.bfloat16)
    grad_tokens = x_grad.reshape(TOKENS, D)[perm].astype(jnp.bfloat16)
    grad_one, grad_query, grad_keyval, grad_out, grad_two, grad_gate, grad_up, grad_down = weight_grads
    return (outputs, grad_tokens, grad_one, grad_query, grad_keyval, grad_out, grad_two, grad_gate, grad_up, grad_down)
```

```python
import functools

import jax
import jax.numpy as jnp
from jax import lax
from jax.experimental import pallas as pl
from jax.experimental.pallas import tpu as pltpu
from jax.sharding import PartitionSpec as P

HD = 128
EPS = 1e-06
ROPE_BASE = 1000000.0
MASKED = -1e30
LOG2E = 1.4426950408889634
F32 = jnp.float32
BF16 = jnp.bfloat16
META = 128


def mm(a, b):
    return lax.dot_general(a, b, (((1,), (0,)), ((), ())), preferred_element_type=F32)


def mm_nt(a, b):
    return lax.dot_general(a, b, (((1,), (1,)), ((), ())), preferred_element_type=F32)


def mm_tn(a, b):
    return lax.dot_general(a, b, (((0,), (0,)), ((), ())), preferred_element_type=F32)


def params(mb=56):
    return pltpu.CompilerParams(vmem_limit_bytes=mb * 2**20)


def swap_halves(u):
    return pltpu.roll(u, HD // 2, 1)


def project_kernel(rotated, x_ref, w_ref, cos_ref, sin_ref, out_ref):
    step = pl.program_id(0)
    raw = mm(x_ref[...], w_ref[...])
    halves = []
    for i in range(raw.shape[1] // HD):
        u = raw[:, i * HD : (i + 1) * HD]
        turned = u * cos_ref[...] + swap_halves(u) * sin_ref[...]
        halves.append(jnp.where(step < rotated, turned, u))
    out_ref[...] = jnp.concatenate(halves, axis=1).astype(BF16)


def project(x, w, cos_full, sin_full, rotated):
    rows, width = x.shape
    columns = w.shape[1]
    return pl.pallas_call(
        functools.partial(project_kernel, rotated),
        grid=(columns // 256,),
        in_specs=[
            pl.BlockSpec((rows, width), lambda i: (0, 0)),
            pl.BlockSpec((width, 256), lambda i: (0, i)),
            pl.BlockSpec((rows, HD), lambda i: (0, 0)),
            pl.BlockSpec((rows, HD), lambda i: (0, 0)),
        ],
        out_specs=pl.BlockSpec((rows, 256), lambda i: (0, i)),
        out_shape=jax.ShapeDtypeStruct((rows, columns), BF16),
        compiler_params=params(),
        name="project",
        cost_estimate=pl.CostEstimate(
            flops=2 * rows * width * columns,
            bytes_accessed=2 * (rows * width + width * columns + rows * columns),
            transcendentals=0,
        ),
    )(x, w, cos_full, sin_full)


def make_bias(z_ref, start_ref, bias_ref):
    rows = start_ref.shape[0]
    blocks = bias_ref.shape[0]
    z = z_ref[0]
    for j in range(blocks):
        key = (z - (blocks - 1) + j) * rows + lax.broadcasted_iota(jnp.int32, (rows, rows), 1)
        query = z * rows + lax.broadcasted_iota(jnp.int32, (rows, rows), 0)
        allowed = (key >= start_ref[...]) & (key <= query)
        bias_ref[j] = jnp.where(allowed, 0.0, MASKED)


def attend_kernel(kv_heads, z_ref, start_ref, q_ref, kv0_ref, kv1_ref, kv2_ref, o_ref, lse_ref, bias_ref):
    head = pl.program_id(0)
    heads = pl.num_programs(0)

    @pl.when(head == 0)
    def _():
        make_bias(z_ref, start_ref, bias_ref)

    kvh = head // (heads // kv_heads)
    scale = HD**-0.5 * LOG2E
    q = q_ref[...]
    kvs = (kv0_ref, kv1_ref, kv2_ref)
    kcol = pl.ds(pl.multiple_of(kvh * HD, HD), HD)
    vcol = pl.ds(pl.multiple_of((kv_heads + kvh) * HD, HD), HD)
    scores = [mm_nt(q, ref[:, kcol]) * scale + bias_ref[j] for j, ref in enumerate(kvs)]
    peak = functools.reduce(
        jnp.maximum, [jnp.max(s, axis=1, keepdims=True) for s in scores]
    )
    soft = [jnp.exp2(s - peak) for s in scores]
    total = sum(jnp.sum(s, axis=1, keepdims=True) for s in soft)
    mixed = sum(mm(s.astype(BF16), ref[:, vcol]) for s, ref in zip(soft, kvs))
    o_ref[...] = (mixed / total).astype(BF16)
    lse_ref[0] = peak + jnp.log2(total)


def attend(z, start, q, kvs, kv_heads):
    rows, columns = q.shape
    heads = columns // HD
    blocks = len(kvs)
    kv_spec = pl.BlockSpec(kvs[0].shape, lambda h, s: (0, 0))
    return pl.pallas_call(
        functools.partial(attend_kernel, kv_heads),
        grid_spec=pltpu.PrefetchScalarGridSpec(
            num_scalar_prefetch=1,
            grid=(heads,),
            in_specs=[
                pl.BlockSpec((rows, 1), lambda h, s: (0, 0)),
                pl.BlockSpec((rows, HD), lambda h, s: (0, h)),
                *[kv_spec] * blocks,
            ],
            out_specs=[
                pl.BlockSpec((rows, HD), lambda h, s: (0, h)),
                pl.BlockSpec((1, rows, 1), lambda h, s: (h, 0, 0)),
            ],
            scratch_shapes=[pltpu.VMEM((blocks, rows, rows), F32)],
        ),
        out_shape=[
            jax.ShapeDtypeStruct((rows, columns), BF16),
            jax.ShapeDtypeStruct((heads, rows, 1), F32),
        ],
        compiler_params=params(),
        name="attend",
        cost_estimate=pl.CostEstimate(
            flops=4 * rows * rows * blocks * columns,
            bytes_accessed=8 * rows * columns,
            transcendentals=rows * rows * blocks * heads,
        ),
    )(z, start, q, *kvs)


def attend_back_kernel(
    kv_heads,
    z_ref,
    start_ref,
    q_ref,
    o_ref,
    do_ref,
    lse_ref,
    cos_ref,
    sin_ref,
    kv0_ref,
    kv1_ref,
    kv2_ref,
    dq_ref,
    d0_ref,
    d1_ref,
    d2_ref,
    bias_ref,
    acc_ref,
):
    head = pl.program_id(0)
    heads = pl.num_programs(0)

    @pl.when(head == 0)
    def _():
        make_bias(z_ref, start_ref, bias_ref)
        acc_ref[...] = jnp.zeros_like(acc_ref)

    kvh = head // (heads // kv_heads)
    scale = HD**-0.5 * LOG2E
    q = q_ref[...]
    do = do_ref[...]
    centre = jnp.sum(do.astype(F32) * o_ref[...].astype(F32), axis=1, keepdims=True)
    lse = lse_ref[0]
    kcol = pl.ds(pl.multiple_of(kvh * HD, HD), HD)
    vcol = pl.ds(pl.multiple_of((kv_heads + kvh) * HD, HD), HD)
    dq = jnp.zeros(q.shape, F32)
    for j, ref in enumerate((kv0_ref, kv1_ref, kv2_ref)):
        keys = ref[:, kcol]
        soft = jnp.exp2(mm_nt(q, keys) * scale + (bias_ref[j] - lse))
        acc_ref[j, :, vcol] += mm_tn(soft.astype(BF16), do)
        dsoft = mm_nt(do, ref[:, vcol])
        dscore = (soft * (dsoft - centre)).astype(BF16)
        dq += mm(dscore, keys)
        acc_ref[j, :, kcol] += mm_tn(dscore, q) * (HD**-0.5)
    dq = dq * (HD**-0.5)
    dq_ref[...] = (dq * cos_ref[...] - swap_halves(dq) * sin_ref[...]).astype(BF16)

    @pl.when(head == heads - 1)
    def _():
        d0_ref[...] = acc_ref[0].astype(BF16)
        d1_ref[...] = acc_ref[1].astype(BF16)
        d2_ref[...] = acc_ref[2]


def attend_back(z, start, q, o, do, lse, cos_full, sin_full, kvs, kv_heads):
    rows, columns = q.shape
    heads = columns // HD
    blocks = len(kvs)
    kv_columns = kvs[0].shape[1]
    kv_spec = pl.BlockSpec((rows, kv_columns), lambda h, s: (0, 0))
    head_spec = pl.BlockSpec((rows, HD), lambda h, s: (0, h))
    table_spec = pl.BlockSpec((rows, HD), lambda h, s: (0, 0))
    return pl.pallas_call(
        functools.partial(attend_back_kernel, kv_heads),
        grid_spec=pltpu.PrefetchScalarGridSpec(
            num_scalar_prefetch=1,
            grid=(heads,),
            in_specs=[
                pl.BlockSpec((rows, 1), lambda h, s: (0, 0)),
                head_spec,
                head_spec,
                head_spec,
                pl.BlockSpec((1, rows, 1), lambda h, s: (h, 0, 0)),
                table_spec,
                table_spec,
                *[kv_spec] * blocks,
            ],
            out_specs=[head_spec, *[kv_spec] * blocks],
            scratch_shapes=[
                pltpu.VMEM((blocks, rows, rows), F32),
                pltpu.VMEM((blocks, rows, kv_columns), F32),
            ],
        ),
        out_shape=[
            jax.ShapeDtypeStruct((rows, columns), BF16),
            jax.ShapeDtypeStruct((rows, kv_columns), BF16),
            jax.ShapeDtypeStruct((rows, kv_columns), BF16),
            jax.ShapeDtypeStruct((rows, kv_columns), F32),
        ],
        compiler_params=params(),
        name="attend_back",
        cost_estimate=pl.CostEstimate(
            flops=10 * rows * rows * blocks * columns,
            bytes_accessed=12 * rows * columns,
            transcendentals=rows * rows * blocks * heads,
        ),
    )(z, start, q, o, do, lse, cos_full, sin_full, *kvs)


def expert_kernel(first, x_ref, dy_ref, gate_ref, wg_ref, wu_ref, wd_ref, *refs):
    if first:
        y_ref, dn_ref, hs_ref, dg_ref, du_ref = refs
    else:
        y0_ref, dn0_ref, y_ref, dn_ref, hs_ref, dg_ref, du_ref = refs
    step = pl.program_id(0)

    @pl.when(step == 0)
    def _():
        if first:
            y_ref[...] = jnp.zeros_like(y_ref)
            dn_ref[...] = jnp.zeros_like(dn_ref)
        else:
            y_ref[...] = y0_ref[...]
            dn_ref[...] = dn0_ref[...]

    x = x_ref[...]
    gate = gate_ref[...].astype(F32)
    g = jnp.maximum(mm(x, wg_ref[...]), 0.0)
    u = mm(x, wu_ref[...])
    square = g * g
    hs = ((square * u).astype(BF16).astype(F32) * gate).astype(BF16)
    hs_ref[...] = hs
    dh = mm_nt(dy_ref[...], wd_ref[...]) * gate
    dg = (dh * u * (2.0 * g)).astype(BF16)
    du = (dh * square).astype(BF16)
    dg_ref[...] = dg
    du_ref[...] = du
    dn_ref[...] += mm_nt(dg, wg_ref[...]) + mm_nt(du, wu_ref[...])
    y_ref[...] += mm(hs, wd_ref[...])


def experts(x, dy, gate, wg, wu, wd, before=None, chunk=256):
    rows, width = x.shape
    hidden = gate.shape[1]
    full = pl.BlockSpec((rows, width), lambda i: (0, 0))
    part = pl.BlockSpec((rows, chunk), lambda i: (0, i))
    columns = pl.BlockSpec((width, chunk), lambda i: (0, i))
    extra = () if before is None else tuple(before)
    return pl.pallas_call(
        functools.partial(expert_kernel, before is None),
        grid=(hidden // chunk,),
        in_specs=[
            full,
            full,
            part,
            columns,
            columns,
            pl.BlockSpec((chunk, width), lambda i: (i, 0)),
            *[full] * len(extra),
        ],
        out_specs=[full, full, part, part, part],
        out_shape=[
            jax.ShapeDtypeStruct((rows, width), F32),
            jax.ShapeDtypeStruct((rows, width), F32),
            *[jax.ShapeDtypeStruct((rows, hidden), BF16)] * 3,
        ],
        compiler_params=params(),
        name="experts",
        cost_estimate=pl.CostEstimate(
            flops=12 * rows * width * hidden,
            bytes_accessed=6 * width * hidden + 16 * rows * width,
            transcendentals=0,
        ),
    )(x, dy, gate, wg, wu, wd, *extra)


def per_device(
    tokens,
    perm,
    routes,
    gates,
    lengths,
    cotangent,
    gain_attn,
    w_query,
    w_keyval,
    w_out,
    gain_moe,
    w_gate,
    w_up,
    w_down,
):
    dp_count = lax.axis_size("dp")
    tensor_count = lax.axis_size("tensor")
    d = lax.axis_index("dp")
    z = lax.axis_index("tensor")
    rows, width = tokens.shape
    group_rows = perm.shape[0]
    share = rows // dp_count
    top = routes.shape[1]
    experts_n, _, part_hidden = w_gate.shape
    hidden = experts_n * part_hidden
    capacity = 9 * group_rows * top // (8 * experts_n)
    kv_heads = w_keyval.shape[1] // (2 * HD)
    query_cols = w_query.shape[1]
    team = 8
    teams = [[t * team + i for i in range(team)] for t in range(dp_count // team)]
    teams = None if len(teams) == 1 else teams
    piece_rows = width // team
    member = d % team

    def z_move(x, pairs):
        return lax.ppermute(x, "tensor", pairs)

    near = [(i, i ^ 1) for i in range(tensor_count)]
    far = [(i, i ^ 2) for i in range(tensor_count)]

    def deal(x):
        return lax.all_to_all(
            x.reshape(dp_count, share, x.shape[1]), "dp", split_axis=0, concat_axis=0, tiled=True
        ).reshape(rows, x.shape[1])

    own_perm = lax.dynamic_slice_in_dim(perm, z * rows, rows, 0)
    own_routes = lax.dynamic_slice_in_dim(routes, z * rows, rows, 0)
    dest = own_perm // group_rows
    place = own_perm % rows
    row_index = jnp.arange(rows, dtype=jnp.int32)
    lower = (row_index[:, None] > row_index[None, :]).astype(BF16)
    dest_hot = (dest[:, None] == jnp.arange(dp_count, dtype=jnp.int32)[None, :]).astype(BF16)
    earlier = jnp.sum(mm(lower, dest_hot) * dest_hot.astype(F32), axis=1).astype(jnp.int32)
    slot = dest * share + earlier
    pack = (row_index[:, None] == slot[None, :]).astype(BF16)
    meta = jnp.concatenate(
        [
            (place // 16)[:, None].astype(BF16),
            (place % 16)[:, None].astype(BF16),
            own_routes.astype(BF16),
            gates,
            jnp.zeros((rows, META - 2 - 2 * top), BF16),
        ],
        axis=1,
    )
    packed = mm(pack, jnp.concatenate([tokens, meta], axis=1)).astype(BF16)
    arrived = deal(packed)
    packed_dy = mm(pack, cotangent).astype(BF16)
    arrived_dy = deal(packed_dy)
    meta_in = arrived[:, width:].astype(F32)
    place_in = (meta_in[:, 0] * 16.0 + meta_in[:, 1]).astype(jnp.int32)
    unpack = (row_index[:, None] == place_in[None, :]).astype(BF16)
    dealt = mm(unpack, arrived)
    x_rows = dealt[:, :width]
    meta_rows = dealt[:, width:]
    dy_rows = mm(unpack, arrived_dy).astype(BF16)

    expert_ids = jnp.arange(experts_n, dtype=jnp.int32).astype(F32)
    route_rows = meta_rows[:, 2 : 2 + top]
    gate_rows = meta_rows[:, 2 + top : 2 + 2 * top]
    hot = route_rows[:, :, None] == expert_ids[None, None, :]
    routed = jnp.sum(hot.astype(F32), axis=1)
    counts = lax.all_gather(jnp.sum(routed, axis=0)[None, :], "tensor", axis=0, tiled=True)
    z_ids = jnp.arange(tensor_count, dtype=jnp.int32)
    base = jnp.sum(jnp.where(z_ids[:, None] < z, counts, 0.0), axis=0)
    position = mm(lower, routed.astype(BF16)) + base[None, :]
    weight = jnp.sum(jnp.where(hot, gate_rows[:, :, None], 0.0), axis=1)
    weight = jnp.where(position < capacity, weight, 0.0).astype(BF16)
    weight_near = z_move(weight, near)
    gate_own = jnp.repeat(weight, part_hidden, axis=1)
    gate_near = jnp.repeat(weight_near, part_hidden, axis=1)
    dy_near = z_move(dy_rows, near)

    def team_gather(x):
        return lax.all_gather(x, "dp", axis=0, tiled=True, axis_index_groups=teams)

    def flat(w):
        return w.transpose(1, 0, 2).reshape(w.shape[1], hidden)

    def piece(w):
        return lax.dynamic_slice_in_dim(w, member * piece_rows, piece_rows, 1)

    wq_piece = lax.dynamic_slice_in_dim(w_query, member * piece_rows, piece_rows, 0)
    wq_piece = lax.all_gather(wq_piece, "tensor", axis=0, tiled=True)
    wq_all = team_gather(wq_piece).reshape(team, tensor_count, piece_rows, query_cols)
    wq = wq_all.transpose(0, 2, 1, 3).reshape(width, tensor_count * query_cols)
    out_rows = query_cols // team
    wo_piece = lax.dynamic_slice_in_dim(w_out, member * out_rows, out_rows, 0)
    wo_piece = lax.all_gather(wo_piece, "tensor", axis=0, tiled=True)
    wo_all = team_gather(wo_piece).reshape(team, tensor_count, out_rows, width)
    wo = wo_all.transpose(1, 0, 2, 3).reshape(tensor_count * query_cols, width)

    wd_own = w_down.reshape(hidden, width)
    wg_own = flat(w_gate)
    wu_own = flat(w_up)
    gu_piece = jnp.concatenate([flat(piece(w_gate)), flat(piece(w_up))], axis=1)
    hidden_piece = hidden // team
    wd_piece = lax.dynamic_slice_in_dim(wd_own, member * hidden_piece, hidden_piece, 0)
    gu_far = team_gather(z_move(gu_piece, far))
    wd_far = team_gather(z_move(wd_piece, far))
    wg_far = gu_far[:, :hidden]
    wu_far = gu_far[:, hidden:]

    seq_lengths = lengths[0]
    seq_index = jnp.arange(seq_lengths.shape[0], dtype=jnp.int32)
    seq_ends = jnp.sum(
        jnp.where(seq_index[None, :] <= seq_index[:, None], seq_lengths[None, :], 0), axis=1
    ).astype(jnp.int32)
    global_row = z * rows + row_index
    start = jnp.max(
        jnp.where(global_row[:, None] >= seq_ends[None, :], seq_ends[None, :], 0), axis=1
    ).astype(jnp.int32)
    offset = (global_row - start).astype(F32)
    frequency = ROPE_BASE ** (-2.0 * jnp.arange(HD // 2, dtype=F32) / HD)
    angles = offset[:, None] * frequency[None, :]
    cosine, sine = jnp.cos(angles), jnp.sin(angles)
    cos_full = jnp.concatenate([cosine, cosine], axis=1)
    sin_full = jnp.concatenate([-sine, sine], axis=1)
    start = start[:, None]
    z_arg = z.astype(jnp.int32)[None]

    inv_one = lax.rsqrt(jnp.mean(x_rows * x_rows, axis=1, keepdims=True) + EPS)
    n1 = (x_rows * inv_one * gain_attn).astype(BF16)
    kv = project(n1, w_keyval, cos_full, sin_full, 1)
    up_one = [(i, i + 1) for i in range(tensor_count - 1)]
    up_two = [(i, i + 2) for i in range(tensor_count - 2)]
    kv_one = z_move(kv, up_one)
    kv_two = z_move(kv, up_two)
    q = project(n1, wq, cos_full, sin_full, wq.shape[1] // 256)
    kvs = (kv_two, kv_one, kv)
    o, lse = attend(z_arg, start, q, kvs, kv_heads)
    h = x_rows + mm(o, wo)
    inv_two = lax.rsqrt(jnp.mean(h * h, axis=1, keepdims=True) + EPS)
    n2 = (h * inv_two * gain_moe).astype(BF16)

    n2_near = z_move(n2, near)
    y, dn2, hs_oo, dg_oo, du_oo = experts(n2, dy_rows, gate_own, wg_own, wu_own, wd_own)
    y, dn2, hs_of, dg_of, du_of = experts(
        n2, dy_rows, gate_own, wg_far, wu_far, wd_far, (y, dn2)
    )
    yn, dnn, hs_no, dg_no, du_no = experts(n2_near, dy_near, gate_near, wg_own, wu_own, wd_own)
    yn, dnn, hs_nf, dg_nf, du_nf = experts(
        n2_near, dy_near, gate_near, wg_far, wu_far, wd_far, (yn, dnn)
    )
    dn2 = dn2 + z_move(dnn.astype(BF16), near).astype(F32)
    result = h + y + z_move(yn.astype(BF16), near).astype(F32)

    def two(a, b, c, e):
        return (mm_tn(a, b) + mm_tn(c, e)).astype(BF16)

    grads_own = [
        two(n2, dg_oo, n2_near, dg_no),
        two(n2, du_oo, n2_near, du_no),
        two(dy_rows, hs_oo, dy_near, hs_no),
    ]
    grads_far = [
        two(n2, dg_of, n2_near, dg_nf),
        two(n2, du_of, n2_near, du_nf),
        two(dy_rows, hs_of, dy_near, hs_nf),
    ]

    def dp_sum(x):
        return lax.psum_scatter(x, "dp", scatter_dimension=0, tiled=True)

    sums_far = [z_move(dp_sum(g), far) for g in grads_far]
    sums = [dp_sum(g).astype(F32) + f.astype(F32) for g, f in zip(grads_own, sums_far)]
    out_w = width // dp_count
    sum_gate, sum_up, sum_down = [g.reshape(out_w, experts_n, part_hidden) for g in sums]
    sum_gate = sum_gate.transpose(1, 0, 2)
    sum_up = sum_up.transpose(1, 0, 2)
    sum_down = sum_down.transpose(1, 2, 0)

    gain_two_part = jnp.sum(dn2 * h * inv_two, axis=0)
    u2 = dn2 * gain_moe
    dh = dy_rows.astype(F32) + inv_two * (
        u2 - h * inv_two * inv_two * jnp.mean(u2 * h, axis=1, keepdims=True)
    )
    dhb = dh.astype(BF16)
    do = mm_nt(dhb, wo).astype(BF16)
    grad_out_part = mm_tn(dhb, o).astype(BF16)

    dq, dkv_two, dkv_one, dkv = attend_back(
        z_arg, start, q, o, do, lse, cos_full, sin_full, kvs, kv_heads
    )
    dkv = dkv + z_move(dkv_one, [(b, a) for a, b in up_one]).astype(F32)
    dkv = dkv + z_move(dkv_two, [(b, a) for a, b in up_two]).astype(F32)

    def unrotate(u):
        swapped = jnp.concatenate([u[:, HD // 2 :], u[:, : HD // 2]], axis=1)
        return u * cos_full - swapped * sin_full

    dkv = jnp.concatenate(
        [unrotate(dkv[:, i * HD : (i + 1) * HD]) for i in range(kv_heads)]
        + [dkv[:, kv_heads * HD :]],
        axis=1,
    ).astype(BF16)
    dn1 = mm_nt(dq, wq) + mm_nt(dkv, w_keyval)
    grad_query_part = mm_tn(n1, dq).astype(BF16)
    grad_keyval_part = mm_tn(n1, dkv).astype(BF16)
    gain_one_part = jnp.sum(dn1 * x_rows * inv_one, axis=0)
    u1 = dn1 * gain_attn
    dx = dh + inv_one * (
        u1 - x_rows * inv_one * inv_one * jnp.mean(u1 * x_rows, axis=1, keepdims=True)
    )

    def give_back(values):
        back = deal(mm_tn(unpack, values.astype(BF16)).astype(BF16))
        return mm_tn(pack, back).astype(BF16)

    outputs = give_back(result)
    grad_tokens = give_back(dx)

    def tensor_sum(x):
        parts = x.reshape(x.shape[0], tensor_count, x.shape[1] // tensor_count).transpose(1, 0, 2)
        return lax.psum_scatter(parts, "tensor", scatter_dimension=0, tiled=True)[0].astype(F32)

    sum_out = tensor_sum(dp_sum(grad_out_part)).T
    sum_query = tensor_sum(dp_sum(grad_query_part))
    small = jnp.concatenate(
        [
            grad_keyval_part,
            gain_one_part[:, None].astype(BF16),
            gain_two_part[:, None].astype(BF16),
            jnp.zeros((width, HD - 2), BF16),
        ],
        axis=1,
    )
    small = lax.psum(dp_sum(small), "tensor").astype(F32)
    kv_cols = w_keyval.shape[1]
    return (
        outputs,
        grad_tokens,
        small[:, kv_cols],
        sum_query,
        small[:, :kv_cols],
        sum_out,
        small[:, kv_cols + 1],
        sum_gate,
        sum_up,
        sum_down,
    )


def solution(mesh):
    in_specs = (
        P(("dp", "tensor"), None),
        P("dp"),
        P("dp", None),
        P(("dp", "tensor"), None),
        P("dp", None),
        P(("dp", "tensor"), None),
        P(),
        P(None, "tensor"),
        P(),
        P("tensor", None),
        P(),
        P(None, None, "tensor"),
        P(None, None, "tensor"),
        P(None, "tensor", None),
    )
    out_specs = (
        P(("dp", "tensor"), None),
        P(("dp", "tensor"), None),
        P("dp"),
        P("dp", "tensor"),
        P("dp", None),
        P("tensor", "dp"),
        P("dp"),
        P(None, "dp", "tensor"),
        P(None, "dp", "tensor"),
        P(None, "tensor", "dp"),
    )
    return jax.shard_map(
        per_device, mesh=mesh, in_specs=in_specs, out_specs=out_specs, check_vma=False
    )
```

```python
import functools

import jax
import jax.numpy as jnp
from jax import lax
from jax.experimental import pallas as pl
from jax.experimental.layout import Layout, with_layout_constraint
from jax.experimental.pallas import tpu as pltpu
from jax.sharding import PartitionSpec as P

HD = 128
EPS = 1e-06
ROPE_BASE = 1000000.0
MASKED = -1e30
LOG2E = 1.4426950408889634
F32 = jnp.float32
BF16 = jnp.bfloat16
META = 128


def mm(a, b):
    return lax.dot_general(a, b, (((1,), (0,)), ((), ())), preferred_element_type=F32)


def mm_nt(a, b):
    return lax.dot_general(a, b, (((1,), (1,)), ((), ())), preferred_element_type=F32)


def mm_tn(a, b):
    return lax.dot_general(a, b, (((0,), (0,)), ((), ())), preferred_element_type=F32)


def params(mb=56):
    return pltpu.CompilerParams(vmem_limit_bytes=mb * 2**20)


def swap_halves(u):
    return pltpu.roll(u, HD // 2, 1)


def keyval_kernel(
    x_ref,
    w_ref,
    cos_ref,
    sin_ref,
    count_ref,
    mark_ref,
    deal_ref,
    kv_ref,
    one_ref,
    two_ref,
    counts_ref,
    near_ref,
    dealt_ref,
    send,
    recv,
    deal_send,
    deal_recv,
):
    z = lax.axis_index("tensor")
    d = lax.axis_index("dp")
    d_count = deal_ref.shape[0]
    z_count = counts_ref.shape[0]
    others = [{"tensor": (z + m) % z_count} for m in range(1, z_count)]
    barrier = pltpu.get_barrier_semaphore()
    peers = [{"dp": (d + p) % d_count} for p in range(1, d_count)]
    for other in others + peers:
        pl.semaphore_signal(barrier, inc=1, device_id=other, device_id_type=pl.DeviceIdType.MESH)
    raw = mm(x_ref[...], w_ref[...])
    turned = raw.shape[1] // 2
    for i in range(turned // HD):
        u = raw[:, i * HD : (i + 1) * HD]
        u = u * cos_ref[...] + swap_halves(u) * sin_ref[...]
        kv_ref[:, i * HD : (i + 1) * HD] = u.astype(BF16)
    kv_ref[:, turned:] = raw[:, turned:].astype(BF16)
    pl.semaphore_wait(barrier, z_count - 1 + d_count - 1)
    moves = [(count_ref, counts_ref.at[m], others[m]) for m in range(z_count - 1)]
    moves += [(mark_ref, near_ref, {"tensor": flip(z, 1)})]
    moves += [(kv_ref, one_ref, others[0]), (kv_ref, two_ref, others[1])]
    copies = []
    for at, (src, dst, to) in enumerate(moves):
        copy = pltpu.make_async_remote_copy(
            src_ref=src,
            dst_ref=dst,
            send_sem=send.at[at],
            recv_sem=recv.at[at],
            device_id=to,
            device_id_type=pl.DeviceIdType.MESH,
        )
        copy.start()
        copies.append(copy)
    for p, peer in enumerate(peers):
        copy = pltpu.make_async_remote_copy(
            src_ref=deal_ref.at[(d + p + 1) % d_count],
            dst_ref=dealt_ref.at[d],
            send_sem=deal_send.at[p],
            recv_sem=deal_recv.at[p],
            device_id=peer,
            device_id_type=pl.DeviceIdType.MESH,
        )
        copy.start()
        copies.append(copy)
    counts_ref[z_count - 1] = count_ref[...]
    dealt_ref[d] = deal_ref[d]
    for copy in copies:
        copy.wait()


def keyval(x, w, cos_full, sin_full, counts, marks, deals, z_count):
    rows = x.shape[0]
    columns = w.shape[1]
    vmem = pl.BlockSpec(memory_space=pltpu.VMEM)
    block = jax.ShapeDtypeStruct((rows, columns), BF16)
    return pl.pallas_call(
        keyval_kernel,
        in_specs=[vmem] * 7,
        out_specs=[vmem] * 6,
        out_shape=[block] * 3
        + [
            jax.ShapeDtypeStruct((z_count, *counts.shape), counts.dtype),
            jax.ShapeDtypeStruct(marks.shape, marks.dtype),
            jax.ShapeDtypeStruct(deals.shape, deals.dtype),
        ],
        scratch_shapes=[
            pltpu.SemaphoreType.DMA((z_count + 2,)),
            pltpu.SemaphoreType.DMA((z_count + 2,)),
            pltpu.SemaphoreType.DMA((deals.shape[0] - 1,)),
            pltpu.SemaphoreType.DMA((deals.shape[0] - 1,)),
        ],
        compiler_params=pltpu.CompilerParams(
            vmem_limit_bytes=40 * 2**20, collective_id=1, has_side_effects=True
        ),
        name="keyval",
    )(x, w, cos_full, sin_full, counts, marks, deals)


def project_query_kernel(x_ref, w_ref, cos_ref, sin_ref, out_ref):
    raw = mm(x_ref[...], w_ref[...].reshape(x_ref.shape[1], out_ref.shape[1]))
    for i in range(raw.shape[1] // HD):
        u = raw[:, i * HD : (i + 1) * HD]
        turned = u * cos_ref[...] + swap_halves(u) * sin_ref[...]
        out_ref[:, i * HD : (i + 1) * HD] = turned.astype(BF16)


def project_query(x, w, cos_full, sin_full):
    rows, width = x.shape
    pieces, blocks, piece, columns = w.shape
    return pl.pallas_call(
        project_query_kernel,
        grid=(blocks,),
        in_specs=[
            pl.BlockSpec((rows, width), lambda i: (0, 0)),
            pl.BlockSpec((pieces, 1, piece, columns), lambda i: (0, i, 0, 0)),
            pl.BlockSpec((rows, HD), lambda i: (0, 0)),
            pl.BlockSpec((rows, HD), lambda i: (0, 0)),
        ],
        out_specs=pl.BlockSpec((rows, columns), lambda i: (0, i)),
        out_shape=jax.ShapeDtypeStruct((rows, blocks * columns), BF16),
        compiler_params=params(),
        name="project_query",
        cost_estimate=pl.CostEstimate(
            flops=2 * rows * width * blocks * columns,
            bytes_accessed=2 * (2 * rows * width + width * blocks * columns),
            transcendentals=0,
        ),
    )(x, w, cos_full, sin_full)


def project_back_kernel(dq_ref, w_ref, dkv_ref, wkv_ref, out_ref):
    step = pl.program_id(0)
    width = out_ref.shape[1]
    part = mm_nt(dq_ref[...], w_ref[...].reshape(width, dq_ref.shape[1]))

    @pl.when(step == 0)
    def _():
        out_ref[...] = part + mm_nt(dkv_ref[...], wkv_ref[...])

    @pl.when(step > 0)
    def _():
        out_ref[...] += part


def project_back(dq, w, dkv, wkv):
    rows = dq.shape[0]
    pieces, blocks, piece, columns = w.shape
    width = pieces * piece
    return pl.pallas_call(
        project_back_kernel,
        grid=(blocks,),
        in_specs=[
            pl.BlockSpec((rows, columns), lambda i: (0, i)),
            pl.BlockSpec((pieces, 1, piece, columns), lambda i: (0, i, 0, 0)),
            pl.BlockSpec(dkv.shape, lambda i: (0, 0)),
            pl.BlockSpec(wkv.shape, lambda i: (0, 0)),
        ],
        out_specs=pl.BlockSpec((rows, width), lambda i: (0, 0)),
        out_shape=jax.ShapeDtypeStruct((rows, width), F32),
        compiler_params=params(),
        name="project_back",
        cost_estimate=pl.CostEstimate(
            flops=2 * rows * width * (blocks * columns + dkv.shape[1]),
            bytes_accessed=2 * width * (3 * rows + blocks * columns),
            transcendentals=0,
        ),
    )(dq, w, dkv, wkv)


def make_bias(z_ref, start_ref, bias_ref):
    rows = start_ref.shape[0]
    blocks = bias_ref.shape[0]
    z = z_ref[0]
    for j in range(blocks):
        key = (z - (blocks - 1) + j) * rows + lax.broadcasted_iota(jnp.int32, (rows, rows), 1)
        query = z * rows + lax.broadcasted_iota(jnp.int32, (rows, rows), 0)
        allowed = (key >= start_ref[...]) & (key <= query)
        bias_ref[j] = jnp.where(allowed, 0.0, MASKED)


def attend_kernel(kv_heads, z_ref, start_ref, q_ref, kv0_ref, kv1_ref, kv2_ref, o_ref, lse_ref, bias_ref):
    head = pl.program_id(0)
    heads = pl.num_programs(0)

    @pl.when(head == 0)
    def _():
        make_bias(z_ref, start_ref, bias_ref)

    kvh = head // (heads // kv_heads)
    scale = HD**-0.5 * LOG2E
    q = q_ref[...]
    kvs = (kv0_ref, kv1_ref, kv2_ref)
    kcol = pl.ds(pl.multiple_of(kvh * HD, HD), HD)
    vcol = pl.ds(pl.multiple_of((kv_heads + kvh) * HD, HD), HD)
    scores = [mm_nt(q, ref[:, kcol]) * scale + bias_ref[j] for j, ref in enumerate(kvs)]
    peak = functools.reduce(
        jnp.maximum, [jnp.max(s, axis=1, keepdims=True) for s in scores]
    )
    soft = [jnp.exp2(s - peak) for s in scores]
    total = sum(jnp.sum(s, axis=1, keepdims=True) for s in soft)
    mixed = sum(mm(s.astype(BF16), ref[:, vcol]) for s, ref in zip(soft, kvs))
    o_ref[...] = (mixed / total).astype(BF16)
    lse_ref[0] = peak + jnp.log2(total)


def attend(z, start, q, kvs, kv_heads):
    rows, columns = q.shape
    heads = columns // HD
    blocks = len(kvs)
    kv_spec = pl.BlockSpec(kvs[0].shape, lambda h, s: (0, 0))
    return pl.pallas_call(
        functools.partial(attend_kernel, kv_heads),
        grid_spec=pltpu.PrefetchScalarGridSpec(
            num_scalar_prefetch=1,
            grid=(heads,),
            in_specs=[
                pl.BlockSpec((rows, 1), lambda h, s: (0, 0)),
                pl.BlockSpec((rows, HD), lambda h, s: (0, h)),
                *[kv_spec] * blocks,
            ],
            out_specs=[
                pl.BlockSpec((rows, HD), lambda h, s: (0, h)),
                pl.BlockSpec((1, rows, 1), lambda h, s: (h, 0, 0)),
            ],
            scratch_shapes=[pltpu.VMEM((blocks, rows, rows), F32)],
        ),
        out_shape=[
            jax.ShapeDtypeStruct((rows, columns), BF16),
            jax.ShapeDtypeStruct((heads, rows, 1), F32),
        ],
        compiler_params=params(),
        name="attend",
        cost_estimate=pl.CostEstimate(
            flops=4 * rows * rows * blocks * columns,
            bytes_accessed=8 * rows * columns,
            transcendentals=rows * rows * blocks * heads,
        ),
    )(z, start, q, *kvs)


def attend_back_kernel(
    kv_heads,
    z_ref,
    start_ref,
    q_ref,
    o_ref,
    do_ref,
    lse_ref,
    cos_ref,
    sin_ref,
    kv0_ref,
    kv1_ref,
    kv2_ref,
    dq_ref,
    d0_ref,
    d1_ref,
    d2_ref,
    bias_ref,
    acc_ref,
):
    head = pl.program_id(0)
    heads = pl.num_programs(0)

    @pl.when(head == 0)
    def _():
        make_bias(z_ref, start_ref, bias_ref)
        acc_ref[...] = jnp.zeros_like(acc_ref)

    kvh = head // (heads // kv_heads)
    scale = HD**-0.5 * LOG2E
    q = q_ref[...]
    do = do_ref[...]
    centre = jnp.sum(do.astype(F32) * o_ref[...].astype(F32), axis=1, keepdims=True)
    lse = lse_ref[0]
    kcol = pl.ds(pl.multiple_of(kvh * HD, HD), HD)
    vcol = pl.ds(pl.multiple_of((kv_heads + kvh) * HD, HD), HD)
    dq = jnp.zeros(q.shape, F32)
    for j, ref in enumerate((kv0_ref, kv1_ref, kv2_ref)):
        keys = ref[:, kcol]
        soft = jnp.exp2(mm_nt(q, keys) * scale + (bias_ref[j] - lse))
        acc_ref[j, :, vcol] += mm_tn(soft.astype(BF16), do)
        dsoft = mm_nt(do, ref[:, vcol])
        dscore = (soft * (dsoft - centre)).astype(BF16)
        dq += mm(dscore, keys)
        acc_ref[j, :, kcol] += mm_tn(dscore, q) * (HD**-0.5)
    dq = dq * (HD**-0.5)
    dq_ref[...] = (dq * cos_ref[...] - swap_halves(dq) * sin_ref[...]).astype(BF16)

    @pl.when(head == heads - 1)
    def _():
        d0_ref[...] = acc_ref[0].astype(BF16)
        d1_ref[...] = acc_ref[1].astype(BF16)
        d2_ref[...] = acc_ref[2]


def attend_back(z, start, q, o, do, lse, cos_full, sin_full, kvs, kv_heads):
    rows, columns = q.shape
    heads = columns // HD
    blocks = len(kvs)
    kv_columns = kvs[0].shape[1]
    kv_spec = pl.BlockSpec((rows, kv_columns), lambda h, s: (0, 0))
    head_spec = pl.BlockSpec((rows, HD), lambda h, s: (0, h))
    table_spec = pl.BlockSpec((rows, HD), lambda h, s: (0, 0))
    return pl.pallas_call(
        functools.partial(attend_back_kernel, kv_heads),
        grid_spec=pltpu.PrefetchScalarGridSpec(
            num_scalar_prefetch=1,
            grid=(heads,),
            in_specs=[
                pl.BlockSpec((rows, 1), lambda h, s: (0, 0)),
                head_spec,
                head_spec,
                head_spec,
                pl.BlockSpec((1, rows, 1), lambda h, s: (h, 0, 0)),
                table_spec,
                table_spec,
                *[kv_spec] * blocks,
            ],
            out_specs=[head_spec, *[kv_spec] * blocks],
            scratch_shapes=[
                pltpu.VMEM((blocks, rows, rows), F32),
                pltpu.VMEM((blocks, rows, kv_columns), F32),
            ],
        ),
        out_shape=[
            jax.ShapeDtypeStruct((rows, columns), BF16),
            jax.ShapeDtypeStruct((rows, kv_columns), BF16),
            jax.ShapeDtypeStruct((rows, kv_columns), BF16),
            jax.ShapeDtypeStruct((rows, kv_columns), F32),
        ],
        compiler_params=params(),
        name="attend_back",
        cost_estimate=pl.CostEstimate(
            flops=10 * rows * rows * blocks * columns,
            bytes_accessed=12 * rows * columns,
            transcendentals=rows * rows * blocks * heads,
        ),
    )(z, start, q, o, do, lse, cos_full, sin_full, *kvs)


def expert_kernel(chunk, first, x_ref, dy_ref, gate_ref, wg_ref, wu_ref, wd_ref, *refs):
    y_ref, dn_ref, hs_ref, dgu_ref = refs[-4:]
    step = pl.program_id(0)

    @pl.when(step == 0)
    def _():
        if first:
            y_ref[...] = jnp.zeros_like(y_ref)
            dn_ref[...] = jnp.zeros_like(dn_ref)
        else:
            y_ref[...] = refs[0][...]
            dn_ref[...] = refs[1][...]

    x = x_ref[...]
    gate = gate_ref[...].astype(F32)
    g = jnp.maximum(mm(x, wg_ref[...]), 0.0)
    u = mm(x, wu_ref[...])
    square = g * g
    hs = ((square * u).astype(BF16).astype(F32) * gate).astype(BF16)
    hs_ref[...] = hs
    dh = mm_nt(dy_ref[...], wd_ref[...]) * gate
    dg = (dh * u * (2.0 * g)).astype(BF16)
    du = (dh * square).astype(BF16)
    dgu_ref[:, :chunk] = dg
    dgu_ref[:, chunk:] = du
    dn_ref[...] += mm_nt(dg, wg_ref[...]) + mm_nt(du, wu_ref[...])
    y_ref[...] += mm(hs, wd_ref[...])


def experts(tile, x, dy, gate, wg, wu, wd, before=None, filled=None, up_at=0, chunk=512):
    rows, width = x.shape
    hidden = gate.shape[1]
    full = pl.BlockSpec((rows, width), lambda i: (0, 0))
    part = pl.BlockSpec((rows, chunk), lambda i: (0, i))
    operands = [x, dy, gate, wg, wu, wd]
    in_specs = [
        full,
        full,
        part,
        pl.BlockSpec((width, chunk), lambda i: (0, i)),
        pl.BlockSpec((width, chunk), lambda i: (0, i + up_at)),
        pl.BlockSpec((chunk, width), lambda i: (i, 0)),
    ]
    aliases = {}
    if before is not None:
        operands += list(before)
        in_specs += [full] * 2
    if filled is not None:
        aliases = {len(operands): 2, len(operands) + 1: 3}
        operands += list(filled)
        in_specs += [pl.BlockSpec(memory_space=pl.ANY)] * 2
    return pl.pallas_call(
        functools.partial(expert_kernel, chunk, before is None),
        grid=(hidden // chunk,),
        in_specs=in_specs,
        out_specs=[
            full,
            full,
            pl.BlockSpec((rows, chunk), lambda i: (tile, i)),
            pl.BlockSpec((rows, 2 * chunk), lambda i: (tile, i)),
        ],
        out_shape=[
            jax.ShapeDtypeStruct((rows, width), F32),
            jax.ShapeDtypeStruct((rows, width), F32),
            jax.ShapeDtypeStruct((2 * rows, hidden), BF16),
            jax.ShapeDtypeStruct((2 * rows, 2 * hidden), BF16),
        ],
        input_output_aliases=aliases,
        compiler_params=params(),
        name="experts",
        cost_estimate=pl.CostEstimate(
            flops=12 * rows * width * hidden,
            bytes_accessed=6 * width * hidden + 16 * rows * width,
            transcendentals=0,
        ),
    )(*operands)


def gradient_kernel(jobs, lefts, rights, keep, *refs):
    left_refs, right_refs, rest = refs[:lefts], refs[lefts : lefts + rights], refs[lefts + rights :]
    step = pl.program_id(0)
    each = len(jobs[0])
    for i, (left, right, _) in enumerate(jobs[0] + jobs[1]):

        @pl.when(step == i)
        def _(i=i, left=left, right=right):
            side = i // each
            value = mm(left_refs[left][...], right_refs[right][...])
            if keep:
                value = value + rest[0][0].astype(F32)
                half = value.shape[0] // 2
                rest[1 + 2 * side][...] = value[:half].astype(BF16)
                rest[2 + 2 * side][...] = value[half:].astype(BF16)
            else:
                rest[0][0] = value.astype(BF16)


def pick(i, values):
    result = values[0]
    for at, value in enumerate(values):
        if at and value != values[at - 1]:
            result = jnp.where(i >= at, value, result)
    return result


def gradients(jobs, lefts, rights, got=None, chunk=768):
    rows, tokens = lefts[0].shape
    each = len(jobs[0])
    first = lambda i: (0, jnp.minimum(i, each - 1))
    second = lambda i: (0, jnp.maximum(i - each, 0))
    whole = [pl.BlockSpec((1, rows, chunk), lambda i: (i // each, 0, i % each))]
    if got is None:
        out_specs = whole[0]
        out_shape = jax.ShapeDtypeStruct((2, rows, each * chunk), BF16)
    else:
        out_specs = [pl.BlockSpec((rows // 2, chunk), at) for at in (first, first, second, second)]
        out_shape = [jax.ShapeDtypeStruct((rows // 2, each * chunk), BF16)] * 4
    right_specs = []
    for r in range(len(rights)):
        at, blocks = None, []
        for _, right, block in jobs[0] + jobs[1]:
            at = block if right == r else at
            blocks.append(at)
        known = next(block for block in blocks if block is not None)
        blocks = tuple(known if block is None else block for block in blocks)
        right_specs.append(
            pl.BlockSpec((tokens, chunk), lambda i, blocks=blocks: (0, pick(i, blocks)))
        )
    return pl.pallas_call(
        functools.partial(gradient_kernel, jobs, len(lefts), len(rights), got is not None),
        grid=(2 * each,),
        in_specs=[
            *[pl.BlockSpec((rows, tokens), lambda i: (0, 0))] * len(lefts),
            *right_specs,
            *(() if got is None else whole),
        ],
        out_specs=out_specs,
        out_shape=out_shape,
        compiler_params=params(),
        name="gradients",
        cost_estimate=pl.CostEstimate(
            flops=4 * each * rows * tokens * chunk,
            bytes_accessed=4 * each * (rows + tokens) * chunk,
            transcendentals=0,
        ),
    )(*lefts, *rights, *(() if got is None else (got,)))


EXPERT_JOBS = (((0, 0, 0), (0, 0, 1), (1, 1, 0)), ((2, 0, 2), (2, 0, 3), (3, 1, 1)))
ATTENTION_JOBS = (((0, 0, 0), (0, 0, 1)), ((1, 1, 0), (1, 1, 1)))


def flip(index, mask):
    for bit in (1, 2, 4):
        if mask & bit:
            index = index + bit - 2 * bit * (index // bit % 2)
    return index


def finish_kernel(
    dx_ref,
    q_keep,
    q_send,
    o_keep,
    o_send,
    s_send,
    s_keep,
    back_ref,
    qo_ref,
    s_ref,
    q_got,
    o_got,
    q_half,
    o_half,
    q_last,
    o_last,
    s_got,
    s_half,
    s_got2,
    s_quarter,
    s_last,
    z_mine,
    z_got,
    k_mine,
    k_got,
    deal_send,
    deal_recv,
    send,
    recv,
):
    d = lax.axis_index("dp")
    z = lax.axis_index("tensor")
    count = dx_ref.shape[0]
    z_count = z_mine.shape[0]
    barrier = pltpu.get_barrier_semaphore()
    for p in range(1, count):
        pl.semaphore_signal(
            barrier, inc=1, device_id={"dp": flip(d, p)}, device_id_type=pl.DeviceIdType.MESH
        )
    for m in range(1, z_count):
        pl.semaphore_signal(
            barrier, inc=1, device_id={"tensor": flip(z, m)}, device_id_type=pl.DeviceIdType.MESH
        )
    pl.semaphore_wait(barrier, count - 1 + z_count - 1)

    def start(src, dst, at, to):
        copy = pltpu.make_async_remote_copy(
            src_ref=src,
            dst_ref=dst,
            send_sem=send.at[at],
            recv_sem=recv.at[at],
            device_id=to,
            device_id_type=pl.DeviceIdType.MESH,
        )
        copy.start()
        return copy

    one, two, four = [{"dp": flip(d, bit)} for bit in (1, 2, 4)]
    s_one = start(s_send, s_got, 0, one)
    q_one = start(q_send, q_got, 1, two)
    o_one = start(o_send, o_got, 2, four)
    deals = []
    for p in range(1, count):
        copy = pltpu.make_async_remote_copy(
            src_ref=dx_ref.at[flip(d, p)],
            dst_ref=back_ref.at[d],
            send_sem=deal_send.at[p - 1],
            recv_sem=deal_recv.at[p - 1],
            device_id={"dp": flip(d, p)},
            device_id_type=pl.DeviceIdType.MESH,
        )
        copy.start()
        deals.append(copy)
    back_ref[d] = dx_ref[d]

    rows = q_last.shape[0]
    s_one.wait()
    total = s_keep[...].astype(F32) + s_got[...].astype(F32)
    s_keep2 = total[: 2 * rows]
    s_half[...] = total[2 * rows :].astype(BF16)
    s_two = start(s_half, s_got2, 3, four)
    q_one.wait()
    q_half[...] = (q_keep[rows:].astype(F32) + q_got[rows:].astype(F32)).astype(BF16)
    q_two = start(q_half, q_last, 4, four)
    o_one.wait()
    o_half[...] = (o_keep[rows:].astype(F32) + o_got[rows:].astype(F32)).astype(BF16)
    o_two = start(o_half, o_last, 5, two)
    s_two.wait()
    total = s_keep2 + s_got2[...].astype(F32)
    s_quarter[...] = total[rows:].astype(BF16)
    s_three = start(s_quarter, s_last, 6, two)
    s_own = total[:rows]
    s_three.wait()
    s_own = s_own + s_last[...].astype(F32)
    k_mine[...] = s_own.astype(BF16)
    finals = [
        start(k_mine, k_got.at[m - 1], 6 + m, {"tensor": flip(z, m)}) for m in range(1, z_count)
    ]
    part = qo_ref.shape[1] // 2
    for two_copy, keep, got, last, side in (
        (q_two, q_keep, q_got, q_last, 0),
        (o_two, o_keep, o_got, o_last, 1),
    ):
        two_copy.wait()
        total = (
            keep[:rows].astype(F32) + got[:rows].astype(F32) + last[...].astype(F32)
        )
        for i in range(z_count):
            block = total[:, i * part : (i + 1) * part]
            z_mine[i, :, side * part : (side + 1) * part] = block.astype(BF16)
    for m in range(1, z_count):
        at = 5 + z_count + m
        finals.append(start(z_mine.at[flip(z, m)], z_got.at[m - 1], at, {"tensor": flip(z, m)}))
    for copy in finals[: z_count - 1]:
        copy.wait()
    for m in range(z_count - 1):
        s_own = s_own + k_got[m].astype(F32)
    s_ref[...] = s_own
    for copy in finals[z_count - 1 :]:
        copy.wait()
    total = z_mine[z].astype(F32)
    for m in range(z_count - 1):
        total = total + z_got[m].astype(F32)
    qo_ref[...] = total
    for copy in deals:
        copy.wait()


def finish(dx, q_keep, q_send, o_keep, o_send, s_send, s_keep, z_count):
    count = dx.shape[0]
    rows = q_keep.shape[0] // 2
    columns = q_keep.shape[1]
    small = s_keep.shape[1]
    part = columns // z_count
    vmem = pl.BlockSpec(memory_space=pltpu.VMEM)
    dma = pltpu.SemaphoreType.DMA
    return pl.pallas_call(
        finish_kernel,
        in_specs=[vmem] * 7,
        out_specs=[vmem] * 3,
        out_shape=[
            jax.ShapeDtypeStruct(dx.shape, BF16),
            jax.ShapeDtypeStruct((rows, 2 * part), F32),
            jax.ShapeDtypeStruct((rows, small), F32),
        ],
        scratch_shapes=[
            pltpu.VMEM((2 * rows, columns), BF16),
            pltpu.VMEM((2 * rows, columns), BF16),
            pltpu.VMEM((rows, columns), BF16),
            pltpu.VMEM((rows, columns), BF16),
            pltpu.VMEM((rows, columns), BF16),
            pltpu.VMEM((rows, columns), BF16),
            pltpu.VMEM((4 * rows, small), BF16),
            pltpu.VMEM((2 * rows, small), BF16),
            pltpu.VMEM((2 * rows, small), BF16),
            pltpu.VMEM((rows, small), BF16),
            pltpu.VMEM((rows, small), BF16),
            pltpu.VMEM((z_count, rows, 2 * part), BF16),
            pltpu.VMEM((z_count - 1, rows, 2 * part), BF16),
            pltpu.VMEM((rows, small), BF16),
            pltpu.VMEM((z_count - 1, rows, small), BF16),
            dma((count - 1,)),
            dma((count - 1,)),
            dma((7 + 2 * z_count,)),
            dma((7 + 2 * z_count,)),
        ],
        compiler_params=pltpu.CompilerParams(
            vmem_limit_bytes=56 * 2**20, collective_id=0, has_side_effects=True
        ),
        name="finish",
    )(dx, q_keep, q_send, o_keep, o_send, s_send, s_keep)


def turn_kernel(orders, d_ref, *refs):
    tiles = len(refs) - 1 - len(orders)
    scratch_ref = refs[-1]
    step = pl.program_id(0)
    for t in range(tiles):

        @pl.when(step == t)
        def _(t=t):
            scratch_ref[...] = refs[t][...].T

    for order, out_ref in zip(orders, refs[tiles:-1]):
        size = out_ref.shape[0] // len(order)
        for i, p in enumerate(order):
            block = jnp.bitwise_xor(d_ref[0], p)
            at = pl.multiple_of(block * size, size)
            out_ref[i * size : (i + 1) * size, :] = scratch_ref[pl.ds(at, size), :]


def turn(d, tiles, orders, blocks):
    rows, width = tiles[0].shape
    size = width // blocks
    return pl.pallas_call(
        functools.partial(turn_kernel, orders),
        grid_spec=pltpu.PrefetchScalarGridSpec(
            num_scalar_prefetch=1,
            grid=(len(tiles),),
            in_specs=[pl.BlockSpec((rows, width), lambda t, s: (0, 0))] * len(tiles),
            out_specs=[
                pl.BlockSpec((len(order) * size, rows), lambda t, s: (0, t)) for order in orders
            ],
            scratch_shapes=[pltpu.VMEM((width, rows), BF16)],
        ),
        out_shape=[
            jax.ShapeDtypeStruct((len(order) * size, rows * len(tiles)), BF16) for order in orders
        ],
        compiler_params=params(),
        name="turn",
        cost_estimate=pl.CostEstimate(
            flops=0, bytes_accessed=6 * rows * width * len(tiles), transcendentals=0
        ),
    )(d, *tiles)


def tie(*values):
    return lax.optimization_barrier(values)


def row_major(x):
    return with_layout_constraint(x, Layout(major_to_minor=tuple(range(x.ndim))))


def per_device(
    tokens,
    perm,
    routes,
    gates,
    lengths,
    cotangent,
    gain_attn,
    w_query,
    w_keyval,
    w_out,
    gain_moe,
    w_gate,
    w_up,
    w_down,
):
    dp_count = lax.axis_size("dp")
    tensor_count = lax.axis_size("tensor")
    d = lax.axis_index("dp")
    z = lax.axis_index("tensor")
    rows, width = tokens.shape
    group_rows = perm.shape[0]
    share = rows // dp_count
    top = routes.shape[1]
    experts_n, _, part_hidden = w_gate.shape
    hidden = experts_n * part_hidden
    capacity = 9 * group_rows * top // (8 * experts_n)
    kv_heads = w_keyval.shape[1] // (2 * HD)
    query_cols = w_query.shape[1]
    team = 8
    teams = [[t * team + i for i in range(team)] for t in range(dp_count // team)]
    teams = None if len(teams) == 1 else teams
    piece_rows = width // team
    member = d % team

    def z_move(x, pairs):
        return lax.ppermute(x, "tensor", pairs)

    def dp_move(x, bit):
        return lax.ppermute(x, "dp", [(i, i ^ bit) for i in range(dp_count)])

    near, far, across = [[(i, i ^ m) for i in range(tensor_count)] for m in (1, 2, 3)]
    up_one, up_two = [[(i, i + m) for i in range(tensor_count - m)] for m in (1, 2)]

    def deal(x):
        return lax.all_to_all(
            x.reshape(dp_count, share, x.shape[1]), "dp", split_axis=0, concat_axis=0, tiled=True
        ).reshape(rows, x.shape[1])

    def team_gather(x):
        return lax.all_gather(x, "dp", axis=0, tiled=True, axis_index_groups=teams)

    def flat(w):
        return row_major(w.transpose(1, 0, 2).reshape(w.shape[1], hidden))

    def z_gather(x):
        parts = jnp.zeros((tensor_count, *x.shape), x.dtype)
        for m, part in enumerate((x, z_move(x, near), z_move(x, far), z_move(x, across))):
            parts = lax.dynamic_update_slice_in_dim(parts, part[None], z ^ m, 0)
        return parts

    own_perm = lax.dynamic_slice_in_dim(perm, z * rows, rows, 0)
    own_routes = lax.dynamic_slice_in_dim(routes, z * rows, rows, 0)
    dest = own_perm // group_rows
    place = own_perm % rows
    row_index = jnp.arange(rows, dtype=jnp.int32)
    lower = (row_index[:, None] > row_index[None, :]).astype(BF16)
    dest_hot = (dest[:, None] == jnp.arange(dp_count, dtype=jnp.int32)[None, :]).astype(BF16)
    earlier = jnp.sum(mm(lower, dest_hot) * dest_hot.astype(F32), axis=1).astype(jnp.int32)
    slot = dest * share + earlier
    pack = (row_index[:, None] == slot[None, :]).astype(BF16)
    meta = jnp.concatenate(
        [
            (place // 16)[:, None].astype(BF16),
            (place % 16)[:, None].astype(BF16),
            own_routes.astype(BF16),
            gates,
            jnp.zeros((rows, META - 2 - 2 * top), BF16),
        ],
        axis=1,
    )
    packed = mm(pack, jnp.concatenate([tokens, meta], axis=1)).astype(BF16)
    packed, pack, w_query, w_out, w_gate, w_up, w_down = tie(
        packed, pack, w_query, w_out, w_gate, w_up, w_down
    )
    arrived = deal(packed)
    packed_dy = mm(pack, cotangent).astype(BF16)
    wg_own = flat(w_gate)
    wq_piece = lax.dynamic_slice_in_dim(w_query, member * piece_rows, piece_rows, 0)
    wq_z = z_gather(wq_piece)

    out_rows = query_cols // team
    wo_piece = lax.dynamic_slice_in_dim(w_out, member * out_rows, out_rows, 0)
    wo_z = z_gather(wo_piece)
    wd_own = w_down.reshape(hidden, width)
    wu_own = flat(w_up)
    gu_piece = jnp.concatenate(
        [
            lax.dynamic_slice_in_dim(w, member * piece_rows, piece_rows, 0)
            for w in (wg_own, wu_own)
        ],
        axis=1,
    )
    hidden_piece = hidden // team
    wd_piece = lax.dynamic_slice_in_dim(wd_own, member * hidden_piece, hidden_piece, 0)
    gu_moved = z_move(gu_piece, far)
    arrived, packed_dy, wq_z, wo_z, wg_own, wu_own, wd_piece = tie(
        arrived, packed_dy, wq_z, wo_z, wg_own, wu_own, wd_piece
    )
    wq_all = team_gather(wq_z).reshape(team, tensor_count, piece_rows, query_cols)
    wo_all = team_gather(wo_z).reshape(team, tensor_count, out_rows, width)
    wo = wo_all.transpose(1, 0, 2, 3).reshape(tensor_count * query_cols, width)

    meta_in = arrived[:, width:].astype(F32)
    place_in = (meta_in[:, 0] * 16.0 + meta_in[:, 1]).astype(jnp.int32)
    unpack = (row_index[:, None] == place_in[None, :]).astype(BF16)
    dealt = mm(unpack, arrived)
    x_rows = dealt[:, :width]
    meta_rows = dealt[:, width:]

    expert_ids = jnp.arange(experts_n, dtype=jnp.int32).astype(F32)
    route_rows = meta_rows[:, 2 : 2 + top]
    gate_rows = meta_rows[:, 2 + top : 2 + 2 * top]
    hot = route_rows[:, :, None] == expert_ids[None, None, :]
    routed = jnp.sum(hot.astype(F32), axis=1)
    counts = jnp.pad(jnp.sum(routed, axis=0)[None, :], ((0, 7), (0, HD - experts_n)))

    seq_lengths = lengths[0]
    seq_index = jnp.arange(seq_lengths.shape[0], dtype=jnp.int32)
    seq_ends = jnp.sum(
        jnp.where(seq_index[None, :] <= seq_index[:, None], seq_lengths[None, :], 0), axis=1
    ).astype(jnp.int32)
    global_row = z * rows + row_index
    start = jnp.max(
        jnp.where(global_row[:, None] >= seq_ends[None, :], seq_ends[None, :], 0), axis=1
    ).astype(jnp.int32)
    offset = (global_row - start).astype(F32)
    frequency = ROPE_BASE ** (-2.0 * jnp.arange(HD // 2, dtype=F32) / HD)
    angles = offset[:, None] * frequency[None, :]
    cosine, sine = jnp.cos(angles), jnp.sin(angles)
    cos_full = jnp.concatenate([cosine, cosine], axis=1)
    sin_full = jnp.concatenate([-sine, sine], axis=1)
    start = start[:, None]
    z_arg = z.astype(jnp.int32)[None]

    inv_one = lax.rsqrt(jnp.mean(x_rows * x_rows, axis=1, keepdims=True) + EPS)
    n1 = (x_rows * inv_one * gain_attn).astype(BF16)
    weight = jnp.sum(jnp.where(hot, gate_rows[:, :, None], 0.0), axis=1)
    marks = jnp.pad(
        jnp.concatenate([routed, weight], axis=1).astype(BF16), ((0, 0), (0, HD - 2 * experts_n))
    )
    kv, kv_one, kv_two, counts, marks_near, arrived_dy = keyval(
        n1,
        w_keyval,
        cos_full,
        sin_full,
        counts,
        marks,
        packed_dy.reshape(dp_count, share, width),
        tensor_count,
    )
    arrived_dy = arrived_dy.reshape(rows, width)
    kv, n1, gu_moved = tie(kv, n1, gu_moved)

    def kept_gates(routed, weight, at):
        block = (z - 1 - jnp.arange(tensor_count, dtype=jnp.int32)) % tensor_count
        base = jnp.sum(
            jnp.where((block < at)[:, None], counts[:, 0, :experts_n], 0.0), axis=0
        )
        position = mm(lower, routed.astype(BF16)) + base[None, :]
        weight = jnp.where(position < capacity, weight, 0.0).astype(BF16)
        return row_major(jnp.repeat(weight, part_hidden, axis=1))

    gate_own = kept_gates(routed, weight, z)
    marks_near = marks_near.astype(F32)
    gate_near = kept_gates(
        marks_near[:, :experts_n], marks_near[:, experts_n : 2 * experts_n], z + 1 - 2 * (z % 2)
    )
    q = project_query(n1, wq_all, cos_full, sin_full)
    dy_rows = mm(unpack, arrived_dy).astype(BF16)
    q, dy_rows, gate_own, gate_near = tie(q, dy_rows, gate_own, gate_near)
    dy_near = z_move(dy_rows, near)
    kvs = (kv_two, kv_one, kv)
    o, lse = attend(z_arg, start, q, kvs, kv_heads)
    o, wd_piece, gu_moved, dy_near = tie(o, wd_piece, gu_moved, dy_near)
    gu_far = team_gather(gu_moved)
    h = x_rows + mm(o, wo)
    inv_two = lax.rsqrt(jnp.mean(h * h, axis=1, keepdims=True) + EPS)
    n2 = (h * inv_two * gain_moe).astype(BF16)

    halving = dp_count == 8
    d_arg = d.astype(jnp.int32)[None]
    out_w = width // dp_count
    orders_a = ((1, 5, 3, 7), (0, 4, 2, 6))
    orders_b = ((1, 3, 5, 7), (0, 2, 4, 6))

    def turned(tiles, *orders):
        if halving:
            return turn(d_arg, tiles, orders, dp_count)
        return [jnp.concatenate(tiles, axis=0).T] * len(orders)

    def dp_sum(x):
        return lax.psum_scatter(x, "dp", scatter_dimension=0, tiled=True)

    def unit_start(jobs, send_lefts, rights):
        return dp_move(gradients(jobs, send_lefts, rights), 1)

    def unit_keep(jobs, keep_lefts, rights, got):
        return gradients(jobs, keep_lefts, rights, got)

    def first_moves(parts):
        return parts[0], dp_move(parts[1], xy[0]), parts[2], dp_move(parts[3], yx[0])

    def second_moves(moved):
        halves = []
        for keep, got, bit in ((*moved[:2], xy[1]), (*moved[2:], yx[1])):
            x = keep.astype(F32) + got.astype(F32)
            half = x.shape[0] // 2
            halves += [x[:half], dp_move(x[half:].astype(BF16), bit)]
        return halves

    def unit_end(moved):
        return moved[0] + moved[1].astype(F32), moved[2] + moved[3].astype(F32)

    def expert_lefts(n_a, d_a, keep):
        return n_a[keep], d_a[keep], n_a[2 + keep], d_a[2 + keep]

    xy, yx = (2, 4), (4, 2)
    n2_near = z_move(n2, near)
    ff = gu_far.shape[1] // 1024
    y, dn2, *own_grads = experts(0, n2, dy_rows, gate_own, wg_own, wu_own, wd_own)
    n2_near, y, dy_near, wd_piece = tie(n2_near, y, dy_near, wd_piece)
    wd_moved = z_move(wd_piece, far)
    wd_far = team_gather(wd_moved)
    yn, dnn, *own_grads = experts(
        1, n2_near, dy_near, gate_near, wg_own, wu_own, wd_own, filled=own_grads
    )
    dy_a = turned((dy_rows, dy_near), *orders_a, *orders_b)
    n2_a = turned((n2, n2_near), *orders_a, *orders_b)
    if halving:
        own_grads = own_grads[::-1]
        got = unit_start(EXPERT_JOBS, expert_lefts(n2_a, dy_a, 0), own_grads)
        own = unit_keep(EXPERT_JOBS, expert_lefts(n2_a, dy_a, 1), own_grads, got)
        gu_far, *own = tie(gu_far, *own)
        own = first_moves(own)
    yn, dnn, *far_grads = experts(
        1, n2_near, dy_near, gate_near, gu_far, gu_far, wd_far, (yn, dnn), up_at=ff
    )
    dnn_moved = z_move(dnn.astype(BF16), near)
    yn_moved = z_move(yn.astype(BF16), near)
    y, dn2, *far_grads = experts(
        0, n2, dy_rows, gate_own, gu_far, gu_far, wd_far, (y, dn2), far_grads, up_at=ff
    )
    if halving:
        far_grads = far_grads[::-1]
        far_sent = gradients(EXPERT_JOBS, expert_lefts(n2_a, dy_a, 0), far_grads)
        dnn_moved, far_sent, *own = tie(dnn_moved, far_sent, *own)
        got = dp_move(far_sent, 1)
        own = second_moves(own)
    dn2 = dn2 + dnn_moved.astype(F32)

    gain_two_part = jnp.sum(dn2 * h * inv_two, axis=0)
    u2 = dn2 * gain_moe
    dh = dy_rows.astype(F32) + inv_two * (
        u2 - h * inv_two * inv_two * jnp.mean(u2 * h, axis=1, keepdims=True)
    )
    dhb = dh.astype(BF16)
    do = mm_nt(dhb, wo).astype(BF16)
    if halving:
        far_w = unit_keep(EXPERT_JOBS, expert_lefts(n2_a, dy_a, 1), far_grads, got)
        do, *far_w = tie(do, *far_w)
        far_w = first_moves(far_w)
    result = h + y + yn_moved.astype(F32)
    result_out = mm_tn(unpack, result.astype(BF16)).astype(BF16)
    do, result_out = tie(do, result_out)

    dq, dkv_two, dkv_one, dkv = attend_back(
        z_arg, start, q, o, do, lse, cos_full, sin_full, kvs, kv_heads
    )
    dkv_one = z_move(dkv_one, [(b, a) for a, b in up_one])
    dkv_two = z_move(dkv_two, [(b, a) for a, b in up_two])
    n1_t = turned((n1,), *orders_a, *orders_b)
    dhb_t = turned((dhb,), *orders_b)
    if halving:
        dq, *far_w = tie(dq, *far_w)
        far_w = second_moves(far_w)
        got = unit_start(ATTENTION_JOBS, (n1_t[0], dhb_t[0]), (dq, o))
        parts = unit_keep(ATTENTION_JOBS, (n1_t[1], dhb_t[1]), (dq, o), got)
        dkv_one, dkv_two, *rest = tie(dkv_one, dkv_two, *parts, *far_w)
        parts, far_w = rest[:4], rest[4:]
        far_sums = [z_move(part.astype(BF16), far) for part in unit_end(far_w)]
    else:
        sum_q, sum_o = [
            dp_sum(mm_tn(a, b).astype(BF16)).astype(F32) for a, b in ((n1, dq), (dhb, o))
        ]
    dkv = dkv + dkv_one.astype(F32) + dkv_two.astype(F32)

    def unrotate(u):
        swapped = jnp.concatenate([u[:, HD // 2 :], u[:, : HD // 2]], axis=1)
        return u * cos_full - swapped * sin_full

    dkv = jnp.concatenate(
        [unrotate(dkv[:, i * HD : (i + 1) * HD]) for i in range(kv_heads)]
        + [dkv[:, kv_heads * HD :]],
        axis=1,
    ).astype(BF16)
    dn1 = project_back(dq, wq_all, dkv, w_keyval)
    gain_one_part = jnp.sum(dn1 * x_rows * inv_one, axis=0)
    u1 = dn1 * gain_attn
    dx = dh + inv_one * (
        u1 - x_rows * inv_one * inv_one * jnp.mean(u1 * x_rows, axis=1, keepdims=True)
    )

    outputs = mm_tn(pack, deal(result_out)).astype(BF16)

    if halving:
        first, second = [a + b.astype(F32) for a, b in zip(unit_end(own), far_sums)]
        sum_gu = jnp.concatenate([first[:, :hidden], second[:, :hidden]], axis=1)
        sum_down = jnp.concatenate([first[:, hidden:], second[:, hidden:]], axis=1)
    else:
        lefts = (n2_a[0], dy_a[0])
        far_sums = [dp_sum(mm(a, b).astype(BF16)) for a, b in zip(lefts, far_grads[::-1])]
        own_sums = [dp_sum(mm(a, b).astype(BF16)) for a, b in zip(lefts, own_grads[::-1])]
        sum_gu, sum_down = [
            a.astype(F32) + z_move(b, far).astype(F32) for a, b in zip(own_sums, far_sums)
        ]
    sum_gu = sum_gu.reshape(out_w, hidden // 512, 2, 512)
    sum_gate, sum_up = [
        sum_gu[:, :, i].reshape(out_w, experts_n, part_hidden).transpose(1, 0, 2) for i in (0, 1)
    ]
    sum_down = sum_down.reshape(out_w, experts_n, part_hidden).transpose(1, 2, 0)

    gains = jnp.stack([gain_one_part, gain_two_part])

    def gain_columns(order):
        blocks = gains.reshape(2, dp_count, out_w)
        if halving:
            blocks = jnp.stack(
                [lax.dynamic_index_in_dim(blocks, d ^ p, 1, keepdims=False) for p in order], 1
            )
        return jnp.pad(blocks.reshape(2, -1).T, ((0, 0), (dkv.shape[1], HD - 2)))

    columns = [gain_columns(order) for order in orders_b]
    dkv_wide = jnp.pad(dkv, ((0, 0), (0, HD)))
    if halving:
        kv_send, kv_keep = [
            (mm(left, dkv_wide) + column).astype(BF16) for left, column in zip(n1_t[2:], columns)
        ]
        dx_out = mm_tn(unpack, dx.astype(BF16)).astype(BF16).reshape(dp_count, share, width)
        back, total, small = finish(dx_out, *parts, kv_send, kv_keep, tensor_count)
        grad_tokens = mm_tn(pack, back.reshape(rows, width)).astype(BF16)
    else:
        grad_tokens = mm_tn(pack, deal(mm_tn(unpack, dx.astype(BF16)).astype(BF16))).astype(BF16)
        small = dp_sum((mm(n1_t[3], dkv_wide) + columns[0]).astype(BF16))
        small = small.astype(F32) + sum(
            z_move(small, move).astype(F32) for move in (near, far, across)
        )

        def z_block(x, m):
            return lax.dynamic_slice_in_dim(x, (z ^ m) * query_cols, query_cols, 1)

        both = [jnp.concatenate([z_block(sum_q, m), z_block(sum_o, m)], axis=1) for m in range(4)]
        total = both[0] + sum(
            z_move(part.astype(BF16), move).astype(F32)
            for part, move in zip(both[1:], (near, far, across))
        )
    sum_query, sum_out = total[:, :query_cols], total[:, query_cols:].T
    kv_cols = w_keyval.shape[1]
    return (
        outputs,
        grad_tokens,
        small[:, kv_cols],
        sum_query,
        small[:, :kv_cols],
        sum_out,
        small[:, kv_cols + 1],
        sum_gate,
        sum_up,
        sum_down,
    )


def solution(mesh):
    in_specs = (
        P(("dp", "tensor"), None),
        P("dp"),
        P("dp", None),
        P(("dp", "tensor"), None),
        P("dp", None),
        P(("dp", "tensor"), None),
        P(),
        P(None, "tensor"),
        P(),
        P("tensor", None),
        P(),
        P(None, None, "tensor"),
        P(None, None, "tensor"),
        P(None, "tensor", None),
    )
    out_specs = (
        P(("dp", "tensor"), None),
        P(("dp", "tensor"), None),
        P("dp"),
        P("dp", "tensor"),
        P("dp", None),
        P("tensor", "dp"),
        P("dp"),
        P(None, "dp", "tensor"),
        P(None, "dp", "tensor"),
        P(None, "tensor", "dp"),
    )
    return jax.shard_map(
        per_device, mesh=mesh, in_specs=in_specs, out_specs=out_specs, check_vma=False
    )
```

```python
import functools

import jax
import jax.numpy as jnp
from jax import lax
from jax.experimental import pallas as pl
from jax.experimental.layout import Layout, with_layout_constraint
from jax.experimental.pallas import tpu as pltpu
from jax.sharding import PartitionSpec as P

HD = 128
EPS = 1e-06
ROPE_BASE = 1000000.0
MASKED = -1e30
LOG2E = 1.4426950408889634
F32 = jnp.float32
BF16 = jnp.bfloat16
META = 128


def mm(a, b):
    return lax.dot_general(a, b, (((1,), (0,)), ((), ())), preferred_element_type=F32)


def mm_nt(a, b):
    return lax.dot_general(a, b, (((1,), (1,)), ((), ())), preferred_element_type=F32)


def mm_tn(a, b):
    return lax.dot_general(a, b, (((0,), (0,)), ((), ())), preferred_element_type=F32)


def params(mb=56):
    return pltpu.CompilerParams(vmem_limit_bytes=mb * 2**20)


def swap_halves(u):
    return pltpu.roll(u, HD // 2, 1)


def open_kernel(
    deal_ref,
    q_ref,
    o_ref,
    dealt_ref,
    q_all,
    o_all,
    send,
    recv,
    deal_send,
    deal_recv,
):
    z = lax.axis_index("tensor")
    d = lax.axis_index("dp")
    d_count = deal_ref.shape[0]
    z_count = q_all.shape[0]
    others = [{"tensor": flip(z, m)} for m in range(1, z_count)]
    peers = [{"dp": (d + p) % d_count} for p in range(1, d_count)]
    barrier = pltpu.get_barrier_semaphore()
    for other in others + peers:
        pl.semaphore_signal(barrier, inc=1, device_id=other, device_id_type=pl.DeviceIdType.MESH)
    pl.semaphore_wait(barrier, len(others) + len(peers))
    moves = [(q_ref, q_all.at[m], others[m - 1]) for m in range(1, z_count)]
    moves += [(o_ref, o_all.at[z], other) for other in others]
    copies = []
    for p, peer in enumerate(peers):
        copy = pltpu.make_async_remote_copy(
            src_ref=deal_ref.at[(d + p + 1) % d_count],
            dst_ref=dealt_ref.at[d],
            send_sem=deal_send.at[p],
            recv_sem=deal_recv.at[p],
            device_id=peer,
            device_id_type=pl.DeviceIdType.MESH,
        )
        copy.start()
        copies.append(copy)
    for at, (src, dst, to) in enumerate(moves):
        copy = pltpu.make_async_remote_copy(
            src_ref=src,
            dst_ref=dst,
            send_sem=send.at[at],
            recv_sem=recv.at[at],
            device_id=to,
            device_id_type=pl.DeviceIdType.MESH,
        )
        copy.start()
        copies.append(copy)
    dealt_ref[d] = deal_ref[d]
    q_all[0] = q_ref[...]
    o_all[z] = o_ref[...]
    for copy in copies:
        copy.wait()


def open_moves(deals, q, o, z_count):
    vmem = pl.BlockSpec(memory_space=pltpu.VMEM)
    shapes = [deals.shape, (z_count, *q.shape), (z_count, *o.shape)]
    moves = 2 * (z_count - 1)
    return pl.pallas_call(
        open_kernel,
        in_specs=[vmem] * 3,
        out_specs=[vmem] * 3,
        out_shape=[jax.ShapeDtypeStruct(shape, BF16) for shape in shapes],
        scratch_shapes=[
            pltpu.SemaphoreType.DMA((moves,)),
            pltpu.SemaphoreType.DMA((moves,)),
            pltpu.SemaphoreType.DMA((deals.shape[0] - 1,)),
            pltpu.SemaphoreType.DMA((deals.shape[0] - 1,)),
        ],
        compiler_params=pltpu.CompilerParams(
            vmem_limit_bytes=40 * 2**20, collective_id=4, has_side_effects=True
        ),
        name="open_moves",
    )(deals, q, o)


def keyval_kernel(
    x_ref,
    w_ref,
    cos_ref,
    sin_ref,
    count_ref,
    mark_ref,
    deal_ref,
    kv_ref,
    one_ref,
    two_ref,
    counts_ref,
    near_ref,
    dealt_ref,
    send,
    recv,
    deal_send,
    deal_recv,
):
    z = lax.axis_index("tensor")
    d = lax.axis_index("dp")
    d_count = deal_ref.shape[0]
    z_count = counts_ref.shape[0]
    others = [{"tensor": (z + m) % z_count} for m in range(1, z_count)]
    barrier = pltpu.get_barrier_semaphore()
    peers = [{"dp": (d + p) % d_count} for p in range(1, d_count)]
    for other in others + peers:
        pl.semaphore_signal(barrier, inc=1, device_id=other, device_id_type=pl.DeviceIdType.MESH)
    raw = mm(x_ref[...], w_ref[...])
    turned = raw.shape[1] // 2
    for i in range(turned // HD):
        u = raw[:, i * HD : (i + 1) * HD]
        u = u * cos_ref[...] + swap_halves(u) * sin_ref[...]
        kv_ref[:, i * HD : (i + 1) * HD] = u.astype(BF16)
    kv_ref[:, turned:] = raw[:, turned:].astype(BF16)
    pl.semaphore_wait(barrier, z_count - 1 + d_count - 1)
    moves = [(count_ref, counts_ref.at[m], others[m]) for m in range(z_count - 1)]
    moves += [(mark_ref, near_ref, {"tensor": flip(z, 1)})]
    moves += [(kv_ref, one_ref, others[0]), (one_ref, two_ref, others[0])]
    copies = []
    for at, (src, dst, to) in enumerate(moves):
        copy = pltpu.make_async_remote_copy(
            src_ref=src,
            dst_ref=dst,
            send_sem=send.at[at],
            recv_sem=recv.at[at],
            device_id=to,
            device_id_type=pl.DeviceIdType.MESH,
        )
        copies.append(copy)
    for copy in copies[:-1]:
        copy.start()
    for p, peer in enumerate(peers):
        copy = pltpu.make_async_remote_copy(
            src_ref=deal_ref.at[(d + p + 1) % d_count],
            dst_ref=dealt_ref.at[d],
            send_sem=deal_send.at[p],
            recv_sem=deal_recv.at[p],
            device_id=peer,
            device_id_type=pl.DeviceIdType.MESH,
        )
        copy.start()
        copies.append(copy)
    counts_ref[z_count - 1] = count_ref[...]
    dealt_ref[d] = deal_ref[d]
    step_one, step_two = copies[z_count], copies[z_count + 1]
    step_one.wait()
    step_two.start()
    for copy in copies[:z_count] + copies[z_count + 1 :]:
        copy.wait()


def keyval(x, w, cos_full, sin_full, counts, marks, deals, z_count):
    rows = x.shape[0]
    columns = w.shape[1]
    vmem = pl.BlockSpec(memory_space=pltpu.VMEM)
    block = jax.ShapeDtypeStruct((rows, columns), BF16)
    return pl.pallas_call(
        keyval_kernel,
        in_specs=[vmem] * 7,
        out_specs=[vmem] * 6,
        out_shape=[block] * 3
        + [
            jax.ShapeDtypeStruct((z_count, *counts.shape), counts.dtype),
            jax.ShapeDtypeStruct(marks.shape, marks.dtype),
            jax.ShapeDtypeStruct(deals.shape, deals.dtype),
        ],
        scratch_shapes=[
            pltpu.SemaphoreType.DMA((z_count + 2,)),
            pltpu.SemaphoreType.DMA((z_count + 2,)),
            pltpu.SemaphoreType.DMA((deals.shape[0] - 1,)),
            pltpu.SemaphoreType.DMA((deals.shape[0] - 1,)),
        ],
        compiler_params=pltpu.CompilerParams(
            vmem_limit_bytes=40 * 2**20, collective_id=1, has_side_effects=True
        ),
        name="keyval",
    )(x, w, cos_full, sin_full, counts, marks, deals)


def project_query_kernel(z_ref, x_ref, w_ref, cos_ref, sin_ref, out_ref):
    raw = mm(x_ref[...], w_ref[...].reshape(x_ref.shape[1], out_ref.shape[1]))
    for i in range(raw.shape[1] // HD):
        u = raw[:, i * HD : (i + 1) * HD]
        turned = u * cos_ref[...] + swap_halves(u) * sin_ref[...]
        out_ref[:, i * HD : (i + 1) * HD] = (turned * SCALE).astype(BF16)


def project_query(z, x, w, cos_full, sin_full):
    rows, width = x.shape
    pieces, blocks, piece, columns = w.shape
    return pl.pallas_call(
        project_query_kernel,
        grid_spec=pltpu.PrefetchScalarGridSpec(
            num_scalar_prefetch=1,
            grid=(blocks,),
            in_specs=[
                pl.BlockSpec((rows, width), lambda i, s: (0, 0)),
                pl.BlockSpec(
                    (pieces, 1, piece, columns), lambda i, s: (0, jnp.bitwise_xor(i, s[0]), 0, 0)
                ),
                pl.BlockSpec((rows, HD), lambda i, s: (0, 0)),
                pl.BlockSpec((rows, HD), lambda i, s: (0, 0)),
            ],
            out_specs=pl.BlockSpec((rows, columns), lambda i, s: (0, i)),
        ),
        out_shape=jax.ShapeDtypeStruct((rows, blocks * columns), BF16),
        compiler_params=params(),
        name="project_query",
        cost_estimate=pl.CostEstimate(
            flops=2 * rows * width * blocks * columns,
            bytes_accessed=2 * (2 * rows * width + width * blocks * columns),
            transcendentals=0,
        ),
    )(z, x, w, cos_full, sin_full)


def project_back_kernel(z_ref, dq_ref, w_ref, dkv_ref, wkv_ref, out_ref):
    step = pl.program_id(0)
    width = out_ref.shape[1]
    part = mm_nt(dq_ref[...], w_ref[...].reshape(width, dq_ref.shape[1]))

    @pl.when(step == 0)
    def _():
        out_ref[...] = part + mm_nt(dkv_ref[...], wkv_ref[...])

    @pl.when(step > 0)
    def _():
        out_ref[...] += part


def project_back(z, dq, w, dkv, wkv):
    rows = dq.shape[0]
    pieces, blocks, piece, columns = w.shape
    width = pieces * piece
    return pl.pallas_call(
        project_back_kernel,
        grid_spec=pltpu.PrefetchScalarGridSpec(
            num_scalar_prefetch=1,
            grid=(blocks,),
            in_specs=[
                pl.BlockSpec((rows, columns), lambda i, s: (0, i)),
                pl.BlockSpec(
                    (pieces, 1, piece, columns), lambda i, s: (0, jnp.bitwise_xor(i, s[0]), 0, 0)
                ),
                pl.BlockSpec(dkv.shape, lambda i, s: (0, 0)),
                pl.BlockSpec(wkv.shape, lambda i, s: (0, 0)),
            ],
            out_specs=pl.BlockSpec((rows, width), lambda i, s: (0, 0)),
        ),
        out_shape=jax.ShapeDtypeStruct((rows, width), F32),
        compiler_params=params(),
        name="project_back",
        cost_estimate=pl.CostEstimate(
            flops=2 * rows * width * (blocks * columns + dkv.shape[1]),
            bytes_accessed=2 * width * (3 * rows + blocks * columns),
            transcendentals=0,
        ),
    )(z, dq, w, dkv, wkv)


ATTEND_TILE = 256
SCALE = HD**-0.5 * LOG2E


def make_bias(z, start_ref, bias_ref):
    tiles, tile, width = bias_ref.shape
    rows = tiles * tile
    for i in range(tiles):
        key = (z - 2) * rows + i * tile + lax.broadcasted_iota(jnp.int32, (tile, width), 1)
        query = z * rows + i * tile + lax.broadcasted_iota(jnp.int32, (tile, width), 0)
        allowed = (key >= start_ref[i * tile : (i + 1) * tile]) & (key <= query)
        bias_ref[i] = jnp.where(allowed, 0.0, MASKED)


def attend_kernel(
    kv_heads, z_ref, start_ref, q_ref, kv0_ref, kv1_ref, kv2_ref, o_ref, lse_ref, bias_ref, k_ref, v_ref
):
    head = pl.program_id(0)
    each = pl.num_programs(0) // kv_heads
    rows = q_ref.shape[0]
    tiles, tile, width = bias_ref.shape

    @pl.when(head == 0)
    def _():
        make_bias(z_ref[0], start_ref, bias_ref)
        v_ref[:, HD:] = jnp.ones((v_ref.shape[0], HD), BF16)

    @pl.when(head % each == 0)
    def _():
        kvh = head // each
        for j, ref in enumerate((kv0_ref, kv1_ref, kv2_ref)):
            at = slice(j * rows, (j + 1) * rows)
            k_ref[at] = ref[:, pl.ds(pl.multiple_of(kvh * HD, HD), HD)]
            v_ref[at, :HD] = ref[:, pl.ds(pl.multiple_of((kv_heads + kvh) * HD, HD), HD)]

    for i in range(tiles):
        at, window = slice(i * tile, (i + 1) * tile), slice(i * tile, i * tile + width)
        score = mm_nt(q_ref[at], k_ref[window]) + bias_ref[i]
        peak = jnp.max(score, axis=1, keepdims=True)
        mixed = mm(jnp.exp2(score - peak).astype(BF16), v_ref[window])
        total = mixed[:, HD : HD + 1]
        o_ref[at] = (mixed[:, :HD] / total).astype(BF16)
        lse_ref[0, at] = peak + jnp.log2(total)


def attend(z, start, q, kvs, kv_heads):
    rows, columns = q.shape
    heads = columns // HD
    tile = ATTEND_TILE
    kv_spec = pl.BlockSpec(kvs[0].shape, lambda h, s: (0, 0))
    return pl.pallas_call(
        functools.partial(attend_kernel, kv_heads),
        grid_spec=pltpu.PrefetchScalarGridSpec(
            num_scalar_prefetch=1,
            grid=(heads,),
            in_specs=[
                pl.BlockSpec((rows, 1), lambda h, s: (0, 0)),
                pl.BlockSpec((rows, HD), lambda h, s: (0, h)),
                *[kv_spec] * 3,
            ],
            out_specs=[
                pl.BlockSpec((rows, HD), lambda h, s: (0, h)),
                pl.BlockSpec((1, rows, 1), lambda h, s: (h, 0, 0)),
            ],
            scratch_shapes=[
                pltpu.VMEM((rows // tile, tile, 2 * rows + tile), F32),
                pltpu.VMEM((3 * rows, HD), BF16),
                pltpu.VMEM((3 * rows, 2 * HD), BF16),
            ],
        ),
        out_shape=[
            jax.ShapeDtypeStruct((rows, columns), BF16),
            jax.ShapeDtypeStruct((heads, rows, 1), F32),
        ],
        compiler_params=params(),
        name="attend",
        cost_estimate=pl.CostEstimate(
            flops=12 * rows * rows * columns,
            bytes_accessed=8 * rows * columns,
            transcendentals=rows * rows * 3 * heads,
        ),
    )(z, start, q, *kvs)


def attend_back_kernel(
    kv_heads,
    z_ref,
    start_ref,
    q_ref,
    o_ref,
    do_ref,
    lse_ref,
    cos_ref,
    sin_ref,
    kv0_ref,
    kv1_ref,
    kv2_ref,
    dq_ref,
    d0_ref,
    d1_ref,
    d2_ref,
    bias_ref,
    k_ref,
    v_ref,
    dk_ref,
    dv_ref,
):
    head = pl.program_id(0)
    each = pl.num_programs(0) // kv_heads
    rows = q_ref.shape[0]
    tiles, tile, width = bias_ref.shape
    kvh = head // each
    kcol = pl.ds(pl.multiple_of(kvh * HD, HD), HD)
    vcol = pl.ds(pl.multiple_of((kv_heads + kvh) * HD, HD), HD)

    @pl.when(head == 0)
    def _():
        make_bias(z_ref[0], start_ref, bias_ref)

    @pl.when(head % each == 0)
    def _():
        for j, ref in enumerate((kv0_ref, kv1_ref, kv2_ref)):
            k_ref[j * rows : (j + 1) * rows] = ref[:, kcol]
            v_ref[j * rows : (j + 1) * rows] = ref[:, vcol]
        dk_ref[...] = jnp.zeros_like(dk_ref)
        dv_ref[...] = jnp.zeros_like(dv_ref)

    for i in range(tiles):
        at, window = slice(i * tile, (i + 1) * tile), slice(i * tile, i * tile + width)
        q = q_ref[at]
        do = do_ref[at]
        centre = jnp.sum(do.astype(F32) * o_ref[at].astype(F32), axis=1, keepdims=True)
        soft = jnp.exp2(mm_nt(q, k_ref[window]) + (bias_ref[i] - lse_ref[0, at]))
        dv_ref[window] += mm_tn(soft.astype(BF16), do)
        dscore = (soft * (mm_nt(do, v_ref[window]) - centre)).astype(BF16)
        dk_ref[window] += mm_tn(dscore, q)
        dq = mm(dscore, k_ref[window]) * (HD**-0.5)
        dq_ref[at] = (dq * cos_ref[at] - swap_halves(dq) * sin_ref[at]).astype(BF16)

    @pl.when(head % each == each - 1)
    def _():
        for j, ref in enumerate((d0_ref, d1_ref, d2_ref)):
            at = slice(j * rows, (j + 1) * rows)
            ref[:, kcol] = (dk_ref[at] * (1 / LOG2E)).astype(ref.dtype)
            ref[:, vcol] = dv_ref[at].astype(ref.dtype)


def attend_back(z, start, q, o, do, lse, cos_full, sin_full, kvs, kv_heads):
    rows, columns = q.shape
    heads = columns // HD
    tile = ATTEND_TILE
    kv_columns = kvs[0].shape[1]
    kv_spec = pl.BlockSpec((rows, kv_columns), lambda h, s: (0, 0))
    head_spec = pl.BlockSpec((rows, HD), lambda h, s: (0, h))
    table_spec = pl.BlockSpec((rows, HD), lambda h, s: (0, 0))
    return pl.pallas_call(
        functools.partial(attend_back_kernel, kv_heads),
        grid_spec=pltpu.PrefetchScalarGridSpec(
            num_scalar_prefetch=1,
            grid=(heads,),
            in_specs=[
                pl.BlockSpec((rows, 1), lambda h, s: (0, 0)),
                head_spec,
                head_spec,
                head_spec,
                pl.BlockSpec((1, rows, 1), lambda h, s: (h, 0, 0)),
                table_spec,
                table_spec,
                *[kv_spec] * 3,
            ],
            out_specs=[head_spec, *[kv_spec] * 3],
            scratch_shapes=[
                pltpu.VMEM((rows // tile, tile, 2 * rows + tile), F32),
                pltpu.VMEM((3 * rows, HD), BF16),
                pltpu.VMEM((3 * rows, HD), BF16),
                pltpu.VMEM((3 * rows, HD), F32),
                pltpu.VMEM((3 * rows, HD), F32),
            ],
        ),
        out_shape=[
            jax.ShapeDtypeStruct((rows, columns), BF16),
            jax.ShapeDtypeStruct((rows, kv_columns), BF16),
            jax.ShapeDtypeStruct((rows, kv_columns), BF16),
            jax.ShapeDtypeStruct((rows, kv_columns), F32),
        ],
        compiler_params=params(),
        name="attend_back",
        cost_estimate=pl.CostEstimate(
            flops=30 * rows * rows * columns,
            bytes_accessed=12 * rows * columns,
            transcendentals=rows * rows * 3 * heads,
        ),
    )(z, start, q, o, do, lse, cos_full, sin_full, *kvs)


def expert_kernel(chunk, first, x_ref, dy_ref, gate_ref, wg_ref, wu_ref, wd_ref, *refs):
    y_ref, dn_ref, hs_ref, dgu_ref = refs[-4:]
    step = pl.program_id(0)

    @pl.when(step == 0)
    def _():
        if first:
            y_ref[...] = jnp.zeros_like(y_ref)
            dn_ref[...] = jnp.zeros_like(dn_ref)
        else:
            y_ref[...] = refs[0][...]
            dn_ref[...] = refs[1][...]

    x = x_ref[...]
    gate = gate_ref[...].astype(F32)
    g = jnp.maximum(mm_nt(x, wg_ref[...]), 0.0)
    u = mm_nt(x, wu_ref[...])
    square = g * g
    hs = ((square * u).astype(BF16).astype(F32) * gate).astype(BF16)
    hs_ref[...] = hs
    dh = mm_nt(dy_ref[...], wd_ref[...]) * gate
    dg = (dh * u * (2.0 * g)).astype(BF16)
    du = (dh * square).astype(BF16)
    dgu_ref[:, :chunk] = dg
    dgu_ref[:, chunk:] = du
    dn_ref[...] += mm(dg, wg_ref[...]) + mm(du, wu_ref[...])
    y_ref[...] += mm(hs, wd_ref[...])


def experts(tile, x, dy, gate, wg, wu, wd, before=None, filled=None, chunk=512):
    rows, width = x.shape
    hidden = gate.shape[1]
    full = pl.BlockSpec((rows, width), lambda i: (0, 0))
    part = pl.BlockSpec((rows, chunk), lambda i: (0, i))
    operands = [x, dy, gate, wg, wu, wd]
    in_specs = [
        full,
        full,
        part,
        *[pl.BlockSpec((chunk, width), lambda i: (i, 0))] * 3,
    ]
    aliases = {}
    if before is not None:
        operands += list(before)
        in_specs += [full] * 2
    if filled is not None:
        aliases = {len(operands): 2, len(operands) + 1: 3}
        operands += list(filled)
        in_specs += [pl.BlockSpec(memory_space=pl.ANY)] * 2
    return pl.pallas_call(
        functools.partial(expert_kernel, chunk, before is None),
        grid=(hidden // chunk,),
        in_specs=in_specs,
        out_specs=[
            full,
            full,
            pl.BlockSpec((rows, chunk), lambda i: (tile, i)),
            pl.BlockSpec((rows, 2 * chunk), lambda i: (tile, i)),
        ],
        out_shape=[
            jax.ShapeDtypeStruct((rows, width), F32),
            jax.ShapeDtypeStruct((rows, width), F32),
            jax.ShapeDtypeStruct((2 * rows, hidden), BF16),
            jax.ShapeDtypeStruct((2 * rows, 2 * hidden), BF16),
        ],
        input_output_aliases=aliases,
        compiler_params=params(),
        name="experts",
        cost_estimate=pl.CostEstimate(
            flops=12 * rows * width * hidden,
            bytes_accessed=6 * width * hidden + 16 * rows * width,
            transcendentals=0,
        ),
    )(*operands)


def pick(i, values):
    result = values[0]
    for at, value in enumerate(values):
        if at and value != values[at - 1]:
            result = jnp.where(i >= at, value, result)
    return result


def gradient_kernel(jobs, lefts, rights, *refs):
    send_refs, keep_refs, right_refs = refs[:lefts], refs[lefts : 2 * lefts], refs[2 * lefts :]
    outs, (sent, got, send, recv) = right_refs[rights:-4], refs[-4:]
    d = lax.axis_index("dp")
    step = pl.program_id(0)
    count = len(jobs)

    @pl.when(step == 0)
    def _():
        barrier = pltpu.get_barrier_semaphore()
        pl.semaphore_signal(
            barrier, inc=1, device_id={"dp": flip(d, 1)}, device_id_type=pl.DeviceIdType.MESH
        )
        pl.semaphore_wait(barrier, 1)

    def copy(i):
        return pltpu.make_async_remote_copy(
            src_ref=sent.at[i],
            dst_ref=got.at[i],
            send_sem=send.at[i],
            recv_sem=recv.at[i],
            device_id={"dp": flip(d, 1)},
            device_id_type=pl.DeviceIdType.MESH,
        )

    for i, (left, right, _) in enumerate(jobs):

        @pl.when(step == i)
        def _(i=i, left=left, right=right):
            sent[i] = mm(send_refs[left][...], right_refs[right][...]).astype(BF16)
            copy(i).start()

        @pl.when(step == count + i)
        def _(i=i, left=left, right=right):
            value = mm(keep_refs[left][...], right_refs[right][...])
            copy(i).wait()
            value = value + got[i].astype(F32)
            half = value.shape[0] // 2
            side = 2 * (i // (count // 2))
            outs[side][...] = value[:half].astype(BF16)
            outs[side + 1][...] = value[half:].astype(BF16)


def gradients(jobs, send_lefts, keep_lefts, rights, ident, chunk=768):
    rows, tokens = keep_lefts[0].shape
    count = len(jobs)
    each = count // 2
    first = lambda i: (0, jnp.clip(i - count, 0, each - 1))
    second = lambda i: (0, jnp.maximum(i - count - each, 0))
    right_specs = []
    for r in range(len(rights)):
        blocks, at = [], None
        for _, right, block in jobs + jobs:
            at = block if right == r else at
            blocks.append(at)
        known = next(block for block in blocks if block is not None)
        blocks = tuple(known if block is None else block for block in blocks)
        right_specs.append(
            pl.BlockSpec((tokens, chunk), lambda i, blocks=blocks: (0, pick(i, blocks)))
        )
    left = pl.BlockSpec((rows, tokens), lambda i: (0, 0), pipeline_mode=pl.Buffered(1))
    return pl.pallas_call(
        functools.partial(gradient_kernel, jobs, len(keep_lefts), len(rights)),
        grid=(2 * count,),
        in_specs=[*[left] * (2 * len(keep_lefts)), *right_specs],
        out_specs=[
            pl.BlockSpec((rows // 2, chunk), at) for at in (first, first, second, second)
        ],
        out_shape=[jax.ShapeDtypeStruct((rows // 2, each * chunk), BF16)] * 4,
        scratch_shapes=[
            pltpu.VMEM((count, rows, chunk), BF16),
            pltpu.VMEM((count, rows, chunk), BF16),
            pltpu.SemaphoreType.DMA((count,)),
            pltpu.SemaphoreType.DMA((count,)),
        ],
        compiler_params=pltpu.CompilerParams(
            vmem_limit_bytes=56 * 2**20, collective_id=ident, has_side_effects=True
        ),
        name="gradients",
        cost_estimate=pl.CostEstimate(flops=10**9, bytes_accessed=10**6, transcendentals=0),
    )(*send_lefts, *keep_lefts, *rights)


def part_kernel(jobs, lefts, rights, keep, *refs):
    left_refs, right_refs, rest = refs[:lefts], refs[lefts : lefts + rights], refs[lefts + rights :]
    step = pl.program_id(0)
    each = len(jobs) // 2
    for i, (left, right, _) in enumerate(jobs):

        @pl.when(step == i)
        def _(i=i, left=left, right=right):
            side = i // each
            value = mm(left_refs[left][...], right_refs[right][...])
            if keep:
                value = value + rest[0][0].astype(F32)
                half = value.shape[0] // 2
                rest[1 + 2 * side][...] = value[:half].astype(BF16)
                rest[2 + 2 * side][...] = value[half:].astype(BF16)
            else:
                rest[0][0] = value.astype(BF16)


def gradient_parts(jobs, lefts, rights, got=None, chunk=768):
    rows, tokens = lefts[0].shape
    each = len(jobs) // 2
    first = lambda i: (0, jnp.minimum(i, each - 1))
    second = lambda i: (0, jnp.maximum(i - each, 0))
    whole = [pl.BlockSpec((1, rows, chunk), lambda i: (i // each, 0, i % each))]
    if got is None:
        out_specs = whole[0]
        out_shape = jax.ShapeDtypeStruct((2, rows, each * chunk), BF16)
    else:
        out_specs = [pl.BlockSpec((rows // 2, chunk), at) for at in (first, first, second, second)]
        out_shape = [jax.ShapeDtypeStruct((rows // 2, each * chunk), BF16)] * 4
    right_specs = []
    for r in range(len(rights)):
        at, blocks = None, []
        for _, right, block in jobs:
            at = block if right == r else at
            blocks.append(at)
        known = next(block for block in blocks if block is not None)
        blocks = tuple(known if block is None else block for block in blocks)
        right_specs.append(
            pl.BlockSpec((tokens, chunk), lambda i, blocks=blocks: (0, pick(i, blocks)))
        )
    return pl.pallas_call(
        functools.partial(part_kernel, jobs, len(lefts), len(rights), got is not None),
        grid=(2 * each,),
        in_specs=[
            *[pl.BlockSpec((rows, tokens), lambda i: (0, 0))] * len(lefts),
            *right_specs,
            *(() if got is None else whole),
        ],
        out_specs=out_specs,
        out_shape=out_shape,
        compiler_params=params(),
        name="gradient_parts",
        cost_estimate=pl.CostEstimate(
            flops=4 * each * rows * tokens * chunk,
            bytes_accessed=4 * each * (rows + tokens) * chunk,
            transcendentals=0,
        ),
    )(*lefts, *rights, *(() if got is None else (got,)))


EXPERT_JOBS = ((0, 0, 0), (0, 0, 1), (1, 1, 0), (2, 0, 2), (2, 0, 3), (3, 1, 1))


def flip(index, mask):
    for bit in (1, 2, 4):
        if mask & bit:
            index = index + bit - 2 * bit * (index // bit % 2)
    return index


def mix_kernel(
    dq_ref,
    o_ref,
    n_send,
    n_keep,
    d_send,
    d_keep,
    one_ref,
    two_ref,
    fa_keep,
    fa_got,
    fb_keep,
    fb_got,
    q_keep,
    q_send,
    o_keep,
    o_send,
    got_one,
    far_ref,
    got_two,
    both_ref,
    sent,
    got,
    halves,
    lasts,
    send,
    recv,
):
    d = lax.axis_index("dp")
    z = lax.axis_index("tensor")
    z_count = lax.axis_size("tensor")
    pairs = [{"dp": flip(d, bit)} for bit in (1, 2, 4)]
    others = [{"tensor": (z + m) % z_count} for m in range(1, z_count)]
    barrier = pltpu.get_barrier_semaphore()
    for peer in pairs + others:
        pl.semaphore_signal(barrier, inc=1, device_id=peer, device_id_type=pl.DeviceIdType.MESH)
    pl.semaphore_wait(barrier, len(pairs) + len(others))

    def start(src, dst, at, to):
        copy = pltpu.make_async_remote_copy(
            src_ref=src,
            dst_ref=dst,
            send_sem=send.at[at],
            recv_sem=recv.at[at],
            device_id=to,
            device_id_type=pl.DeviceIdType.MESH,
        )
        copy.start()
        return copy

    step_two = start(two_ref, got_two, 1, others[-1])
    rows = halves.shape[1]
    far_copies = []
    for side, (keep, arrived) in enumerate(((fa_keep, fa_got), (fb_keep, fb_got))):
        total = keep[rows:].astype(F32) + arrived[rows:].astype(F32)
        halves[side] = total.astype(BF16)
        far_copies.append(start(halves.at[side], lasts.at[side], 2 + side, pairs[2 - side]))

    step_two.wait()
    both_ref[...] = (one_ref[...].astype(F32) + got_two[...].astype(F32)).astype(BF16)
    step_one = start(both_ref, got_one, 0, others[-1])
    columns = dq_ref.shape[1]
    chunk = columns // 4

    def at_chunk(i):
        return pl.ds(pl.multiple_of(i * chunk, chunk), chunk)

    sides = ((dq_ref, n_send, n_keep, q_keep, q_send), (o_ref, d_send, d_keep, o_keep, o_send))
    core_copies = []
    for side, (right, left, _, _, _) in enumerate(sides):

        def compute_send(i, carry, side=side, right=right, left=left):
            at = at_chunk(i)
            sent[side, :, at] = mm(left[...], right[:, at]).astype(BF16)
            return carry

        lax.fori_loop(0, 4, compute_send, 0)
        core_copies.append(start(sent.at[side], got.at[side], 4 + side, pairs[0]))
    for side, (right, _, left, keep, away) in enumerate(sides):
        core_copies[side].wait()

        def compute_keep(i, carry, side=side, right=right, left=left, keep=keep, away=away):
            at = at_chunk(i)
            value = mm(left[...], right[:, at]) + got[side, :, at].astype(F32)
            half = value.shape[0] // 2
            keep[:, at] = value[:half].astype(BF16)
            away[:, at] = value[half:].astype(BF16)
            return carry

        lax.fori_loop(0, 4, compute_keep, 0)
    for side, (keep, arrived) in enumerate(((fa_keep, fa_got), (fb_keep, fb_got))):
        far_copies[side].wait()
        total = keep[:rows].astype(F32) + arrived[:rows].astype(F32) + lasts[side].astype(F32)
        far_ref[side] = total.astype(BF16)
    step_one.wait()


def mix(dq, o, lefts, dkv_one, dkv_two, far_parts):
    rows2, columns = far_parts[0].shape
    rows = rows2 // 2
    wide = dq.shape[1]
    vmem = pl.BlockSpec(memory_space=pltpu.VMEM)
    half = jax.ShapeDtypeStruct((rows2, wide), BF16)
    block = jax.ShapeDtypeStruct(dkv_one.shape, BF16)
    return pl.pallas_call(
        mix_kernel,
        in_specs=[vmem] * 12,
        out_specs=[vmem] * 6,
        out_shape=[half] * 4 + [block] + [jax.ShapeDtypeStruct((2, rows, columns), BF16)],
        scratch_shapes=[
            pltpu.VMEM(block.shape, BF16),
            pltpu.VMEM(block.shape, BF16),
            pltpu.VMEM((2, 2 * rows2, wide), BF16),
            pltpu.VMEM((2, 2 * rows2, wide), BF16),
            pltpu.VMEM((2, rows, columns), BF16),
            pltpu.VMEM((2, rows, columns), BF16),
            pltpu.SemaphoreType.DMA((6,)),
            pltpu.SemaphoreType.DMA((6,)),
        ],
        compiler_params=pltpu.CompilerParams(
            vmem_limit_bytes=56 * 2**20, collective_id=2, has_side_effects=True
        ),
        name="mix",
    )(dq, o, *lefts, dkv_one, dkv_two, *far_parts)


def finish_kernel(
    dx_ref,
    q_keep,
    q_send,
    o_keep,
    o_send,
    s_send,
    s_keep,
    back_ref,
    qo_ref,
    s_ref,
    q_got,
    o_got,
    q_half,
    o_half,
    q_last,
    o_last,
    s_got,
    s_half,
    s_got2,
    s_quarter,
    s_last,
    z_mine,
    z_got,
    k_mine,
    k_half,
    k_got,
    deal_send,
    deal_recv,
    send,
    recv,
):
    d = lax.axis_index("dp")
    z = lax.axis_index("tensor")
    count = dx_ref.shape[0]
    z_count = z_mine.shape[0]
    barrier = pltpu.get_barrier_semaphore()
    for p in range(1, count):
        pl.semaphore_signal(
            barrier, inc=1, device_id={"dp": flip(d, p)}, device_id_type=pl.DeviceIdType.MESH
        )
    for m in range(1, z_count):
        pl.semaphore_signal(
            barrier, inc=1, device_id={"tensor": flip(z, m)}, device_id_type=pl.DeviceIdType.MESH
        )
    pl.semaphore_wait(barrier, count - 1 + z_count - 1)

    def start(src, dst, at, to):
        copy = pltpu.make_async_remote_copy(
            src_ref=src,
            dst_ref=dst,
            send_sem=send.at[at],
            recv_sem=recv.at[at],
            device_id=to,
            device_id_type=pl.DeviceIdType.MESH,
        )
        copy.start()
        return copy

    one, two, four = [{"dp": flip(d, bit)} for bit in (1, 2, 4)]
    q_one = start(q_send, q_got, 1, two)
    o_one = start(o_send, o_got, 2, four)
    s_one = start(s_send, s_got, 0, one)
    back_ref[d] = dx_ref[d]
    rows = q_last.shape[0]
    s_one.wait()
    total = s_keep[...].astype(F32) + s_got[...].astype(F32)
    s_keep2 = total[: 2 * rows]
    s_half[...] = total[2 * rows :].astype(BF16)
    s_two = start(s_half, s_got2, 3, four)
    q_one.wait()
    q_half[...] = (q_keep[rows:].astype(F32) + q_got[rows:].astype(F32)).astype(BF16)
    q_two = start(q_half, q_last, 4, four)
    o_one.wait()
    o_half[...] = (o_keep[rows:].astype(F32) + o_got[rows:].astype(F32)).astype(BF16)
    o_two = start(o_half, o_last, 5, two)
    s_two.wait()
    total = s_keep2 + s_got2[...].astype(F32)
    s_quarter[...] = total[rows:].astype(BF16)
    s_three = start(s_quarter, s_last, 6, two)
    deals = []
    for p in range(1, count):
        copy = pltpu.make_async_remote_copy(
            src_ref=dx_ref.at[flip(d, p)],
            dst_ref=back_ref.at[d],
            send_sem=deal_send.at[p - 1],
            recv_sem=deal_recv.at[p - 1],
            device_id={"dp": flip(d, p)},
            device_id_type=pl.DeviceIdType.MESH,
        )
        copy.start()
        deals.append(copy)
    s_own = total[:rows]
    s_three.wait()
    s_own = s_own + s_last[...].astype(F32)
    k_mine[...] = s_own.astype(BF16)
    k_near = start(k_mine, k_got.at[0], 7, {"tensor": flip(z, 1)})
    finals = []
    part = qo_ref.shape[1] // 2
    for two_copy, keep, got, last, side in (
        (q_two, q_keep, q_got, q_last, 0),
        (o_two, o_keep, o_got, o_last, 1),
    ):
        two_copy.wait()
        total = (
            keep[:rows].astype(F32) + got[:rows].astype(F32) + last[...].astype(F32)
        )
        for i in range(z_count):
            block = total[:, i * part : (i + 1) * part]
            z_mine[i, :, side * part : (side + 1) * part] = block.astype(BF16)
    for m in range(1, z_count):
        finals.append(start(z_mine.at[flip(z, m)], z_got.at[m - 1], 8 + m, {"tensor": flip(z, m)}))
    k_near.wait()
    s_own = s_own + k_got[0].astype(F32)
    k_half[...] = s_own.astype(BF16)
    k_far = start(k_half, k_got.at[1], 8, {"tensor": flip(z, 2)})
    for copy in finals:
        copy.wait()
    total = z_mine[z].astype(F32)
    for m in range(z_count - 1):
        total = total + z_got[m].astype(F32)
    qo_ref[...] = total
    k_far.wait()
    s_ref[...] = s_own + k_got[1].astype(F32)
    for copy in deals:
        copy.wait()


def finish(dx, q_keep, q_send, o_keep, o_send, s_send, s_keep, z_count):
    count = dx.shape[0]
    rows = q_keep.shape[0] // 2
    columns = q_keep.shape[1]
    small = s_keep.shape[1]
    part = columns // z_count
    vmem = pl.BlockSpec(memory_space=pltpu.VMEM)
    dma = pltpu.SemaphoreType.DMA
    return pl.pallas_call(
        finish_kernel,
        in_specs=[vmem] * 7,
        out_specs=[vmem] * 3,
        out_shape=[
            jax.ShapeDtypeStruct(dx.shape, BF16),
            jax.ShapeDtypeStruct((rows, 2 * part), F32),
            jax.ShapeDtypeStruct((rows, small), F32),
        ],
        scratch_shapes=[
            pltpu.VMEM((2 * rows, columns), BF16),
            pltpu.VMEM((2 * rows, columns), BF16),
            pltpu.VMEM((rows, columns), BF16),
            pltpu.VMEM((rows, columns), BF16),
            pltpu.VMEM((rows, columns), BF16),
            pltpu.VMEM((rows, columns), BF16),
            pltpu.VMEM((4 * rows, small), BF16),
            pltpu.VMEM((2 * rows, small), BF16),
            pltpu.VMEM((2 * rows, small), BF16),
            pltpu.VMEM((rows, small), BF16),
            pltpu.VMEM((rows, small), BF16),
            pltpu.VMEM((z_count, rows, 2 * part), BF16),
            pltpu.VMEM((z_count - 1, rows, 2 * part), BF16),
            pltpu.VMEM((rows, small), BF16),
            pltpu.VMEM((rows, small), BF16),
            pltpu.VMEM((2, rows, small), BF16),
            dma((count - 1,)),
            dma((count - 1,)),
            dma((7 + 2 * z_count,)),
            dma((7 + 2 * z_count,)),
        ],
        compiler_params=pltpu.CompilerParams(
            vmem_limit_bytes=56 * 2**20, collective_id=0, has_side_effects=True
        ),
        name="finish",
    )(dx, q_keep, q_send, o_keep, o_send, s_send, s_keep)


def turn_kernel(orders, d_ref, *refs):
    tiles = len(refs) - 1 - len(orders)
    scratch_ref = refs[-1]
    step = pl.program_id(0)
    for t in range(tiles):

        @pl.when(step == t)
        def _(t=t):
            scratch_ref[...] = refs[t][...].T

    for order, out_ref in zip(orders, refs[tiles:-1]):
        size = out_ref.shape[0] // len(order)
        for i, p in enumerate(order):
            block = jnp.bitwise_xor(d_ref[0], p)
            at = pl.multiple_of(block * size, size)
            out_ref[i * size : (i + 1) * size, :] = scratch_ref[pl.ds(at, size), :]


def turn(d, tiles, orders, blocks):
    rows, width = tiles[0].shape
    size = width // blocks
    return pl.pallas_call(
        functools.partial(turn_kernel, orders),
        grid_spec=pltpu.PrefetchScalarGridSpec(
            num_scalar_prefetch=1,
            grid=(len(tiles),),
            in_specs=[pl.BlockSpec((rows, width), lambda t, s: (0, 0))] * len(tiles),
            out_specs=[
                pl.BlockSpec((len(order) * size, rows), lambda t, s: (0, t)) for order in orders
            ],
            scratch_shapes=[pltpu.VMEM((width, rows), BF16)],
        ),
        out_shape=[
            jax.ShapeDtypeStruct((len(order) * size, rows * len(tiles)), BF16) for order in orders
        ],
        compiler_params=params(),
        name="turn",
        cost_estimate=pl.CostEstimate(
            flops=0, bytes_accessed=6 * rows * width * len(tiles), transcendentals=0
        ),
    )(d, *tiles)


def tie(*values):
    return lax.optimization_barrier(values)


def row_major(x):
    return with_layout_constraint(x, Layout(major_to_minor=tuple(range(x.ndim))))


def per_device(
    tokens,
    perm,
    routes,
    gates,
    lengths,
    cotangent,
    gain_attn,
    w_query,
    w_keyval,
    w_out,
    gain_moe,
    w_gate,
    w_up,
    w_down,
):
    dp_count = lax.axis_size("dp")
    tensor_count = lax.axis_size("tensor")
    d = lax.axis_index("dp")
    z = lax.axis_index("tensor")
    rows, width = tokens.shape
    group_rows = perm.shape[0]
    share = rows // dp_count
    top = routes.shape[1]
    experts_n, _, part_hidden = w_gate.shape
    hidden = experts_n * part_hidden
    capacity = 9 * group_rows * top // (8 * experts_n)
    kv_heads = w_keyval.shape[1] // (2 * HD)
    query_cols = w_query.shape[1]
    team = 8
    teams = [[t * team + i for i in range(team)] for t in range(dp_count // team)]
    teams = None if len(teams) == 1 else teams
    piece_rows = width // team
    member = d % team

    def z_move(x, pairs):
        return lax.ppermute(x, "tensor", pairs)

    def dp_move(x, bit):
        return lax.ppermute(x, "dp", [(i, i ^ bit) for i in range(dp_count)])

    near, far, across = [[(i, i ^ m) for i in range(tensor_count)] for m in (1, 2, 3)]
    up_one, up_two = [[(i, i + m) for i in range(tensor_count - m)] for m in (1, 2)]

    def deal(x):
        return lax.all_to_all(
            x.reshape(dp_count, share, x.shape[1]), "dp", split_axis=0, concat_axis=0, tiled=True
        ).reshape(rows, x.shape[1])

    def team_gather(x):
        return lax.all_gather(x, "dp", axis=0, tiled=True, axis_index_groups=teams)

    def flat(w):
        return w.transpose(0, 2, 1).reshape(hidden, w.shape[1])

    own_perm = lax.dynamic_slice_in_dim(perm, z * rows, rows, 0)
    own_routes = lax.dynamic_slice_in_dim(routes, z * rows, rows, 0)
    dest = own_perm // group_rows
    place = own_perm % rows
    row_index = jnp.arange(rows, dtype=jnp.int32)
    lower = (row_index[:, None] > row_index[None, :]).astype(BF16)
    dest_hot = (dest[:, None] == jnp.arange(dp_count, dtype=jnp.int32)[None, :]).astype(BF16)
    earlier = jnp.sum(mm(lower, dest_hot) * dest_hot.astype(F32), axis=1).astype(jnp.int32)
    slot = dest * share + earlier
    pack = (row_index[:, None] == slot[None, :]).astype(BF16)
    meta = jnp.concatenate(
        [
            (place // 16)[:, None].astype(BF16),
            (place % 16)[:, None].astype(BF16),
            own_routes.astype(BF16),
            gates,
            jnp.zeros((rows, META - 2 - 2 * top), BF16),
        ],
        axis=1,
    )
    packed = mm(pack, jnp.concatenate([tokens, meta], axis=1)).astype(BF16)
    wg_own, wu_own = flat(w_gate), flat(w_up)
    wd_own = w_down.reshape(hidden, width)
    out_rows = query_cols // team
    hidden_piece = hidden // team

    def piece(w, count):
        return lax.dynamic_slice_in_dim(w, member * count, count, 0)

    wg_piece, wu_piece, wd_piece = [piece(w, hidden_piece) for w in (wg_own, wu_own, wd_own)]
    packed_dy = mm(pack, cotangent).astype(BF16)
    packed, packed_dy = tie(packed, packed_dy)
    arrived, wq_z, wo_z = open_moves(
        packed.reshape(dp_count, share, width + META),
        piece(w_query, piece_rows),
        piece(w_out, out_rows),
        tensor_count,
    )
    arrived = arrived.reshape(rows, width + META)
    wq_all = team_gather(wq_z).reshape(team, tensor_count, piece_rows, query_cols)
    wo_all = team_gather(wo_z).reshape(team, tensor_count, out_rows, width)
    wo = wo_all.transpose(1, 0, 2, 3).reshape(tensor_count * query_cols, width)

    meta_in = arrived[:, width:].astype(F32)
    place_in = (meta_in[:, 0] * 16.0 + meta_in[:, 1]).astype(jnp.int32)
    unpack = (row_index[:, None] == place_in[None, :]).astype(BF16)
    dealt = mm(unpack, arrived)
    x_rows = dealt[:, :width]
    meta_rows = dealt[:, width:]

    expert_ids = jnp.arange(experts_n, dtype=jnp.int32).astype(F32)
    route_rows = meta_rows[:, 2 : 2 + top]
    gate_rows = meta_rows[:, 2 + top : 2 + 2 * top]
    hot = route_rows[:, :, None] == expert_ids[None, None, :]
    routed = jnp.sum(hot.astype(F32), axis=1)
    counts = jnp.pad(jnp.sum(routed, axis=0)[None, :], ((0, 7), (0, HD - experts_n)))

    seq_lengths = lengths[0]
    seq_index = jnp.arange(seq_lengths.shape[0], dtype=jnp.int32)
    seq_ends = jnp.sum(
        jnp.where(seq_index[None, :] <= seq_index[:, None], seq_lengths[None, :], 0), axis=1
    ).astype(jnp.int32)
    global_row = z * rows + row_index
    start = jnp.max(
        jnp.where(global_row[:, None] >= seq_ends[None, :], seq_ends[None, :], 0), axis=1
    ).astype(jnp.int32)
    offset = (global_row - start).astype(F32)
    frequency = ROPE_BASE ** (-2.0 * jnp.arange(HD // 2, dtype=F32) / HD)
    angles = offset[:, None] * frequency[None, :]
    cosine, sine = jnp.cos(angles), jnp.sin(angles)
    cos_full = jnp.concatenate([cosine, cosine], axis=1)
    sin_full = jnp.concatenate([-sine, sine], axis=1)
    start = start[:, None]
    z_arg = z.astype(jnp.int32)[None]

    inv_one = lax.rsqrt(jnp.mean(x_rows * x_rows, axis=1, keepdims=True) + EPS)
    n1 = (x_rows * inv_one * gain_attn).astype(BF16)
    weight = jnp.sum(jnp.where(hot, gate_rows[:, :, None], 0.0), axis=1)
    marks = jnp.pad(
        jnp.concatenate([routed, weight], axis=1).astype(BF16), ((0, 0), (0, HD - 2 * experts_n))
    )
    kv, kv_one, kv_two, counts, marks_near, arrived_dy = keyval(
        n1,
        w_keyval,
        cos_full,
        sin_full,
        counts,
        marks,
        packed_dy.reshape(dp_count, share, width),
        tensor_count,
    )
    arrived_dy = arrived_dy.reshape(rows, width)
    kv, n1, wg_piece, wu_piece = tie(kv, n1, wg_piece, wu_piece)
    wg_moved, wu_moved = z_move(wg_piece, far), z_move(wu_piece, far)

    def kept_gates(routed, weight, at):
        block = (z - 1 - jnp.arange(tensor_count, dtype=jnp.int32)) % tensor_count
        base = jnp.sum(
            jnp.where((block < at)[:, None], counts[:, 0, :experts_n], 0.0), axis=0
        )
        position = mm(lower, routed.astype(BF16)) + base[None, :]
        weight = jnp.where(position < capacity, weight, 0.0).astype(BF16)
        return row_major(jnp.repeat(weight, part_hidden, axis=1))

    gate_own = kept_gates(routed, weight, z)
    marks_near = marks_near.astype(F32)
    gate_near = kept_gates(
        marks_near[:, :experts_n], marks_near[:, experts_n : 2 * experts_n], z + 1 - 2 * (z % 2)
    )
    q = project_query(z_arg, n1, wq_all, cos_full, sin_full)
    dy_rows = mm(unpack, arrived_dy).astype(BF16)
    q, dy_rows, gate_own, gate_near = tie(q, dy_rows, gate_own, gate_near)
    dy_near = z_move(dy_rows, near)
    kvs = (kv_two, kv_one, kv)
    o, lse = attend(z_arg, start, q, kvs, kv_heads)
    o, wd_piece, wg_moved, wu_moved = tie(o, wd_piece, wg_moved, wu_moved)
    wg_far = team_gather(wg_moved)
    wu_far = team_gather(wu_moved)
    h = x_rows + mm(o, wo)
    inv_two = lax.rsqrt(jnp.mean(h * h, axis=1, keepdims=True) + EPS)
    n2 = (h * inv_two * gain_moe).astype(BF16)

    halving = dp_count == 8
    d_arg = d.astype(jnp.int32)[None]
    out_w = width // dp_count
    orders_a = ((1, 5, 3, 7), (0, 4, 2, 6))
    orders_b = ((1, 3, 5, 7), (0, 2, 4, 6))

    def turned(tiles, *orders):
        if halving:
            return turn(d_arg, tiles, orders, dp_count)
        return [jnp.concatenate(tiles, axis=0).T] * len(orders)

    def dp_sum(x):
        return lax.psum_scatter(x, "dp", scatter_dimension=0, tiled=True)

    def first_moves(parts):
        return parts[0], dp_move(parts[1], xy[0]), parts[2], dp_move(parts[3], yx[0])

    def second_moves(moved):
        halves = []
        for keep, got, bit in ((*moved[:2], xy[1]), (*moved[2:], yx[1])):
            x = keep.astype(F32) + got.astype(F32)
            half = x.shape[0] // 2
            halves += [x[:half], dp_move(x[half:].astype(BF16), bit)]
        return halves

    def unit_end(moved):
        return moved[0] + moved[1].astype(F32), moved[2] + moved[3].astype(F32)

    def expert_lefts(n_a, d_a, keep):
        return n_a[keep], d_a[keep], n_a[2 + keep], d_a[2 + keep]

    xy, yx = (2, 4), (4, 2)
    n2_near = z_move(n2, near)
    y, dn2, *own_grads = experts(0, n2, dy_rows, gate_own, wg_own, wu_own, wd_own)
    n2_near, y, dy_near, wd_piece = tie(n2_near, y, dy_near, wd_piece)
    wd_moved = z_move(wd_piece, far)
    yn, dnn, *own_grads = experts(
        1, n2_near, dy_near, gate_near, wg_own, wu_own, wd_own, filled=own_grads
    )
    yn, wd_moved, *own_grads = tie(yn, wd_moved, *own_grads)
    wd_far = team_gather(wd_moved)
    dy_a = turned((dy_rows, dy_near), *orders_a, *orders_b)
    n2_a = turned((n2, n2_near), *orders_a, *orders_b)
    if halving:
        own = gradients(
            EXPERT_JOBS,
            expert_lefts(n2_a, dy_a, 0),
            expert_lefts(n2_a, dy_a, 1),
            own_grads[::-1],
            3,
        )
        wg_far, *own = tie(wg_far, *own)
        own = first_moves(own)
    yn, dnn, *far_grads = experts(
        1, n2_near, dy_near, gate_near, wg_far, wu_far, wd_far, (yn, dnn)
    )
    dnn_moved = z_move(dnn.astype(BF16), near)
    y, dn2, *far_grads = experts(
        0, n2, dy_rows, gate_own, wg_far, wu_far, wd_far, (y, dn2), far_grads
    )
    if halving:
        far_grads = far_grads[::-1]
        far_sent = gradient_parts(EXPERT_JOBS, expert_lefts(n2_a, dy_a, 0), far_grads)
        dnn_moved, far_sent, *own = tie(dnn_moved, far_sent, *own)
        got = dp_move(far_sent, 1)
        own = second_moves(own)
    yn, dnn_moved = tie(yn, dnn_moved)
    yn_moved = z_move(yn.astype(BF16), near)
    dn2 = dn2 + dnn_moved.astype(F32)

    gain_two_part = jnp.sum(dn2 * h * inv_two, axis=0)
    u2 = dn2 * gain_moe
    dh = dy_rows.astype(F32) + inv_two * (
        u2 - h * inv_two * inv_two * jnp.mean(u2 * h, axis=1, keepdims=True)
    )
    dhb = dh.astype(BF16)
    do = mm_nt(dhb, wo).astype(BF16)
    if halving:
        far_w = gradient_parts(EXPERT_JOBS, expert_lefts(n2_a, dy_a, 1), far_grads, got)
        do, *far_w = tie(do, *far_w)
        far_w = first_moves(far_w)
    result = h + y + yn_moved.astype(F32)
    result_out = mm_tn(unpack, result.astype(BF16)).astype(BF16)
    if halving:
        do, result_out, *own = tie(do, result_out, *own)
    else:
        do, result_out = tie(do, result_out)

    dq, dkv_two, dkv_one, dkv = attend_back(
        z_arg, start, q, o, do, lse, cos_full, sin_full, kvs, kv_heads
    )
    n1_t = turned((n1,), *orders_a, *orders_b)
    dhb_t = turned((dhb,), *orders_b)
    if halving:
        dq, *far_w = tie(dq, *far_w)
        *parts, dkv_sum, far_sum = mix(
            dq, o, (n1_t[0], n1_t[1], *dhb_t), dkv_one, dkv_two, far_w
        )
        far_sum = z_move(far_sum, far)
    else:
        dkv_one = z_move(dkv_one, [(b, a) for a, b in up_one])
        dkv_two = z_move(dkv_two, [(b, a) for a, b in up_two])
        dkv_sum = dkv_one.astype(F32) + dkv_two.astype(F32)
        sum_q, sum_o = [
            dp_sum(mm_tn(a, b).astype(BF16)).astype(F32) for a, b in ((n1, dq), (dhb, o))
        ]
    dkv = dkv + dkv_sum.astype(F32)

    def unrotate(u):
        swapped = jnp.concatenate([u[:, HD // 2 :], u[:, : HD // 2]], axis=1)
        return u * cos_full - swapped * sin_full

    dkv = jnp.concatenate(
        [unrotate(dkv[:, i * HD : (i + 1) * HD]) for i in range(kv_heads)]
        + [dkv[:, kv_heads * HD :]],
        axis=1,
    ).astype(BF16)
    dn1 = project_back(z_arg, dq, wq_all, dkv, w_keyval)
    gain_one_part = jnp.sum(dn1 * x_rows * inv_one, axis=0)
    u1 = dn1 * gain_attn
    dx = dh + inv_one * (
        u1 - x_rows * inv_one * inv_one * jnp.mean(u1 * x_rows, axis=1, keepdims=True)
    )

    outputs = mm_tn(pack, deal(result_out)).astype(BF16)

    if halving:
        first, second = [a + b.astype(F32) for a, b in zip(unit_end(own), far_sum)]
        sum_gu = jnp.concatenate([first[:, :hidden], second[:, :hidden]], axis=1)
        sum_down = jnp.concatenate([first[:, hidden:], second[:, hidden:]], axis=1)
    else:
        lefts = (n2_a[0], dy_a[0])
        far_sums = [dp_sum(mm(a, b).astype(BF16)) for a, b in zip(lefts, far_grads[::-1])]
        own_sums = [dp_sum(mm(a, b).astype(BF16)) for a, b in zip(lefts, own_grads[::-1])]
        sum_gu, sum_down = [
            a.astype(F32) + z_move(b, far).astype(F32) for a, b in zip(own_sums, far_sums)
        ]
    sum_gu = sum_gu.reshape(out_w, hidden // 512, 2, 512)
    sum_gate, sum_up = [
        sum_gu[:, :, i].reshape(out_w, experts_n, part_hidden).transpose(1, 0, 2) for i in (0, 1)
    ]
    sum_down = sum_down.reshape(out_w, experts_n, part_hidden).transpose(1, 2, 0)

    gains = jnp.stack([gain_one_part, gain_two_part])

    def gain_columns(order):
        blocks = gains.reshape(2, dp_count, out_w)
        if halving:
            blocks = jnp.stack(
                [lax.dynamic_index_in_dim(blocks, d ^ p, 1, keepdims=False) for p in order], 1
            )
        return jnp.pad(blocks.reshape(2, -1).T, ((0, 0), (dkv.shape[1], HD - 2)))

    columns = [gain_columns(order) for order in orders_b]
    dkv_wide = jnp.pad(dkv, ((0, 0), (0, HD)))
    if halving:
        kv_send, kv_keep = [
            (mm(left, dkv_wide) + column).astype(BF16) for left, column in zip(n1_t[2:], columns)
        ]
        dx_out = mm_tn(unpack, dx.astype(BF16)).astype(BF16).reshape(dp_count, share, width)
        back, total, small = finish(dx_out, *parts, kv_send, kv_keep, tensor_count)
        grad_tokens = mm_tn(pack, back.reshape(rows, width)).astype(BF16)
    else:
        grad_tokens = mm_tn(pack, deal(mm_tn(unpack, dx.astype(BF16)).astype(BF16))).astype(BF16)
        small = dp_sum((mm(n1_t[3], dkv_wide) + columns[0]).astype(BF16))
        small = small.astype(F32) + sum(
            z_move(small, move).astype(F32) for move in (near, far, across)
        )

        def z_block(x, m):
            return lax.dynamic_slice_in_dim(x, (z ^ m) * query_cols, query_cols, 1)

        both = [jnp.concatenate([z_block(sum_q, m), z_block(sum_o, m)], axis=1) for m in range(4)]
        total = both[0] + sum(
            z_move(part.astype(BF16), move).astype(F32)
            for part, move in zip(both[1:], (near, far, across))
        )
    sum_query, sum_out = total[:, :query_cols], total[:, query_cols:].T
    kv_cols = w_keyval.shape[1]
    return (
        outputs,
        grad_tokens,
        small[:, kv_cols],
        sum_query,
        small[:, :kv_cols],
        sum_out,
        small[:, kv_cols + 1],
        sum_gate,
        sum_up,
        sum_down,
    )


def solution(mesh):
    in_specs = (
        P(("dp", "tensor"), None),
        P("dp"),
        P("dp", None),
        P(("dp", "tensor"), None),
        P("dp", None),
        P(("dp", "tensor"), None),
        P(),
        P(None, "tensor"),
        P(),
        P("tensor", None),
        P(),
        P(None, None, "tensor"),
        P(None, None, "tensor"),
        P(None, "tensor", None),
    )
    out_specs = (
        P(("dp", "tensor"), None),
        P(("dp", "tensor"), None),
        P("dp"),
        P("dp", "tensor"),
        P("dp", None),
        P("tensor", "dp"),
        P("dp"),
        P(None, "dp", "tensor"),
        P(None, "dp", "tensor"),
        P(None, "tensor", "dp"),
    )
    return jax.shard_map(
        per_device, mesh=mesh, in_specs=in_specs, out_specs=out_specs, check_vma=False
    )
```

```python
import functools

import jax
import jax.numpy as jnp
from jax import lax
from jax.experimental import pallas as pl
from jax.experimental.layout import Layout, with_layout_constraint
from jax.experimental.pallas import tpu as pltpu
from jax.sharding import PartitionSpec as P

HD = 128
EPS = 1e-06
ROPE_BASE = 1000000.0
MASKED = -1e30
LOG2E = 1.4426950408889634
F32 = jnp.float32
BF16 = jnp.bfloat16
META = 128


def mm(a, b):
    return lax.dot_general(a, b, (((1,), (0,)), ((), ())), preferred_element_type=F32)


def mm_nt(a, b):
    return lax.dot_general(a, b, (((1,), (1,)), ((), ())), preferred_element_type=F32)


def mm_tn(a, b):
    return lax.dot_general(a, b, (((0,), (0,)), ((), ())), preferred_element_type=F32)


def params(mb=56):
    return pltpu.CompilerParams(vmem_limit_bytes=mb * 2**20)


def swap_halves(u):
    return pltpu.roll(u, HD // 2, 1)


def open_kernel(
    deal_ref,
    q_ref,
    o_ref,
    dealt_ref,
    q_all,
    o_all,
    send,
    recv,
    deal_send,
    deal_recv,
):
    z = lax.axis_index("tensor")
    d = lax.axis_index("dp")
    d_count = deal_ref.shape[0]
    z_count = q_all.shape[0]
    others = [{"tensor": flip(z, m)} for m in range(1, z_count)]
    peers = [{"dp": (d + p) % d_count} for p in range(1, d_count)]
    barrier = pltpu.get_barrier_semaphore()
    for other in others + peers:
        pl.semaphore_signal(barrier, inc=1, device_id=other, device_id_type=pl.DeviceIdType.MESH)
    pl.semaphore_wait(barrier, len(others) + len(peers))
    moves = [(q_ref, q_all.at[m], others[m - 1]) for m in range(1, z_count)]
    moves += [(o_ref, o_all.at[z], other) for other in others]
    copies = []
    for p, peer in enumerate(peers):
        copy = pltpu.make_async_remote_copy(
            src_ref=deal_ref.at[(d + p + 1) % d_count],
            dst_ref=dealt_ref.at[d],
            send_sem=deal_send.at[p],
            recv_sem=deal_recv.at[p],
            device_id=peer,
            device_id_type=pl.DeviceIdType.MESH,
        )
        copy.start()
        copies.append(copy)
    for at, (src, dst, to) in enumerate(moves):
        copy = pltpu.make_async_remote_copy(
            src_ref=src,
            dst_ref=dst,
            send_sem=send.at[at],
            recv_sem=recv.at[at],
            device_id=to,
            device_id_type=pl.DeviceIdType.MESH,
        )
        copy.start()
        copies.append(copy)
    dealt_ref[d] = deal_ref[d]
    q_all[0] = q_ref[...]
    o_all[z] = o_ref[...]
    for copy in copies:
        copy.wait()


def open_moves(deals, q, o, z_count):
    vmem = pl.BlockSpec(memory_space=pltpu.VMEM)
    shapes = [deals.shape, (z_count, *q.shape), (z_count, *o.shape)]
    moves = 2 * (z_count - 1)
    return pl.pallas_call(
        open_kernel,
        in_specs=[vmem] * 3,
        out_specs=[vmem] * 3,
        out_shape=[jax.ShapeDtypeStruct(shape, BF16) for shape in shapes],
        scratch_shapes=[
            pltpu.SemaphoreType.DMA((moves,)),
            pltpu.SemaphoreType.DMA((moves,)),
            pltpu.SemaphoreType.DMA((deals.shape[0] - 1,)),
            pltpu.SemaphoreType.DMA((deals.shape[0] - 1,)),
        ],
        compiler_params=pltpu.CompilerParams(
            vmem_limit_bytes=40 * 2**20, collective_id=4, has_side_effects=True
        ),
        name="open_moves",
    )(deals, q, o)


def keyval_kernel(
    x_ref,
    w_ref,
    cos_ref,
    sin_ref,
    count_ref,
    mark_ref,
    deal_ref,
    kv_ref,
    one_ref,
    two_ref,
    counts_ref,
    near_ref,
    dealt_ref,
    send,
    recv,
    deal_send,
    deal_recv,
):
    z = lax.axis_index("tensor")
    d = lax.axis_index("dp")
    d_count = deal_ref.shape[0]
    z_count = counts_ref.shape[0]
    others = [{"tensor": (z + m) % z_count} for m in range(1, z_count)]
    barrier = pltpu.get_barrier_semaphore()
    peers = [{"dp": (d + p) % d_count} for p in range(1, d_count)]
    for other in others + peers:
        pl.semaphore_signal(barrier, inc=1, device_id=other, device_id_type=pl.DeviceIdType.MESH)
    raw = mm(x_ref[...], w_ref[...])
    turned = raw.shape[1] // 2
    for i in range(turned // HD):
        u = raw[:, i * HD : (i + 1) * HD]
        u = u * cos_ref[...] + swap_halves(u) * sin_ref[...]
        kv_ref[:, i * HD : (i + 1) * HD] = u.astype(BF16)
    kv_ref[:, turned:] = raw[:, turned:].astype(BF16)
    pl.semaphore_wait(barrier, z_count - 1 + d_count - 1)
    moves = [(count_ref, counts_ref.at[m], others[m]) for m in range(z_count - 1)]
    moves += [(mark_ref, near_ref, {"tensor": flip(z, 1)})]
    moves += [(kv_ref, one_ref, others[0]), (one_ref, two_ref, others[0])]
    copies = []
    for at, (src, dst, to) in enumerate(moves):
        copy = pltpu.make_async_remote_copy(
            src_ref=src,
            dst_ref=dst,
            send_sem=send.at[at],
            recv_sem=recv.at[at],
            device_id=to,
            device_id_type=pl.DeviceIdType.MESH,
        )
        copies.append(copy)
    for copy in copies[:-1]:
        copy.start()
    for p, peer in enumerate(peers):
        copy = pltpu.make_async_remote_copy(
            src_ref=deal_ref.at[(d + p + 1) % d_count],
            dst_ref=dealt_ref.at[d],
            send_sem=deal_send.at[p],
            recv_sem=deal_recv.at[p],
            device_id=peer,
            device_id_type=pl.DeviceIdType.MESH,
        )
        copy.start()
        copies.append(copy)
    counts_ref[z_count - 1] = count_ref[...]
    dealt_ref[d] = deal_ref[d]
    step_one, step_two = copies[z_count], copies[z_count + 1]
    step_one.wait()
    step_two.start()
    for copy in copies[:z_count] + copies[z_count + 1 :]:
        copy.wait()


def keyval(x, w, cos_full, sin_full, counts, marks, deals, z_count):
    rows = x.shape[0]
    columns = w.shape[1]
    vmem = pl.BlockSpec(memory_space=pltpu.VMEM)
    block = jax.ShapeDtypeStruct((rows, columns), BF16)
    return pl.pallas_call(
        keyval_kernel,
        in_specs=[vmem] * 7,
        out_specs=[vmem] * 6,
        out_shape=[block] * 3
        + [
            jax.ShapeDtypeStruct((z_count, *counts.shape), counts.dtype),
            jax.ShapeDtypeStruct(marks.shape, marks.dtype),
            jax.ShapeDtypeStruct(deals.shape, deals.dtype),
        ],
        scratch_shapes=[
            pltpu.SemaphoreType.DMA((z_count + 2,)),
            pltpu.SemaphoreType.DMA((z_count + 2,)),
            pltpu.SemaphoreType.DMA((deals.shape[0] - 1,)),
            pltpu.SemaphoreType.DMA((deals.shape[0] - 1,)),
        ],
        compiler_params=pltpu.CompilerParams(
            vmem_limit_bytes=40 * 2**20, collective_id=1, has_side_effects=True
        ),
        name="keyval",
    )(x, w, cos_full, sin_full, counts, marks, deals)


def project_query_kernel(z_ref, x_ref, w_ref, cos_ref, sin_ref, out_ref):
    raw = mm(x_ref[...], w_ref[...].reshape(x_ref.shape[1], out_ref.shape[1]))
    for i in range(raw.shape[1] // HD):
        u = raw[:, i * HD : (i + 1) * HD]
        turned = u * cos_ref[...] + swap_halves(u) * sin_ref[...]
        out_ref[:, i * HD : (i + 1) * HD] = (turned * SCALE).astype(BF16)


def project_query(z, x, w, cos_full, sin_full):
    rows, width = x.shape
    pieces, blocks, piece, columns = w.shape
    return pl.pallas_call(
        project_query_kernel,
        grid_spec=pltpu.PrefetchScalarGridSpec(
            num_scalar_prefetch=1,
            grid=(blocks,),
            in_specs=[
                pl.BlockSpec((rows, width), lambda i, s: (0, 0)),
                pl.BlockSpec(
                    (pieces, 1, piece, columns), lambda i, s: (0, jnp.bitwise_xor(i, s[0]), 0, 0)
                ),
                pl.BlockSpec((rows, HD), lambda i, s: (0, 0)),
                pl.BlockSpec((rows, HD), lambda i, s: (0, 0)),
            ],
            out_specs=pl.BlockSpec((rows, columns), lambda i, s: (0, i)),
        ),
        out_shape=jax.ShapeDtypeStruct((rows, blocks * columns), BF16),
        compiler_params=params(),
        name="project_query",
        cost_estimate=pl.CostEstimate(
            flops=2 * rows * width * blocks * columns,
            bytes_accessed=2 * (2 * rows * width + width * blocks * columns),
            transcendentals=0,
        ),
    )(z, x, w, cos_full, sin_full)


def project_back_kernel(z_ref, dq_ref, w_ref, dkv_ref, wkv_ref, out_ref):
    step = pl.program_id(0)
    width = out_ref.shape[1]
    part = mm_nt(dq_ref[...], w_ref[...].reshape(width, dq_ref.shape[1]))

    @pl.when(step == 0)
    def _():
        out_ref[...] = part + mm_nt(dkv_ref[...], wkv_ref[...])

    @pl.when(step > 0)
    def _():
        out_ref[...] += part


def project_back(z, dq, w, dkv, wkv):
    rows = dq.shape[0]
    pieces, blocks, piece, columns = w.shape
    width = pieces * piece
    return pl.pallas_call(
        project_back_kernel,
        grid_spec=pltpu.PrefetchScalarGridSpec(
            num_scalar_prefetch=1,
            grid=(blocks,),
            in_specs=[
                pl.BlockSpec((rows, columns), lambda i, s: (0, i)),
                pl.BlockSpec(
                    (pieces, 1, piece, columns), lambda i, s: (0, jnp.bitwise_xor(i, s[0]), 0, 0)
                ),
                pl.BlockSpec(dkv.shape, lambda i, s: (0, 0)),
                pl.BlockSpec(wkv.shape, lambda i, s: (0, 0)),
            ],
            out_specs=pl.BlockSpec((rows, width), lambda i, s: (0, 0)),
        ),
        out_shape=jax.ShapeDtypeStruct((rows, width), F32),
        compiler_params=params(),
        name="project_back",
        cost_estimate=pl.CostEstimate(
            flops=2 * rows * width * (blocks * columns + dkv.shape[1]),
            bytes_accessed=2 * width * (3 * rows + blocks * columns),
            transcendentals=0,
        ),
    )(z, dq, w, dkv, wkv)


ATTEND_TILE = 256
SCALE = HD**-0.5 * LOG2E


def make_bias(z, start_ref, bias_ref):
    tiles, tile, width = bias_ref.shape
    rows = tiles * tile
    for i in range(tiles):
        key = (z - 2) * rows + i * tile + lax.broadcasted_iota(jnp.int32, (tile, width), 1)
        query = z * rows + i * tile + lax.broadcasted_iota(jnp.int32, (tile, width), 0)
        allowed = (key >= start_ref[i * tile : (i + 1) * tile]) & (key <= query)
        bias_ref[i] = jnp.where(allowed, 0.0, MASKED)


def attend_kernel(
    kv_heads, z_ref, start_ref, q_ref, kv0_ref, kv1_ref, kv2_ref, o_ref, lse_ref, bias_ref, k_ref, v_ref
):
    head = pl.program_id(0)
    each = pl.num_programs(0) // kv_heads
    rows = q_ref.shape[0]
    tiles, tile, width = bias_ref.shape

    @pl.when(head == 0)
    def _():
        make_bias(z_ref[0], start_ref, bias_ref)
        v_ref[:, HD:] = jnp.ones((v_ref.shape[0], HD), BF16)

    @pl.when(head % each == 0)
    def _():
        kvh = head // each
        for j, ref in enumerate((kv0_ref, kv1_ref, kv2_ref)):
            at = slice(j * rows, (j + 1) * rows)
            k_ref[at] = ref[:, pl.ds(pl.multiple_of(kvh * HD, HD), HD)]
            v_ref[at, :HD] = ref[:, pl.ds(pl.multiple_of((kv_heads + kvh) * HD, HD), HD)]

    for i in range(tiles):
        at, window = slice(i * tile, (i + 1) * tile), slice(i * tile, i * tile + width)
        score = mm_nt(q_ref[at], k_ref[window]) + bias_ref[i]
        peak = jnp.max(score, axis=1, keepdims=True)
        mixed = mm(jnp.exp2(score - peak).astype(BF16), v_ref[window])
        total = mixed[:, HD : HD + 1]
        o_ref[at] = (mixed[:, :HD] / total).astype(BF16)
        lse_ref[0, at] = peak + jnp.log2(total)


def attend(z, start, q, kvs, kv_heads):
    rows, columns = q.shape
    heads = columns // HD
    tile = ATTEND_TILE
    kv_spec = pl.BlockSpec(kvs[0].shape, lambda h, s: (0, 0))
    return pl.pallas_call(
        functools.partial(attend_kernel, kv_heads),
        grid_spec=pltpu.PrefetchScalarGridSpec(
            num_scalar_prefetch=1,
            grid=(heads,),
            in_specs=[
                pl.BlockSpec((rows, 1), lambda h, s: (0, 0)),
                pl.BlockSpec((rows, HD), lambda h, s: (0, h)),
                *[kv_spec] * 3,
            ],
            out_specs=[
                pl.BlockSpec((rows, HD), lambda h, s: (0, h)),
                pl.BlockSpec((1, rows, 1), lambda h, s: (h, 0, 0)),
            ],
            scratch_shapes=[
                pltpu.VMEM((rows // tile, tile, 2 * rows + tile), F32),
                pltpu.VMEM((3 * rows, HD), BF16),
                pltpu.VMEM((3 * rows, 2 * HD), BF16),
            ],
        ),
        out_shape=[
            jax.ShapeDtypeStruct((rows, columns), BF16),
            jax.ShapeDtypeStruct((heads, rows, 1), F32),
        ],
        compiler_params=params(),
        name="attend",
        cost_estimate=pl.CostEstimate(
            flops=12 * rows * rows * columns,
            bytes_accessed=8 * rows * columns,
            transcendentals=rows * rows * 3 * heads,
        ),
    )(z, start, q, *kvs)


def attend_back_kernel(
    kv_heads,
    z_ref,
    start_ref,
    q_ref,
    o_ref,
    do_ref,
    lse_ref,
    cos_ref,
    sin_ref,
    kv0_ref,
    kv1_ref,
    kv2_ref,
    dq_ref,
    d0_ref,
    d1_ref,
    d2_ref,
    bias_ref,
    k_ref,
    v_ref,
    dk_ref,
    dv_ref,
):
    head = pl.program_id(0)
    each = pl.num_programs(0) // kv_heads
    rows = q_ref.shape[0]
    tiles, tile, width = bias_ref.shape
    kvh = head // each
    kcol = pl.ds(pl.multiple_of(kvh * HD, HD), HD)
    vcol = pl.ds(pl.multiple_of((kv_heads + kvh) * HD, HD), HD)

    @pl.when(head == 0)
    def _():
        make_bias(z_ref[0], start_ref, bias_ref)

    @pl.when(head % each == 0)
    def _():
        for j, ref in enumerate((kv0_ref, kv1_ref, kv2_ref)):
            k_ref[j * rows : (j + 1) * rows] = ref[:, kcol]
            v_ref[j * rows : (j + 1) * rows] = ref[:, vcol]
        dk_ref[...] = jnp.zeros_like(dk_ref)
        dv_ref[...] = jnp.zeros_like(dv_ref)

    for i in range(tiles):
        at, window = slice(i * tile, (i + 1) * tile), slice(i * tile, i * tile + width)
        q = q_ref[at]
        do = do_ref[at]
        centre = jnp.sum(do.astype(F32) * o_ref[at].astype(F32), axis=1, keepdims=True)
        soft = jnp.exp2(mm_nt(q, k_ref[window]) + (bias_ref[i] - lse_ref[0, at]))
        dv_ref[window] += mm_tn(soft.astype(BF16), do)
        dscore = (soft * (mm_nt(do, v_ref[window]) - centre)).astype(BF16)
        dk_ref[window] += mm_tn(dscore, q)
        dq = mm(dscore, k_ref[window]) * (HD**-0.5)
        dq_ref[at] = (dq * cos_ref[at] - swap_halves(dq) * sin_ref[at]).astype(BF16)

    @pl.when(head % each == each - 1)
    def _():
        for j, ref in enumerate((d0_ref, d1_ref, d2_ref)):
            at = slice(j * rows, (j + 1) * rows)
            ref[:, kcol] = (dk_ref[at] * (1 / LOG2E)).astype(ref.dtype)
            ref[:, vcol] = dv_ref[at].astype(ref.dtype)


def attend_back(z, start, q, o, do, lse, cos_full, sin_full, kvs, kv_heads):
    rows, columns = q.shape
    heads = columns // HD
    tile = ATTEND_TILE
    kv_columns = kvs[0].shape[1]
    kv_spec = pl.BlockSpec((rows, kv_columns), lambda h, s: (0, 0))
    head_spec = pl.BlockSpec((rows, HD), lambda h, s: (0, h))
    table_spec = pl.BlockSpec((rows, HD), lambda h, s: (0, 0))
    return pl.pallas_call(
        functools.partial(attend_back_kernel, kv_heads),
        grid_spec=pltpu.PrefetchScalarGridSpec(
            num_scalar_prefetch=1,
            grid=(heads,),
            in_specs=[
                pl.BlockSpec((rows, 1), lambda h, s: (0, 0)),
                head_spec,
                head_spec,
                head_spec,
                pl.BlockSpec((1, rows, 1), lambda h, s: (h, 0, 0)),
                table_spec,
                table_spec,
                *[kv_spec] * 3,
            ],
            out_specs=[head_spec, *[kv_spec] * 3],
            scratch_shapes=[
                pltpu.VMEM((rows // tile, tile, 2 * rows + tile), F32),
                pltpu.VMEM((3 * rows, HD), BF16),
                pltpu.VMEM((3 * rows, HD), BF16),
                pltpu.VMEM((3 * rows, HD), F32),
                pltpu.VMEM((3 * rows, HD), F32),
            ],
        ),
        out_shape=[
            jax.ShapeDtypeStruct((rows, columns), BF16),
            jax.ShapeDtypeStruct((rows, kv_columns), BF16),
            jax.ShapeDtypeStruct((rows, kv_columns), BF16),
            jax.ShapeDtypeStruct((rows, kv_columns), F32),
        ],
        compiler_params=params(),
        name="attend_back",
        cost_estimate=pl.CostEstimate(
            flops=30 * rows * rows * columns,
            bytes_accessed=12 * rows * columns,
            transcendentals=rows * rows * 3 * heads,
        ),
    )(z, start, q, o, do, lse, cos_full, sin_full, *kvs)


def expert_kernel(chunk, first, last, x_ref, dy_ref, gate_ref, wg_ref, wu_ref, wd_ref, *refs):
    if last:
        y_out, dn_out, hs_ref, dgu_ref, y_ref, dn_ref = refs[-6:]
    else:
        y_ref, dn_ref, hs_ref, dgu_ref = refs[-4:]
    step = pl.program_id(0)

    @pl.when(step == 0)
    def _():
        if first:
            y_ref[...] = jnp.zeros_like(y_ref)
            dn_ref[...] = jnp.zeros_like(dn_ref)
        else:
            y_ref[...] = refs[0][...]
            dn_ref[...] = refs[1][...]

    x = x_ref[...]
    gate = gate_ref[...].astype(F32)
    g = jnp.maximum(mm_nt(x, wg_ref[...]), 0.0)
    u = mm_nt(x, wu_ref[...])
    square = g * g
    hs = ((square * u).astype(BF16).astype(F32) * gate).astype(BF16)
    hs_ref[...] = hs
    dh = mm_nt(dy_ref[...], wd_ref[...]) * gate
    dg = (dh * u * (2.0 * g)).astype(BF16)
    du = (dh * square).astype(BF16)
    dgu_ref[:, :chunk] = dg
    dgu_ref[:, chunk:] = du
    dn_ref[...] += mm(dg, wg_ref[...]) + mm(du, wu_ref[...])
    y_ref[...] += mm(hs, wd_ref[...])
    if last:

        @pl.when(step == pl.num_programs(0) - 1)
        def _():
            y_out[...] = y_ref[...].astype(BF16)
            dn_out[...] = dn_ref[...].astype(BF16)


def experts(tile, x, dy, gate, wg, wu, wd, before=None, filled=None, last=False, chunk=512):
    rows, width = x.shape
    hidden = gate.shape[1]
    full = pl.BlockSpec((rows, width), lambda i: (0, 0))
    part = pl.BlockSpec((rows, chunk), lambda i: (0, i))
    operands = [x, dy, gate, wg, wu, wd]
    in_specs = [
        full,
        full,
        part,
        *[pl.BlockSpec((chunk, width), lambda i: (i, 0))] * 3,
    ]
    aliases = {}
    if before is not None:
        operands += list(before)
        in_specs += [full] * 2
    if filled is not None:
        aliases = {len(operands): 2, len(operands) + 1: 3}
        operands += list(filled)
        in_specs += [pl.BlockSpec(memory_space=pl.ANY)] * 2
    return pl.pallas_call(
        functools.partial(expert_kernel, chunk, before is None, last),
        grid=(hidden // chunk,),
        in_specs=in_specs,
        out_specs=[
            full,
            full,
            pl.BlockSpec((rows, chunk), lambda i: (tile, i)),
            pl.BlockSpec((rows, 2 * chunk), lambda i: (tile, i)),
        ],
        out_shape=[
            *[jax.ShapeDtypeStruct((rows, width), BF16 if last else F32)] * 2,
            jax.ShapeDtypeStruct((2 * rows, hidden), BF16),
            jax.ShapeDtypeStruct((2 * rows, 2 * hidden), BF16),
        ],
        scratch_shapes=[pltpu.VMEM((rows, width), F32)] * (2 if last else 0),
        input_output_aliases=aliases,
        compiler_params=params(),
        name="experts",
        cost_estimate=pl.CostEstimate(
            flops=12 * rows * width * hidden,
            bytes_accessed=6 * width * hidden + 16 * rows * width,
            transcendentals=0,
        ),
    )(*operands)


def pick(i, values):
    result = values[0]
    for at, value in enumerate(values):
        if at and value != values[at - 1]:
            result = jnp.where(i >= at, value, result)
    return result


def gradient_kernel(jobs, lefts, rights, *refs):
    send_refs, keep_refs, right_refs = refs[:lefts], refs[lefts : 2 * lefts], refs[2 * lefts :]
    outs, (sent, got, send, recv) = right_refs[rights:-4], refs[-4:]
    d = lax.axis_index("dp")
    step = pl.program_id(0)
    count = len(jobs)

    @pl.when(step == 0)
    def _():
        barrier = pltpu.get_barrier_semaphore()
        pl.semaphore_signal(
            barrier, inc=1, device_id={"dp": flip(d, 1)}, device_id_type=pl.DeviceIdType.MESH
        )
        pl.semaphore_wait(barrier, 1)

    def copy(i):
        return pltpu.make_async_remote_copy(
            src_ref=sent.at[i],
            dst_ref=got.at[i],
            send_sem=send.at[i],
            recv_sem=recv.at[i],
            device_id={"dp": flip(d, 1)},
            device_id_type=pl.DeviceIdType.MESH,
        )

    for i, (left, right, _) in enumerate(jobs):

        @pl.when(step == i)
        def _(i=i, left=left, right=right):
            sent[i] = mm(send_refs[left][...], right_refs[right][...]).astype(BF16)
            copy(i).start()

        @pl.when(step == count + i)
        def _(i=i, left=left, right=right):
            value = mm(keep_refs[left][...], right_refs[right][...])
            copy(i).wait()
            value = value + got[i].astype(F32)
            half = value.shape[0] // 2
            side = 2 * (i // (count // 2))
            outs[side][...] = value[:half].astype(BF16)
            outs[side + 1][...] = value[half:].astype(BF16)


def gradients(jobs, send_lefts, keep_lefts, rights, ident, chunk=768):
    rows, tokens = keep_lefts[0].shape
    count = len(jobs)
    each = count // 2
    first = lambda i: (0, jnp.clip(i - count, 0, each - 1))
    second = lambda i: (0, jnp.maximum(i - count - each, 0))
    right_specs = []
    for r in range(len(rights)):
        blocks, at = [], None
        for _, right, block in jobs + jobs:
            at = block if right == r else at
            blocks.append(at)
        known = next(block for block in blocks if block is not None)
        blocks = tuple(known if block is None else block for block in blocks)
        right_specs.append(
            pl.BlockSpec((tokens, chunk), lambda i, blocks=blocks: (0, pick(i, blocks)))
        )
    left = pl.BlockSpec((rows, tokens), lambda i: (0, 0), pipeline_mode=pl.Buffered(1))
    return pl.pallas_call(
        functools.partial(gradient_kernel, jobs, len(keep_lefts), len(rights)),
        grid=(2 * count,),
        in_specs=[*[left] * (2 * len(keep_lefts)), *right_specs],
        out_specs=[
            pl.BlockSpec((rows // 2, chunk), at) for at in (first, first, second, second)
        ],
        out_shape=[jax.ShapeDtypeStruct((rows // 2, each * chunk), BF16)] * 4,
        scratch_shapes=[
            pltpu.VMEM((count, rows, chunk), BF16),
            pltpu.VMEM((count, rows, chunk), BF16),
            pltpu.SemaphoreType.DMA((count,)),
            pltpu.SemaphoreType.DMA((count,)),
        ],
        compiler_params=pltpu.CompilerParams(
            vmem_limit_bytes=56 * 2**20, collective_id=ident, has_side_effects=True
        ),
        name="gradients",
        cost_estimate=pl.CostEstimate(flops=10**9, bytes_accessed=10**6, transcendentals=0),
    )(*send_lefts, *keep_lefts, *rights)


def part_kernel(jobs, lefts, rights, keep, *refs):
    left_refs, right_refs, rest = refs[:lefts], refs[lefts : lefts + rights], refs[lefts + rights :]
    step = pl.program_id(0)
    each = len(jobs) // 2
    for i, (left, right, _) in enumerate(jobs):

        @pl.when(step == i)
        def _(i=i, left=left, right=right):
            side = i // each
            value = mm(left_refs[left][...], right_refs[right][...])
            if keep:
                value = value + rest[0][0].astype(F32)
                half = value.shape[0] // 2
                rest[1 + 2 * side][...] = value[:half].astype(BF16)
                rest[2 + 2 * side][...] = value[half:].astype(BF16)
            else:
                rest[0][0] = value.astype(BF16)


def gradient_parts(jobs, lefts, rights, got=None, chunk=768):
    rows, tokens = lefts[0].shape
    each = len(jobs) // 2
    first = lambda i: (0, jnp.minimum(i, each - 1))
    second = lambda i: (0, jnp.maximum(i - each, 0))
    whole = [pl.BlockSpec((1, rows, chunk), lambda i: (i // each, 0, i % each))]
    if got is None:
        out_specs = whole[0]
        out_shape = jax.ShapeDtypeStruct((2, rows, each * chunk), BF16)
    else:
        out_specs = [pl.BlockSpec((rows // 2, chunk), at) for at in (first, first, second, second)]
        out_shape = [jax.ShapeDtypeStruct((rows // 2, each * chunk), BF16)] * 4
    right_specs = []
    for r in range(len(rights)):
        at, blocks = None, []
        for _, right, block in jobs:
            at = block if right == r else at
            blocks.append(at)
        known = next(block for block in blocks if block is not None)
        blocks = tuple(known if block is None else block for block in blocks)
        right_specs.append(
            pl.BlockSpec((tokens, chunk), lambda i, blocks=blocks: (0, pick(i, blocks)))
        )
    return pl.pallas_call(
        functools.partial(part_kernel, jobs, len(lefts), len(rights), got is not None),
        grid=(2 * each,),
        in_specs=[
            *[pl.BlockSpec((rows, tokens), lambda i: (0, 0))] * len(lefts),
            *right_specs,
            *(() if got is None else whole),
        ],
        out_specs=out_specs,
        out_shape=out_shape,
        compiler_params=params(),
        name="gradient_parts",
        cost_estimate=pl.CostEstimate(
            flops=4 * each * rows * tokens * chunk,
            bytes_accessed=4 * each * (rows + tokens) * chunk,
            transcendentals=0,
        ),
    )(*lefts, *rights, *(() if got is None else (got,)))


EXPERT_JOBS = ((0, 0, 0), (0, 0, 1), (1, 1, 0), (2, 0, 2), (2, 0, 3), (3, 1, 1))


def flip(index, mask):
    for bit in (1, 2, 4):
        if mask & bit:
            index = index + bit - 2 * bit * (index // bit % 2)
    return index


def mix_kernel(
    dq_ref,
    o_ref,
    n_send,
    n_keep,
    d_send,
    d_keep,
    one_ref,
    two_ref,
    fa_keep,
    fa_got,
    fb_keep,
    fb_got,
    q_keep,
    q_send,
    o_keep,
    o_send,
    got_one,
    far_ref,
    got_two,
    both_ref,
    sent,
    got,
    halves,
    lasts,
    send,
    recv,
):
    d = lax.axis_index("dp")
    z = lax.axis_index("tensor")
    z_count = lax.axis_size("tensor")
    pairs = [{"dp": flip(d, bit)} for bit in (1, 2, 4)]
    others = [{"tensor": (z + m) % z_count} for m in range(1, z_count)]
    barrier = pltpu.get_barrier_semaphore()
    for peer in pairs + others:
        pl.semaphore_signal(barrier, inc=1, device_id=peer, device_id_type=pl.DeviceIdType.MESH)
    pl.semaphore_wait(barrier, len(pairs) + len(others))

    def start(src, dst, at, to):
        copy = pltpu.make_async_remote_copy(
            src_ref=src,
            dst_ref=dst,
            send_sem=send.at[at],
            recv_sem=recv.at[at],
            device_id=to,
            device_id_type=pl.DeviceIdType.MESH,
        )
        copy.start()
        return copy

    step_two = start(two_ref, got_two, 1, others[-1])
    rows = halves.shape[1]
    far_copies = []
    for side, (keep, arrived) in enumerate(((fa_keep, fa_got), (fb_keep, fb_got))):
        total = keep[rows:].astype(F32) + arrived[rows:].astype(F32)
        halves[side] = total.astype(BF16)
        far_copies.append(start(halves.at[side], lasts.at[side], 2 + side, pairs[2 - side]))

    columns = dq_ref.shape[1]
    chunk = columns // 4

    def at_chunk(i):
        return pl.ds(pl.multiple_of(i * chunk, chunk), chunk)

    sides = ((dq_ref, n_send, n_keep, q_keep, q_send), (o_ref, d_send, d_keep, o_keep, o_send))
    core_copies = []
    for side, (right, left, _, _, _) in enumerate(sides):

        def compute_send(i, carry, side=side, right=right, left=left):
            at = at_chunk(i)
            sent[side, :, at] = mm(left[...], right[:, at]).astype(BF16)
            return carry

        lax.fori_loop(0, 4, compute_send, 0)
        core_copies.append(start(sent.at[side], got.at[side], 4 + side, pairs[0]))
        if side == 0:
            step_two.wait()
            both_ref[...] = (one_ref[...].astype(F32) + got_two[...].astype(F32)).astype(BF16)
            step_one = start(both_ref, got_one, 0, others[-1])
    for side, (right, _, left, keep, away) in enumerate(sides):
        core_copies[side].wait()

        def compute_keep(i, carry, side=side, right=right, left=left, keep=keep, away=away):
            at = at_chunk(i)
            value = mm(left[...], right[:, at]) + got[side, :, at].astype(F32)
            half = value.shape[0] // 2
            keep[:, at] = value[:half].astype(BF16)
            away[:, at] = value[half:].astype(BF16)
            return carry

        lax.fori_loop(0, 4, compute_keep, 0)
    for side, (keep, arrived) in enumerate(((fa_keep, fa_got), (fb_keep, fb_got))):
        far_copies[side].wait()
        total = keep[:rows].astype(F32) + arrived[:rows].astype(F32) + lasts[side].astype(F32)
        far_ref[side] = total.astype(BF16)
    step_one.wait()


def mix(dq, o, lefts, dkv_one, dkv_two, far_parts):
    rows2, columns = far_parts[0].shape
    rows = rows2 // 2
    wide = dq.shape[1]
    vmem = pl.BlockSpec(memory_space=pltpu.VMEM)
    half = jax.ShapeDtypeStruct((rows2, wide), BF16)
    block = jax.ShapeDtypeStruct(dkv_one.shape, BF16)
    return pl.pallas_call(
        mix_kernel,
        in_specs=[vmem] * 12,
        out_specs=[vmem] * 6,
        out_shape=[half] * 4 + [block] + [jax.ShapeDtypeStruct((2, rows, columns), BF16)],
        scratch_shapes=[
            pltpu.VMEM(block.shape, BF16),
            pltpu.VMEM(block.shape, BF16),
            pltpu.VMEM((2, 2 * rows2, wide), BF16),
            pltpu.VMEM((2, 2 * rows2, wide), BF16),
            pltpu.VMEM((2, rows, columns), BF16),
            pltpu.VMEM((2, rows, columns), BF16),
            pltpu.SemaphoreType.DMA((6,)),
            pltpu.SemaphoreType.DMA((6,)),
        ],
        compiler_params=pltpu.CompilerParams(
            vmem_limit_bytes=56 * 2**20, collective_id=2, has_side_effects=True
        ),
        name="mix",
    )(dq, o, *lefts, dkv_one, dkv_two, *far_parts)


def finish_kernel(
    dx_ref,
    out_ref,
    q_keep,
    q_send,
    o_keep,
    o_send,
    s_send,
    s_keep,
    a_keep,
    a_got,
    b_keep,
    b_got,
    back_ref,
    back_out_ref,
    q_ref,
    o_ref,
    s_ref,
    own_ref,
    own_half,
    own_last,
    q_got,
    o_got,
    q_half,
    o_half,
    q_last,
    o_last,
    s_got,
    s_half,
    s_got2,
    s_quarter,
    s_last,
    z_mine,
    z_got,
    k_mine,
    k_half,
    k_got,
    deal_send,
    deal_recv,
    send,
    recv,
):
    d = lax.axis_index("dp")
    z = lax.axis_index("tensor")
    count = dx_ref.shape[0]
    z_count = z_mine.shape[0]
    barrier = pltpu.get_barrier_semaphore()
    for p in range(1, count):
        pl.semaphore_signal(
            barrier, inc=1, device_id={"dp": flip(d, p)}, device_id_type=pl.DeviceIdType.MESH
        )
    for m in range(1, z_count):
        pl.semaphore_signal(
            barrier, inc=1, device_id={"tensor": flip(z, m)}, device_id_type=pl.DeviceIdType.MESH
        )
    pl.semaphore_wait(barrier, count - 1 + z_count - 1)

    def start(src, dst, at, to):
        copy = pltpu.make_async_remote_copy(
            src_ref=src,
            dst_ref=dst,
            send_sem=send.at[at],
            recv_sem=recv.at[at],
            device_id=to,
            device_id_type=pl.DeviceIdType.MESH,
        )
        copy.start()
        return copy

    one, two, four = [{"dp": flip(d, bit)} for bit in (1, 2, 4)]
    q_one = start(q_send, q_got, 1, two)
    o_one = start(o_send, o_got, 2, four)
    s_one = start(s_send, s_got, 0, one)
    back_ref[d] = dx_ref[d]
    back_out_ref[d] = out_ref[d]
    rows = q_last.shape[0]
    s_one.wait()
    total = s_keep[...].astype(F32) + s_got[...].astype(F32)
    s_keep2 = total[: 2 * rows]
    s_half[...] = total[2 * rows :].astype(BF16)
    s_two = start(s_half, s_got2, 3, four)
    q_one.wait()
    q_half[...] = (q_keep[rows:].astype(F32) + q_got[rows:].astype(F32)).astype(BF16)
    q_two = start(q_half, q_last, 4, four)
    o_one.wait()
    o_half[...] = (o_keep[rows:].astype(F32) + o_got[rows:].astype(F32)).astype(BF16)
    o_two = start(o_half, o_last, 5, two)
    s_two.wait()
    total = s_keep2 + s_got2[...].astype(F32)
    s_quarter[...] = total[rows:].astype(BF16)
    s_three = start(s_quarter, s_last, 6, two)
    own_copies = []
    for side, (keep, got, to) in enumerate(((a_keep, a_got, four), (b_keep, b_got, two))):
        total = keep[...].astype(F32) + got[...].astype(F32)
        own_ref[side] = total[:rows]
        own_half[side] = total[rows:].astype(BF16)
        own_copies.append(start(own_half.at[side], own_last.at[side], 12 + side, to))
    total = s_keep2 + s_got2[...].astype(F32)
    deals = []
    for i, (src, dst) in enumerate(((dx_ref, back_ref), (out_ref, back_out_ref))):
        for p in range(1, count):
            copy = pltpu.make_async_remote_copy(
                src_ref=src.at[flip(d, p)],
                dst_ref=dst.at[d],
                send_sem=deal_send.at[i, p - 1],
                recv_sem=deal_recv.at[i, p - 1],
                device_id={"dp": flip(d, p)},
                device_id_type=pl.DeviceIdType.MESH,
            )
            copy.start()
            deals.append(copy)
    s_own = total[:rows]
    s_three.wait()
    s_own = s_own + s_last[...].astype(F32)
    k_mine[...] = s_own.astype(BF16)
    k_near = start(k_mine, k_got.at[0], 7, {"tensor": flip(z, 1)})
    finals = []
    part = q_ref.shape[1]
    for two_copy, keep, got, last, side in (
        (q_two, q_keep, q_got, q_last, 0),
        (o_two, o_keep, o_got, o_last, 1),
    ):
        two_copy.wait()
        total = (
            keep[:rows].astype(F32) + got[:rows].astype(F32) + last[...].astype(F32)
        )
        for i in range(z_count):
            block = total[:, i * part : (i + 1) * part]
            z_mine[i, :, side * part : (side + 1) * part] = block.astype(BF16)
    for m in range(1, z_count):
        finals.append(start(z_mine.at[flip(z, m)], z_got.at[m - 1], 8 + m, {"tensor": flip(z, m)}))
    k_near.wait()
    s_own = s_own + k_got[0].astype(F32)
    k_half[...] = s_own.astype(BF16)
    k_far = start(k_half, k_got.at[1], 8, {"tensor": flip(z, 2)})
    for copy in finals:
        copy.wait()
    total = z_mine[z].astype(F32)
    for m in range(z_count - 1):
        total = total + z_got[m].astype(F32)
    q_ref[...] = total[:, :part]
    o_ref[...] = total[:, part:]
    k_far.wait()
    s_ref[...] = s_own + k_got[1].astype(F32)
    for side, copy in enumerate(own_copies):
        copy.wait()
        own_ref[side] += own_last[side].astype(F32)
    for copy in deals:
        copy.wait()


def finish(dx, out, q_keep, q_send, o_keep, o_send, s_send, s_keep, own, z_count):
    count = dx.shape[0]
    rows = q_keep.shape[0] // 2
    columns = q_keep.shape[1]
    small = s_keep.shape[1]
    part = columns // z_count
    vmem = pl.BlockSpec(memory_space=pltpu.VMEM)
    dma = pltpu.SemaphoreType.DMA
    return pl.pallas_call(
        finish_kernel,
        in_specs=[vmem] * 12,
        out_specs=[vmem] * 6,
        out_shape=[
            jax.ShapeDtypeStruct(dx.shape, BF16),
            jax.ShapeDtypeStruct(dx.shape, BF16),
            jax.ShapeDtypeStruct((rows, part), F32),
            jax.ShapeDtypeStruct((rows, part), F32),
            jax.ShapeDtypeStruct((rows, small), F32),
            jax.ShapeDtypeStruct((2, rows, own[0].shape[1]), F32),
        ],
        scratch_shapes=[
            pltpu.VMEM((2, rows, own[0].shape[1]), BF16),
            pltpu.VMEM((2, rows, own[0].shape[1]), BF16),
            pltpu.VMEM((2 * rows, columns), BF16),
            pltpu.VMEM((2 * rows, columns), BF16),
            pltpu.VMEM((rows, columns), BF16),
            pltpu.VMEM((rows, columns), BF16),
            pltpu.VMEM((rows, columns), BF16),
            pltpu.VMEM((rows, columns), BF16),
            pltpu.VMEM((4 * rows, small), BF16),
            pltpu.VMEM((2 * rows, small), BF16),
            pltpu.VMEM((2 * rows, small), BF16),
            pltpu.VMEM((rows, small), BF16),
            pltpu.VMEM((rows, small), BF16),
            pltpu.VMEM((z_count, rows, 2 * part), BF16),
            pltpu.VMEM((z_count - 1, rows, 2 * part), BF16),
            pltpu.VMEM((rows, small), BF16),
            pltpu.VMEM((rows, small), BF16),
            pltpu.VMEM((2, rows, small), BF16),
            dma((2, count - 1)),
            dma((2, count - 1)),
            dma((7 + 2 * z_count,)),
            dma((7 + 2 * z_count,)),
        ],
        compiler_params=pltpu.CompilerParams(
            vmem_limit_bytes=56 * 2**20, collective_id=0, has_side_effects=True
        ),
        name="finish",
    )(dx, out, q_keep, q_send, o_keep, o_send, s_send, s_keep, *own)


def assemble_kernel(own_ref, far_ref, gate_ref, up_ref, down_ref):
    count, rows, columns = gate_ref.shape
    a, b = [own_ref[side] + far_ref[side].astype(F32) for side in (0, 1)]
    gate = jnp.concatenate([a[:, :512], a[:, 1024:1536], b[:, 512:1024]], axis=1)
    up = jnp.concatenate([a[:, 512:1024], b[:, :512], b[:, 1024:1536]], axis=1)
    down = jnp.concatenate([a[:, 1536:], b[:, 1536:]], axis=1)
    pad = jnp.zeros((256 - rows, down.shape[1]), F32)
    down = jnp.concatenate([down, pad], axis=0).T[:, :rows]
    for e in range(count):
        at = slice(e * columns, (e + 1) * columns)
        gate_ref[e] = gate[:, at]
        up_ref[e] = up[:, at]
        down_ref[e] = down[at]


def assemble(own, far_sum, count):
    _, rows, columns = own.shape
    part = columns * 2 // (3 * count)
    vmem = pl.BlockSpec(memory_space=pltpu.VMEM)
    wide = jax.ShapeDtypeStruct((count, rows, part), F32)
    return pl.pallas_call(
        assemble_kernel,
        in_specs=[vmem] * 2,
        out_specs=[vmem] * 3,
        out_shape=[wide, wide, jax.ShapeDtypeStruct((count, part, rows), F32)],
        compiler_params=params(),
        name="assemble",
    )(own, far_sum)


def turn_kernel(orders, d_ref, *refs):
    tiles = len(refs) - 1 - len(orders)
    scratch_ref = refs[-1]
    step = pl.program_id(0)
    for t in range(tiles):

        @pl.when(step == t)
        def _(t=t):
            scratch_ref[...] = refs[t][...].T

    for order, out_ref in zip(orders, refs[tiles:-1]):
        size = out_ref.shape[0] // len(order)
        for i, p in enumerate(order):
            block = jnp.bitwise_xor(d_ref[0], p)
            at = pl.multiple_of(block * size, size)
            out_ref[i * size : (i + 1) * size, :] = scratch_ref[pl.ds(at, size), :]


def turn(d, tiles, orders, blocks):
    rows, width = tiles[0].shape
    size = width // blocks
    return pl.pallas_call(
        functools.partial(turn_kernel, orders),
        grid_spec=pltpu.PrefetchScalarGridSpec(
            num_scalar_prefetch=1,
            grid=(len(tiles),),
            in_specs=[pl.BlockSpec((rows, width), lambda t, s: (0, 0))] * len(tiles),
            out_specs=[
                pl.BlockSpec((len(order) * size, rows), lambda t, s: (0, t)) for order in orders
            ],
            scratch_shapes=[pltpu.VMEM((width, rows), BF16)],
        ),
        out_shape=[
            jax.ShapeDtypeStruct((len(order) * size, rows * len(tiles)), BF16) for order in orders
        ],
        compiler_params=params(),
        name="turn",
        cost_estimate=pl.CostEstimate(
            flops=0, bytes_accessed=6 * rows * width * len(tiles), transcendentals=0
        ),
    )(d, *tiles)


def tie(*values):
    return lax.optimization_barrier(values)


def row_major(x):
    return with_layout_constraint(x, Layout(major_to_minor=tuple(range(x.ndim))))


def per_device(
    tokens,
    perm,
    routes,
    gates,
    lengths,
    cotangent,
    gain_attn,
    w_query,
    w_keyval,
    w_out,
    gain_moe,
    w_gate,
    w_up,
    w_down,
):
    dp_count = lax.axis_size("dp")
    tensor_count = lax.axis_size("tensor")
    d = lax.axis_index("dp")
    z = lax.axis_index("tensor")
    rows, width = tokens.shape
    group_rows = perm.shape[0]
    share = rows // dp_count
    top = routes.shape[1]
    experts_n, _, part_hidden = w_gate.shape
    hidden = experts_n * part_hidden
    capacity = 9 * group_rows * top // (8 * experts_n)
    kv_heads = w_keyval.shape[1] // (2 * HD)
    query_cols = w_query.shape[1]
    team = 8
    teams = [[t * team + i for i in range(team)] for t in range(dp_count // team)]
    teams = None if len(teams) == 1 else teams
    piece_rows = width // team
    member = d % team

    def z_move(x, pairs):
        return lax.ppermute(x, "tensor", pairs)

    def dp_move(x, bit):
        return lax.ppermute(x, "dp", [(i, i ^ bit) for i in range(dp_count)])

    near, far, across = [[(i, i ^ m) for i in range(tensor_count)] for m in (1, 2, 3)]
    up_one, up_two = [[(i, i + m) for i in range(tensor_count - m)] for m in (1, 2)]

    def deal(x):
        return lax.all_to_all(
            x.reshape(dp_count, share, x.shape[1]), "dp", split_axis=0, concat_axis=0, tiled=True
        ).reshape(rows, x.shape[1])

    def team_gather(x):
        return lax.all_gather(x, "dp", axis=0, tiled=True, axis_index_groups=teams)

    def flat(w):
        return w.transpose(0, 2, 1).reshape(hidden, w.shape[1])

    own_perm = lax.dynamic_slice_in_dim(perm, z * rows, rows, 0)
    own_routes = lax.dynamic_slice_in_dim(routes, z * rows, rows, 0)
    dest = own_perm // group_rows
    place = own_perm % rows
    row_index = jnp.arange(rows, dtype=jnp.int32)
    lower = (row_index[:, None] > row_index[None, :]).astype(BF16)
    dest_hot = (dest[:, None] == jnp.arange(dp_count, dtype=jnp.int32)[None, :]).astype(BF16)
    earlier = jnp.sum(mm(lower, dest_hot) * dest_hot.astype(F32), axis=1).astype(jnp.int32)
    slot = dest * share + earlier
    pack = (row_index[:, None] == slot[None, :]).astype(BF16)
    meta = jnp.concatenate(
        [
            (place // 16)[:, None].astype(BF16),
            (place % 16)[:, None].astype(BF16),
            own_routes.astype(BF16),
            gates,
            jnp.zeros((rows, META - 2 - 2 * top), BF16),
        ],
        axis=1,
    )
    packed = mm(pack, jnp.concatenate([tokens, meta], axis=1)).astype(BF16)
    wg_own, wu_own = flat(w_gate), flat(w_up)
    wd_own = w_down.reshape(hidden, width)
    out_rows = query_cols // team
    hidden_piece = hidden // team

    def piece(w, count):
        return lax.dynamic_slice_in_dim(w, member * count, count, 0)

    wg_piece, wu_piece, wd_piece = [piece(w, hidden_piece) for w in (wg_own, wu_own, wd_own)]
    packed_dy = mm(pack, cotangent).astype(BF16)
    packed, packed_dy = tie(packed, packed_dy)
    arrived, wq_z, wo_z = open_moves(
        packed.reshape(dp_count, share, width + META),
        piece(w_query, piece_rows),
        piece(w_out, out_rows),
        tensor_count,
    )
    arrived, wg_piece, wu_piece = tie(arrived.reshape(rows, width + META), wg_piece, wu_piece)
    wg_moved, wu_moved = z_move(wg_piece, far), z_move(wu_piece, far)
    wq_all = team_gather(wq_z).reshape(team, tensor_count, piece_rows, query_cols)
    wo_all = team_gather(wo_z).reshape(team, tensor_count, out_rows, width)
    wo = wo_all.transpose(1, 0, 2, 3).reshape(tensor_count * query_cols, width)

    meta_in = arrived[:, width:].astype(F32)
    place_in = (meta_in[:, 0] * 16.0 + meta_in[:, 1]).astype(jnp.int32)
    unpack = (row_index[:, None] == place_in[None, :]).astype(BF16)
    dealt = mm(unpack, arrived)
    x_rows = dealt[:, :width]
    meta_rows = dealt[:, width:]

    expert_ids = jnp.arange(experts_n, dtype=jnp.int32).astype(F32)
    route_rows = meta_rows[:, 2 : 2 + top]
    gate_rows = meta_rows[:, 2 + top : 2 + 2 * top]
    hot = route_rows[:, :, None] == expert_ids[None, None, :]
    routed = jnp.sum(hot.astype(F32), axis=1)
    counts = jnp.pad(jnp.sum(routed, axis=0)[None, :], ((0, 7), (0, HD - experts_n)))

    seq_lengths = lengths[0]
    seq_index = jnp.arange(seq_lengths.shape[0], dtype=jnp.int32)
    seq_ends = jnp.sum(
        jnp.where(seq_index[None, :] <= seq_index[:, None], seq_lengths[None, :], 0), axis=1
    ).astype(jnp.int32)
    global_row = z * rows + row_index
    start = jnp.max(
        jnp.where(global_row[:, None] >= seq_ends[None, :], seq_ends[None, :], 0), axis=1
    ).astype(jnp.int32)
    offset = (global_row - start).astype(F32)
    frequency = ROPE_BASE ** (-2.0 * jnp.arange(HD // 2, dtype=F32) / HD)
    angles = offset[:, None] * frequency[None, :]
    cosine, sine = jnp.cos(angles), jnp.sin(angles)
    cos_full = jnp.concatenate([cosine, cosine], axis=1)
    sin_full = jnp.concatenate([-sine, sine], axis=1)
    start = start[:, None]
    z_arg = z.astype(jnp.int32)[None]

    inv_one = lax.rsqrt(jnp.mean(x_rows * x_rows, axis=1, keepdims=True) + EPS)
    n1 = (x_rows * inv_one * gain_attn).astype(BF16)
    weight = jnp.sum(jnp.where(hot, gate_rows[:, :, None], 0.0), axis=1)
    marks = jnp.pad(
        jnp.concatenate([routed, weight], axis=1).astype(BF16), ((0, 0), (0, HD - 2 * experts_n))
    )
    kv, kv_one, kv_two, counts, marks_near, arrived_dy = keyval(
        n1,
        w_keyval,
        cos_full,
        sin_full,
        counts,
        marks,
        packed_dy.reshape(dp_count, share, width),
        tensor_count,
    )
    arrived_dy = arrived_dy.reshape(rows, width)
    kv, n1, wg_moved, wu_moved = tie(kv, n1, wg_moved, wu_moved)

    dy_rows = mm(unpack, arrived_dy).astype(BF16)
    n1, dy_rows = tie(n1, dy_rows)
    q = project_query(z_arg, n1, wq_all, cos_full, sin_full)
    dy_near = z_move(dy_rows, near)
    kvs = (kv_two, kv_one, kv)
    o, lse = attend(z_arg, start, q, kvs, kv_heads)
    o, wd_piece, dy_near, counts, weight, marks_near = tie(
        o, wd_piece, dy_near, counts, weight, marks_near
    )

    def kept_gates(routed, weight, at):
        block = (z - 1 - jnp.arange(tensor_count, dtype=jnp.int32)) % tensor_count
        base = jnp.sum(
            jnp.where((block < at)[:, None], counts[:, 0, :experts_n], 0.0), axis=0
        )
        position = mm(lower, routed.astype(BF16)) + base[None, :]
        weight = jnp.where(position < capacity, weight, 0.0).astype(BF16)
        return row_major(jnp.repeat(weight, part_hidden, axis=1))

    gate_own = kept_gates(routed, weight, z)
    marks_near = marks_near.astype(F32)
    gate_near = kept_gates(
        marks_near[:, :experts_n], marks_near[:, experts_n : 2 * experts_n], z + 1 - 2 * (z % 2)
    )
    wg_far = team_gather(wg_moved)
    wu_far = team_gather(wu_moved)
    h = x_rows + mm(o, wo)
    inv_two = lax.rsqrt(jnp.mean(h * h, axis=1, keepdims=True) + EPS)
    n2 = (h * inv_two * gain_moe).astype(BF16)

    halving = dp_count == 8
    d_arg = d.astype(jnp.int32)[None]
    out_w = width // dp_count
    orders_a = ((1, 5, 3, 7), (0, 4, 2, 6))
    orders_b = ((1, 3, 5, 7), (0, 2, 4, 6))

    def turned(tiles, *orders):
        if halving:
            return turn(d_arg, tiles, orders, dp_count)
        return [jnp.concatenate(tiles, axis=0).T] * len(orders)

    def dp_sum(x):
        return lax.psum_scatter(x, "dp", scatter_dimension=0, tiled=True)

    def first_moves(parts):
        return parts[0], dp_move(parts[1], xy[0]), parts[2], dp_move(parts[3], yx[0])

    def expert_lefts(n_a, d_a, keep):
        return n_a[keep], d_a[keep], n_a[2 + keep], d_a[2 + keep]

    xy, yx = (2, 4), (4, 2)
    n2_near = z_move(n2, near)
    y, dn2, *own_grads = experts(0, n2, dy_rows, gate_own, wg_own, wu_own, wd_own)
    n2_near, y, wd_piece = tie(n2_near, y, wd_piece)
    n2_a = turned((n2, n2_near), *orders_a, *orders_b)
    n1_t = turned((n1,), *orders_a, *orders_b)
    dy_near, *turns = tie(dy_near, *n2_a, *n1_t)
    n2_a, n1_t = turns[:4], turns[4:]
    wd_moved = z_move(wd_piece, far)
    yn, dnn, *own_grads = experts(
        1, n2_near, dy_near, gate_near, wg_own, wu_own, wd_own, filled=own_grads
    )
    yn, wd_moved, *own_grads = tie(yn, wd_moved, *own_grads)
    wd_far = team_gather(wd_moved)
    dy_a = turned((dy_rows, dy_near), *orders_a, *orders_b)
    if halving:
        own = gradients(
            EXPERT_JOBS,
            expert_lefts(n2_a, dy_a, 0),
            expert_lefts(n2_a, dy_a, 1),
            own_grads[::-1],
            3,
        )
        wg_far, *own = tie(wg_far, *own)
        own = first_moves(own)
    yn, dnn, *far_grads = experts(
        1, n2_near, dy_near, gate_near, wg_far, wu_far, wd_far, (yn, dnn), last=True
    )
    dnn_moved = z_move(dnn, near)
    y, dn2, *far_grads = experts(
        0, n2, dy_rows, gate_own, wg_far, wu_far, wd_far, (y, dn2), far_grads
    )
    if halving:
        far_grads = far_grads[::-1]
        far_sent = gradient_parts(EXPERT_JOBS, expert_lefts(n2_a, dy_a, 0), far_grads)
        dnn_moved, far_sent, *own = tie(dnn_moved, far_sent, *own)
        got = dp_move(far_sent, 1)
    yn, dnn_moved = tie(yn, dnn_moved)
    yn_moved = z_move(yn, near)
    dn2 = dn2 + dnn_moved.astype(F32)

    gain_two_part = jnp.sum(dn2 * h * inv_two, axis=0)
    u2 = dn2 * gain_moe
    dh = dy_rows.astype(F32) + inv_two * (
        u2 - h * inv_two * inv_two * jnp.mean(u2 * h, axis=1, keepdims=True)
    )
    dhb = dh.astype(BF16)
    do = mm_nt(dhb, wo).astype(BF16)
    if halving:
        far_w = gradient_parts(EXPERT_JOBS, expert_lefts(n2_a, dy_a, 1), far_grads, got)
        do, *far_w = tie(do, *far_w)
        far_w = first_moves(far_w)
    dq, dkv_two, dkv_one, dkv = attend_back(
        z_arg, start, q, o, do, lse, cos_full, sin_full, kvs, kv_heads
    )
    dhb_t = turned((dhb,), *orders_b)
    if halving:
        dq, *far_w = tie(dq, *far_w)
        *parts, dkv_sum, far_sum = mix(
            dq, o, (n1_t[0], n1_t[1], *dhb_t), dkv_one, dkv_two, far_w
        )
        far_sum = [z_move(part, far) for part in jnp.split(far_sum.reshape(-1, far_sum.shape[2]), 2, axis=0)]
        far_sum = jnp.concatenate(far_sum, axis=0).reshape(2, out_w, -1)
        dkv_sum, yn_moved = tie(dkv_sum, yn_moved)
    else:
        dkv_one = z_move(dkv_one, [(b, a) for a, b in up_one])
        dkv_two = z_move(dkv_two, [(b, a) for a, b in up_two])
        dkv_sum = dkv_one.astype(F32) + dkv_two.astype(F32)
        sum_q, sum_o = [
            dp_sum(mm_tn(a, b).astype(BF16)).astype(F32) for a, b in ((n1, dq), (dhb, o))
        ]
    dkv = dkv + dkv_sum.astype(F32)

    def unrotate(u):
        swapped = jnp.concatenate([u[:, HD // 2 :], u[:, : HD // 2]], axis=1)
        return u * cos_full - swapped * sin_full

    dkv = jnp.concatenate(
        [unrotate(dkv[:, i * HD : (i + 1) * HD]) for i in range(kv_heads)]
        + [dkv[:, kv_heads * HD :]],
        axis=1,
    ).astype(BF16)
    dn1 = project_back(z_arg, dq, wq_all, dkv, w_keyval)
    gain_one_part = jnp.sum(dn1 * x_rows * inv_one, axis=0)
    u1 = dn1 * gain_attn
    dx = dh + inv_one * (
        u1 - x_rows * inv_one * inv_one * jnp.mean(u1 * x_rows, axis=1, keepdims=True)
    )

    result = h + y + yn_moved.astype(F32)
    result_out = mm_tn(unpack, result.astype(BF16)).astype(BF16)

    if not halving:
        lefts = (n2_a[0], dy_a[0])
        far_sums = [dp_sum(mm(a, b).astype(BF16)) for a, b in zip(lefts, far_grads[::-1])]
        own_sums = [dp_sum(mm(a, b).astype(BF16)) for a, b in zip(lefts, own_grads[::-1])]
        sum_gu, sum_down = [
            a.astype(F32) + z_move(b, far).astype(F32) for a, b in zip(own_sums, far_sums)
        ]
        sum_gu = sum_gu.reshape(out_w, hidden // 512, 2, 512)
        sum_gate, sum_up = [
            sum_gu[:, :, i].reshape(out_w, experts_n, part_hidden).transpose(1, 0, 2) for i in (0, 1)
        ]
        sum_down = sum_down.reshape(out_w, experts_n, part_hidden).transpose(1, 2, 0)

    gains = jnp.stack([gain_one_part, gain_two_part])

    def gain_columns(order):
        blocks = gains.reshape(2, dp_count, out_w)
        if halving:
            blocks = jnp.stack(
                [lax.dynamic_index_in_dim(blocks, d ^ p, 1, keepdims=False) for p in order], 1
            )
        return jnp.pad(blocks.reshape(2, -1).T, ((0, 0), (dkv.shape[1], HD - 2)))

    columns = [gain_columns(order) for order in orders_b]
    dkv_wide = jnp.pad(dkv, ((0, 0), (0, HD)))
    if halving:
        kv_send, kv_keep = [
            (mm(left, dkv_wide) + column).astype(BF16) for left, column in zip(n1_t[2:], columns)
        ]
        dx_out = mm_tn(unpack, dx.astype(BF16)).astype(BF16).reshape(dp_count, share, width)
        back, back_out, sum_query, sum_out, small, own_sum = finish(
            dx_out,
            result_out.reshape(dp_count, share, width),
            *parts,
            kv_send,
            kv_keep,
            own,
            tensor_count,
        )
        sum_gate, sum_up, sum_down = assemble(own_sum, far_sum, experts_n)
        grad_tokens = mm_tn(pack, back.reshape(rows, width)).astype(BF16)
        outputs = mm_tn(pack, back_out.reshape(rows, width)).astype(BF16)
    else:
        outputs = mm_tn(pack, deal(result_out)).astype(BF16)
        grad_tokens = mm_tn(pack, deal(mm_tn(unpack, dx.astype(BF16)).astype(BF16))).astype(BF16)
        small = dp_sum((mm(n1_t[3], dkv_wide) + columns[0]).astype(BF16))
        small = small.astype(F32) + sum(
            z_move(small, move).astype(F32) for move in (near, far, across)
        )

        def z_block(x, m):
            return lax.dynamic_slice_in_dim(x, (z ^ m) * query_cols, query_cols, 1)

        both = [jnp.concatenate([z_block(sum_q, m), z_block(sum_o, m)], axis=1) for m in range(4)]
        total = both[0] + sum(
            z_move(part.astype(BF16), move).astype(F32)
            for part, move in zip(both[1:], (near, far, across))
        )
        sum_query, sum_out = total[:, :query_cols], total[:, query_cols:]
    sum_out = sum_out.T
    kv_cols = w_keyval.shape[1]
    return (
        outputs,
        grad_tokens,
        small[:, kv_cols],
        sum_query,
        small[:, :kv_cols],
        sum_out,
        small[:, kv_cols + 1],
        sum_gate,
        sum_up,
        sum_down,
    )


def solution(mesh):
    in_specs = (
        P(("dp", "tensor"), None),
        P("dp"),
        P("dp", None),
        P(("dp", "tensor"), None),
        P("dp", None),
        P(("dp", "tensor"), None),
        P(),
        P(None, "tensor"),
        P(),
        P("tensor", None),
        P(),
        P(None, None, "tensor"),
        P(None, None, "tensor"),
        P(None, "tensor", None),
    )
    out_specs = (
        P(("dp", "tensor"), None),
        P(("dp", "tensor"), None),
        P("dp"),
        P("dp", "tensor"),
        P("dp", None),
        P("tensor", "dp"),
        P("dp"),
        P(None, "dp", "tensor"),
        P(None, "dp", "tensor"),
        P(None, "tensor", "dp"),
    )
    return jax.shard_map(
        per_device, mesh=mesh, in_specs=in_specs, out_specs=out_specs, check_vma=False
    )
```

```python
import functools

import jax
import jax.numpy as jnp
from jax import lax
from jax.experimental import pallas as pl
from jax.experimental.layout import Layout, with_layout_constraint
from jax.experimental.pallas import tpu as pltpu
from jax.sharding import PartitionSpec as P

HD = 128
EPS = 1e-06
ROPE_BASE = 1000000.0
MASKED = -1e30
LOG2E = 1.4426950408889634
F32 = jnp.float32
BF16 = jnp.bfloat16
META = 128


def mm(a, b):
    return lax.dot_general(a, b, (((1,), (0,)), ((), ())), preferred_element_type=F32)


def mm_nt(a, b):
    return lax.dot_general(a, b, (((1,), (1,)), ((), ())), preferred_element_type=F32)


def mm_tn(a, b):
    return lax.dot_general(a, b, (((0,), (0,)), ((), ())), preferred_element_type=F32)


def params(mb=56):
    return pltpu.CompilerParams(vmem_limit_bytes=mb * 2**20)


def swap_halves(u):
    return pltpu.roll(u, HD // 2, 1)


def open_kernel(
    deal_ref,
    q_ref,
    o_ref,
    dealt_ref,
    q_all,
    o_all,
    send,
    recv,
    deal_send,
    deal_recv,
):
    z = lax.axis_index("tensor")
    d = lax.axis_index("dp")
    d_count = deal_ref.shape[0]
    z_count = q_all.shape[0]
    others = [{"tensor": flip(z, m)} for m in range(1, z_count)]
    peers = [{"dp": (d + p) % d_count} for p in range(1, d_count)]
    barrier = pltpu.get_barrier_semaphore()
    for other in others + peers:
        pl.semaphore_signal(barrier, inc=1, device_id=other, device_id_type=pl.DeviceIdType.MESH)
    pl.semaphore_wait(barrier, len(others) + len(peers))
    moves = [(q_ref, q_all.at[m], others[m - 1]) for m in range(1, z_count)]
    moves += [(o_ref, o_all.at[z], other) for other in others]
    copies = []
    for p, peer in enumerate(peers):
        copy = pltpu.make_async_remote_copy(
            src_ref=deal_ref.at[(d + p + 1) % d_count],
            dst_ref=dealt_ref.at[d],
            send_sem=deal_send.at[p],
            recv_sem=deal_recv.at[p],
            device_id=peer,
            device_id_type=pl.DeviceIdType.MESH,
        )
        copy.start()
        copies.append(copy)
    for at, (src, dst, to) in enumerate(moves):
        copy = pltpu.make_async_remote_copy(
            src_ref=src,
            dst_ref=dst,
            send_sem=send.at[at],
            recv_sem=recv.at[at],
            device_id=to,
            device_id_type=pl.DeviceIdType.MESH,
        )
        copy.start()
        copies.append(copy)
    dealt_ref[d] = deal_ref[d]
    q_all[0] = q_ref[...]
    o_all[z] = o_ref[...]
    for copy in copies:
        copy.wait()


def open_moves(deals, q, o, z_count):
    vmem = pl.BlockSpec(memory_space=pltpu.VMEM)
    shapes = [deals.shape, (z_count, *q.shape), (z_count, *o.shape)]
    moves = 2 * (z_count - 1)
    return pl.pallas_call(
        open_kernel,
        in_specs=[vmem] * 3,
        out_specs=[vmem] * 3,
        out_shape=[jax.ShapeDtypeStruct(shape, BF16) for shape in shapes],
        scratch_shapes=[
            pltpu.SemaphoreType.DMA((moves,)),
            pltpu.SemaphoreType.DMA((moves,)),
            pltpu.SemaphoreType.DMA((deals.shape[0] - 1,)),
            pltpu.SemaphoreType.DMA((deals.shape[0] - 1,)),
        ],
        compiler_params=pltpu.CompilerParams(
            vmem_limit_bytes=40 * 2**20, collective_id=4, has_side_effects=True
        ),
        name="open_moves",
    )(deals, q, o)


def keyval_kernel(
    x_ref,
    w_ref,
    cos_ref,
    sin_ref,
    count_ref,
    mark_ref,
    deal_ref,
    kv_ref,
    one_ref,
    two_ref,
    counts_ref,
    near_ref,
    dealt_ref,
    send,
    recv,
    deal_send,
    deal_recv,
):
    z = lax.axis_index("tensor")
    d = lax.axis_index("dp")
    d_count = deal_ref.shape[0]
    z_count = counts_ref.shape[0]
    others = [{"tensor": (z + m) % z_count} for m in range(1, z_count)]
    barrier = pltpu.get_barrier_semaphore()
    peers = [{"dp": (d + p) % d_count} for p in range(1, d_count)]
    for other in others + peers:
        pl.semaphore_signal(barrier, inc=1, device_id=other, device_id_type=pl.DeviceIdType.MESH)
    raw = mm(x_ref[...], w_ref[...])
    turned = raw.shape[1] // 2
    for i in range(turned // HD):
        u = raw[:, i * HD : (i + 1) * HD]
        u = u * cos_ref[...] + swap_halves(u) * sin_ref[...]
        kv_ref[:, i * HD : (i + 1) * HD] = u.astype(BF16)
    kv_ref[:, turned:] = raw[:, turned:].astype(BF16)
    pl.semaphore_wait(barrier, z_count - 1 + d_count - 1)
    moves = [(count_ref, counts_ref.at[m], others[m]) for m in range(z_count - 1)]
    moves += [(mark_ref, near_ref, {"tensor": flip(z, 1)})]
    moves += [(kv_ref, one_ref, others[0]), (one_ref, two_ref, others[0])]
    copies = []
    for at, (src, dst, to) in enumerate(moves):
        copy = pltpu.make_async_remote_copy(
            src_ref=src,
            dst_ref=dst,
            send_sem=send.at[at],
            recv_sem=recv.at[at],
            device_id=to,
            device_id_type=pl.DeviceIdType.MESH,
        )
        copies.append(copy)
    for copy in copies[:-1]:
        copy.start()
    for p, peer in enumerate(peers):
        copy = pltpu.make_async_remote_copy(
            src_ref=deal_ref.at[(d + p + 1) % d_count],
            dst_ref=dealt_ref.at[d],
            send_sem=deal_send.at[p],
            recv_sem=deal_recv.at[p],
            device_id=peer,
            device_id_type=pl.DeviceIdType.MESH,
        )
        copy.start()
        copies.append(copy)
    counts_ref[z_count - 1] = count_ref[...]
    dealt_ref[d] = deal_ref[d]
    step_one, step_two = copies[z_count], copies[z_count + 1]
    step_one.wait()
    step_two.start()
    for copy in copies[:z_count] + copies[z_count + 1 :]:
        copy.wait()


def keyval(x, w, cos_full, sin_full, counts, marks, deals, z_count):
    rows = x.shape[0]
    columns = w.shape[1]
    vmem = pl.BlockSpec(memory_space=pltpu.VMEM)
    block = jax.ShapeDtypeStruct((rows, columns), BF16)
    return pl.pallas_call(
        keyval_kernel,
        in_specs=[vmem] * 7,
        out_specs=[vmem] * 6,
        out_shape=[block] * 3
        + [
            jax.ShapeDtypeStruct((z_count, *counts.shape), counts.dtype),
            jax.ShapeDtypeStruct(marks.shape, marks.dtype),
            jax.ShapeDtypeStruct(deals.shape, deals.dtype),
        ],
        scratch_shapes=[
            pltpu.SemaphoreType.DMA((z_count + 2,)),
            pltpu.SemaphoreType.DMA((z_count + 2,)),
            pltpu.SemaphoreType.DMA((deals.shape[0] - 1,)),
            pltpu.SemaphoreType.DMA((deals.shape[0] - 1,)),
        ],
        compiler_params=pltpu.CompilerParams(
            vmem_limit_bytes=40 * 2**20, collective_id=1, has_side_effects=True
        ),
        name="keyval",
    )(x, w, cos_full, sin_full, counts, marks, deals)


def project_query_kernel(z_ref, x_ref, w_ref, cos_ref, sin_ref, out_ref):
    raw = mm(x_ref[...], w_ref[...].reshape(x_ref.shape[1], out_ref.shape[1]))
    for i in range(raw.shape[1] // HD):
        u = raw[:, i * HD : (i + 1) * HD]
        turned = u * cos_ref[...] + swap_halves(u) * sin_ref[...]
        out_ref[:, i * HD : (i + 1) * HD] = (turned * SCALE).astype(BF16)


def project_query(z, x, w, cos_full, sin_full):
    rows, width = x.shape
    pieces, blocks, piece, columns = w.shape
    return pl.pallas_call(
        project_query_kernel,
        grid_spec=pltpu.PrefetchScalarGridSpec(
            num_scalar_prefetch=1,
            grid=(blocks,),
            in_specs=[
                pl.BlockSpec((rows, width), lambda i, s: (0, 0)),
                pl.BlockSpec(
                    (pieces, 1, piece, columns), lambda i, s: (0, jnp.bitwise_xor(i, s[0]), 0, 0)
                ),
                pl.BlockSpec((rows, HD), lambda i, s: (0, 0)),
                pl.BlockSpec((rows, HD), lambda i, s: (0, 0)),
            ],
            out_specs=pl.BlockSpec((rows, columns), lambda i, s: (0, i)),
        ),
        out_shape=jax.ShapeDtypeStruct((rows, blocks * columns), BF16),
        compiler_params=params(),
        name="project_query",
        cost_estimate=pl.CostEstimate(
            flops=2 * rows * width * blocks * columns,
            bytes_accessed=2 * (2 * rows * width + width * blocks * columns),
            transcendentals=0,
        ),
    )(z, x, w, cos_full, sin_full)


def project_back_kernel(z_ref, dq_ref, w_ref, dkv_ref, wkv_ref, out_ref):
    step = pl.program_id(0)
    width = out_ref.shape[1]
    part = mm_nt(dq_ref[...], w_ref[...].reshape(width, dq_ref.shape[1]))

    @pl.when(step == 0)
    def _():
        out_ref[...] = part + mm_nt(dkv_ref[...], wkv_ref[...])

    @pl.when(step > 0)
    def _():
        out_ref[...] += part


def project_back(z, dq, w, dkv, wkv):
    rows = dq.shape[0]
    pieces, blocks, piece, columns = w.shape
    width = pieces * piece
    return pl.pallas_call(
        project_back_kernel,
        grid_spec=pltpu.PrefetchScalarGridSpec(
            num_scalar_prefetch=1,
            grid=(blocks,),
            in_specs=[
                pl.BlockSpec((rows, columns), lambda i, s: (0, i)),
                pl.BlockSpec(
                    (pieces, 1, piece, columns), lambda i, s: (0, jnp.bitwise_xor(i, s[0]), 0, 0)
                ),
                pl.BlockSpec(dkv.shape, lambda i, s: (0, 0)),
                pl.BlockSpec(wkv.shape, lambda i, s: (0, 0)),
            ],
            out_specs=pl.BlockSpec((rows, width), lambda i, s: (0, 0)),
        ),
        out_shape=jax.ShapeDtypeStruct((rows, width), F32),
        compiler_params=params(),
        name="project_back",
        cost_estimate=pl.CostEstimate(
            flops=2 * rows * width * (blocks * columns + dkv.shape[1]),
            bytes_accessed=2 * width * (3 * rows + blocks * columns),
            transcendentals=0,
        ),
    )(z, dq, w, dkv, wkv)


ATTEND_TILE = 256
SCALE = HD**-0.5 * LOG2E


def make_bias(z, start_ref, bias_ref):
    tiles, tile, width = bias_ref.shape
    rows = tiles * tile
    for i in range(tiles):
        key = (z - 2) * rows + i * tile + lax.broadcasted_iota(jnp.int32, (tile, width), 1)
        query = z * rows + i * tile + lax.broadcasted_iota(jnp.int32, (tile, width), 0)
        allowed = (key >= start_ref[i * tile : (i + 1) * tile]) & (key <= query)
        bias_ref[i] = jnp.where(allowed, 0.0, MASKED)


def attend_kernel(
    kv_heads, z_ref, start_ref, q_ref, kv0_ref, kv1_ref, kv2_ref, o_ref, lse_ref, bias_ref, k_ref, v_ref
):
    head = pl.program_id(0)
    each = pl.num_programs(0) // kv_heads
    rows = q_ref.shape[0]
    tiles, tile, width = bias_ref.shape

    @pl.when(head == 0)
    def _():
        make_bias(z_ref[0], start_ref, bias_ref)
        v_ref[:, HD:] = jnp.ones((v_ref.shape[0], HD), BF16)

    @pl.when(head % each == 0)
    def _():
        kvh = head // each
        for j, ref in enumerate((kv0_ref, kv1_ref, kv2_ref)):
            at = slice(j * rows, (j + 1) * rows)
            k_ref[at] = ref[:, pl.ds(pl.multiple_of(kvh * HD, HD), HD)]
            v_ref[at, :HD] = ref[:, pl.ds(pl.multiple_of((kv_heads + kvh) * HD, HD), HD)]

    for i in range(tiles):
        at, window = slice(i * tile, (i + 1) * tile), slice(i * tile, i * tile + width)
        score = mm_nt(q_ref[at], k_ref[window]) + bias_ref[i]
        peak = jnp.max(score, axis=1, keepdims=True)
        mixed = mm(jnp.exp2(score - peak).astype(BF16), v_ref[window])
        total = mixed[:, HD : HD + 1]
        o_ref[at] = (mixed[:, :HD] / total).astype(BF16)
        lse_ref[0, at] = peak + jnp.log2(total)


def attend(z, start, q, kvs, kv_heads):
    rows, columns = q.shape
    heads = columns // HD
    tile = ATTEND_TILE
    kv_spec = pl.BlockSpec(kvs[0].shape, lambda h, s: (0, 0))
    return pl.pallas_call(
        functools.partial(attend_kernel, kv_heads),
        grid_spec=pltpu.PrefetchScalarGridSpec(
            num_scalar_prefetch=1,
            grid=(heads,),
            in_specs=[
                pl.BlockSpec((rows, 1), lambda h, s: (0, 0)),
                pl.BlockSpec((rows, HD), lambda h, s: (0, h)),
                *[kv_spec] * 3,
            ],
            out_specs=[
                pl.BlockSpec((rows, HD), lambda h, s: (0, h)),
                pl.BlockSpec((1, rows, 1), lambda h, s: (h, 0, 0)),
            ],
            scratch_shapes=[
                pltpu.VMEM((rows // tile, tile, 2 * rows + tile), F32),
                pltpu.VMEM((3 * rows, HD), BF16),
                pltpu.VMEM((3 * rows, 2 * HD), BF16),
            ],
        ),
        out_shape=[
            jax.ShapeDtypeStruct((rows, columns), BF16),
            jax.ShapeDtypeStruct((heads, rows, 1), F32),
        ],
        compiler_params=params(),
        name="attend",
        cost_estimate=pl.CostEstimate(
            flops=12 * rows * rows * columns,
            bytes_accessed=8 * rows * columns,
            transcendentals=rows * rows * 3 * heads,
        ),
    )(z, start, q, *kvs)


def attend_back_kernel(
    kv_heads,
    z_ref,
    start_ref,
    q_ref,
    o_ref,
    do_ref,
    lse_ref,
    cos_ref,
    sin_ref,
    kv0_ref,
    kv1_ref,
    kv2_ref,
    dq_ref,
    d0_ref,
    d1_ref,
    d2_ref,
    bias_ref,
    k_ref,
    v_ref,
    dk_ref,
    dv_ref,
):
    head = pl.program_id(0)
    each = pl.num_programs(0) // kv_heads
    rows = q_ref.shape[0]
    tiles, tile, width = bias_ref.shape
    kvh = head // each
    kcol = pl.ds(pl.multiple_of(kvh * HD, HD), HD)
    vcol = pl.ds(pl.multiple_of((kv_heads + kvh) * HD, HD), HD)

    @pl.when(head == 0)
    def _():
        make_bias(z_ref[0], start_ref, bias_ref)

    @pl.when(head % each == 0)
    def _():
        for j, ref in enumerate((kv0_ref, kv1_ref, kv2_ref)):
            k_ref[j * rows : (j + 1) * rows] = ref[:, kcol]
            v_ref[j * rows : (j + 1) * rows] = ref[:, vcol]
        dk_ref[...] = jnp.zeros_like(dk_ref)
        dv_ref[...] = jnp.zeros_like(dv_ref)

    for i in range(tiles):
        at, window = slice(i * tile, (i + 1) * tile), slice(i * tile, i * tile + width)
        q = q_ref[at]
        do = do_ref[at]
        centre = jnp.sum(do.astype(F32) * o_ref[at].astype(F32), axis=1, keepdims=True)
        soft = jnp.exp2(mm_nt(q, k_ref[window]) + (bias_ref[i] - lse_ref[0, at]))
        dv_ref[window] += mm_tn(soft.astype(BF16), do)
        dscore = (soft * (mm_nt(do, v_ref[window]) - centre)).astype(BF16)
        dk_ref[window] += mm_tn(dscore, q)
        dq = mm(dscore, k_ref[window]) * (HD**-0.5)
        dq_ref[at] = (dq * cos_ref[at] - swap_halves(dq) * sin_ref[at]).astype(BF16)

    @pl.when(head % each == each - 1)
    def _():
        for j, ref in enumerate((d0_ref, d1_ref, d2_ref)):
            at = slice(j * rows, (j + 1) * rows)
            ref[:, kcol] = (dk_ref[at] * (1 / LOG2E)).astype(ref.dtype)
            ref[:, vcol] = dv_ref[at].astype(ref.dtype)


def attend_back(z, start, q, o, do, lse, cos_full, sin_full, kvs, kv_heads):
    rows, columns = q.shape
    heads = columns // HD
    tile = ATTEND_TILE
    kv_columns = kvs[0].shape[1]
    kv_spec = pl.BlockSpec((rows, kv_columns), lambda h, s: (0, 0))
    head_spec = pl.BlockSpec((rows, HD), lambda h, s: (0, h))
    table_spec = pl.BlockSpec((rows, HD), lambda h, s: (0, 0))
    return pl.pallas_call(
        functools.partial(attend_back_kernel, kv_heads),
        grid_spec=pltpu.PrefetchScalarGridSpec(
            num_scalar_prefetch=1,
            grid=(heads,),
            in_specs=[
                pl.BlockSpec((rows, 1), lambda h, s: (0, 0)),
                head_spec,
                head_spec,
                head_spec,
                pl.BlockSpec((1, rows, 1), lambda h, s: (h, 0, 0)),
                table_spec,
                table_spec,
                *[kv_spec] * 3,
            ],
            out_specs=[head_spec, *[kv_spec] * 3],
            scratch_shapes=[
                pltpu.VMEM((rows // tile, tile, 2 * rows + tile), F32),
                pltpu.VMEM((3 * rows, HD), BF16),
                pltpu.VMEM((3 * rows, HD), BF16),
                pltpu.VMEM((3 * rows, HD), F32),
                pltpu.VMEM((3 * rows, HD), F32),
            ],
        ),
        out_shape=[
            jax.ShapeDtypeStruct((rows, columns), BF16),
            jax.ShapeDtypeStruct((rows, kv_columns), BF16),
            jax.ShapeDtypeStruct((rows, kv_columns), BF16),
            jax.ShapeDtypeStruct((rows, kv_columns), F32),
        ],
        compiler_params=params(),
        name="attend_back",
        cost_estimate=pl.CostEstimate(
            flops=30 * rows * rows * columns,
            bytes_accessed=12 * rows * columns,
            transcendentals=rows * rows * 3 * heads,
        ),
    )(z, start, q, o, do, lse, cos_full, sin_full, *kvs)


def expert_kernel(chunk, first, last, x_ref, dy_ref, gate_ref, wg_ref, wu_ref, wd_ref, *refs):
    if last:
        y_out, dn_out, hs_ref, dgu_ref, y_ref, dn_ref = refs[-6:]
    else:
        y_ref, dn_ref, hs_ref, dgu_ref = refs[-4:]
    step = pl.program_id(0)

    @pl.when(step == 0)
    def _():
        if first:
            y_ref[...] = jnp.zeros_like(y_ref)
            dn_ref[...] = jnp.zeros_like(dn_ref)
        else:
            y_ref[...] = refs[0][...]
            dn_ref[...] = refs[1][...]

    x = x_ref[...]
    gate = gate_ref[...].astype(F32)
    g = jnp.maximum(mm_nt(x, wg_ref[...]), 0.0)
    u = mm_nt(x, wu_ref[...])
    square = g * g
    hs = ((square * u).astype(BF16).astype(F32) * gate).astype(BF16)
    hs_ref[...] = hs
    dh = mm_nt(dy_ref[...], wd_ref[...]) * gate
    dg = (dh * u * (2.0 * g)).astype(BF16)
    du = (dh * square).astype(BF16)
    dgu_ref[:, :chunk] = dg
    dgu_ref[:, chunk:] = du
    dn_ref[...] += mm(dg, wg_ref[...]) + mm(du, wu_ref[...])
    y_ref[...] += mm(hs, wd_ref[...])
    if last:

        @pl.when(step == pl.num_programs(0) - 1)
        def _():
            y_out[...] = y_ref[...].astype(BF16)
            dn_out[...] = dn_ref[...].astype(BF16)


def experts(tile, x, dy, gate, wg, wu, wd, before=None, filled=None, last=False, chunk=512):
    rows, width = x.shape
    hidden = gate.shape[1]
    full = pl.BlockSpec((rows, width), lambda i: (0, 0))
    part = pl.BlockSpec((rows, chunk), lambda i: (0, i))
    operands = [x, dy, gate, wg, wu, wd]
    in_specs = [
        full,
        full,
        part,
        *[pl.BlockSpec((chunk, width), lambda i: (i, 0))] * 3,
    ]
    aliases = {}
    if before is not None:
        operands += list(before)
        in_specs += [full] * 2
    if filled is not None:
        aliases = {len(operands): 2, len(operands) + 1: 3}
        operands += list(filled)
        in_specs += [pl.BlockSpec(memory_space=pl.ANY)] * 2
    return pl.pallas_call(
        functools.partial(expert_kernel, chunk, before is None, last),
        grid=(hidden // chunk,),
        in_specs=in_specs,
        out_specs=[
            full,
            full,
            pl.BlockSpec((rows, chunk), lambda i: (tile, i)),
            pl.BlockSpec((rows, 2 * chunk), lambda i: (tile, i)),
        ],
        out_shape=[
            *[jax.ShapeDtypeStruct((rows, width), BF16 if last else F32)] * 2,
            jax.ShapeDtypeStruct((2 * rows, hidden), BF16),
            jax.ShapeDtypeStruct((2 * rows, 2 * hidden), BF16),
        ],
        scratch_shapes=[pltpu.VMEM((rows, width), F32)] * (2 if last else 0),
        input_output_aliases=aliases,
        compiler_params=params(),
        name="experts",
        cost_estimate=pl.CostEstimate(
            flops=12 * rows * width * hidden,
            bytes_accessed=6 * width * hidden + 16 * rows * width,
            transcendentals=0,
        ),
    )(*operands)


def pick(i, values):
    result = values[0]
    for at, value in enumerate(values):
        if at and value != values[at - 1]:
            result = jnp.where(i >= at, value, result)
    return result


def gradient_kernel(jobs, lefts, rights, *refs):
    send_refs, keep_refs, right_refs = refs[:lefts], refs[lefts : 2 * lefts], refs[2 * lefts :]
    outs, (sent, got, send, recv) = right_refs[rights:-4], refs[-4:]
    d = lax.axis_index("dp")
    step = pl.program_id(0)
    count = len(jobs)

    @pl.when(step == 0)
    def _():
        barrier = pltpu.get_barrier_semaphore()
        pl.semaphore_signal(
            barrier, inc=1, device_id={"dp": flip(d, 1)}, device_id_type=pl.DeviceIdType.MESH
        )
        pl.semaphore_wait(barrier, 1)

    def copy(i):
        return pltpu.make_async_remote_copy(
            src_ref=sent.at[i],
            dst_ref=got.at[i],
            send_sem=send.at[i],
            recv_sem=recv.at[i],
            device_id={"dp": flip(d, 1)},
            device_id_type=pl.DeviceIdType.MESH,
        )

    for i, (left, right, _) in enumerate(jobs):

        @pl.when(step == i)
        def _(i=i, left=left, right=right):
            sent[i] = mm(send_refs[left][...], right_refs[right][...]).astype(BF16)
            copy(i).start()

        @pl.when(step == count + i)
        def _(i=i, left=left, right=right):
            value = mm(keep_refs[left][...], right_refs[right][...])
            copy(i).wait()
            value = value + got[i].astype(F32)
            half = value.shape[0] // 2
            side = 2 * (i // (count // 2))
            outs[side][...] = value[:half].astype(BF16)
            outs[side + 1][...] = value[half:].astype(BF16)


def gradients(jobs, send_lefts, keep_lefts, rights, ident, chunk=768):
    rows, tokens = keep_lefts[0].shape
    count = len(jobs)
    each = count // 2
    first = lambda i: (0, jnp.clip(i - count, 0, each - 1))
    second = lambda i: (0, jnp.maximum(i - count - each, 0))
    right_specs = []
    for r in range(len(rights)):
        blocks, at = [], None
        for _, right, block in jobs + jobs:
            at = block if right == r else at
            blocks.append(at)
        known = next(block for block in blocks if block is not None)
        blocks = tuple(known if block is None else block for block in blocks)
        right_specs.append(
            pl.BlockSpec((tokens, chunk), lambda i, blocks=blocks: (0, pick(i, blocks)))
        )
    left = pl.BlockSpec((rows, tokens), lambda i: (0, 0), pipeline_mode=pl.Buffered(1))
    return pl.pallas_call(
        functools.partial(gradient_kernel, jobs, len(keep_lefts), len(rights)),
        grid=(2 * count,),
        in_specs=[*[left] * (2 * len(keep_lefts)), *right_specs],
        out_specs=[
            pl.BlockSpec((rows // 2, chunk), at) for at in (first, first, second, second)
        ],
        out_shape=[jax.ShapeDtypeStruct((rows // 2, each * chunk), BF16)] * 4,
        scratch_shapes=[
            pltpu.VMEM((count, rows, chunk), BF16),
            pltpu.VMEM((count, rows, chunk), BF16),
            pltpu.SemaphoreType.DMA((count,)),
            pltpu.SemaphoreType.DMA((count,)),
        ],
        compiler_params=pltpu.CompilerParams(
            vmem_limit_bytes=56 * 2**20, collective_id=ident, has_side_effects=True
        ),
        name="gradients",
        cost_estimate=pl.CostEstimate(flops=10**9, bytes_accessed=10**6, transcendentals=0),
    )(*send_lefts, *keep_lefts, *rights)


def part_kernel(jobs, lefts, rights, keep, *refs):
    left_refs, right_refs, rest = refs[:lefts], refs[lefts : lefts + rights], refs[lefts + rights :]
    step = pl.program_id(0)
    each = len(jobs) // 2
    for i, (left, right, _) in enumerate(jobs):

        @pl.when(step == i)
        def _(i=i, left=left, right=right):
            side = i // each
            value = mm(left_refs[left][...], right_refs[right][...])
            if keep:
                value = value + rest[0][0].astype(F32)
                half = value.shape[0] // 2
                rest[1 + 2 * side][...] = value[:half].astype(BF16)
                rest[2 + 2 * side][...] = value[half:].astype(BF16)
            else:
                rest[0][0] = value.astype(BF16)


def gradient_parts(jobs, lefts, rights, got=None, chunk=768):
    rows, tokens = lefts[0].shape
    each = len(jobs) // 2
    first = lambda i: (0, jnp.minimum(i, each - 1))
    second = lambda i: (0, jnp.maximum(i - each, 0))
    whole = [pl.BlockSpec((1, rows, chunk), lambda i: (i // each, 0, i % each))]
    if got is None:
        out_specs = whole[0]
        out_shape = jax.ShapeDtypeStruct((2, rows, each * chunk), BF16)
    else:
        out_specs = [pl.BlockSpec((rows // 2, chunk), at) for at in (first, first, second, second)]
        out_shape = [jax.ShapeDtypeStruct((rows // 2, each * chunk), BF16)] * 4
    right_specs = []
    for r in range(len(rights)):
        at, blocks = None, []
        for _, right, block in jobs:
            at = block if right == r else at
            blocks.append(at)
        known = next(block for block in blocks if block is not None)
        blocks = tuple(known if block is None else block for block in blocks)
        right_specs.append(
            pl.BlockSpec((tokens, chunk), lambda i, blocks=blocks: (0, pick(i, blocks)))
        )
    return pl.pallas_call(
        functools.partial(part_kernel, jobs, len(lefts), len(rights), got is not None),
        grid=(2 * each,),
        in_specs=[
            *[pl.BlockSpec((rows, tokens), lambda i: (0, 0))] * len(lefts),
            *right_specs,
            *(() if got is None else whole),
        ],
        out_specs=out_specs,
        out_shape=out_shape,
        compiler_params=params(),
        name="gradient_parts",
        cost_estimate=pl.CostEstimate(
            flops=4 * each * rows * tokens * chunk,
            bytes_accessed=4 * each * (rows + tokens) * chunk,
            transcendentals=0,
        ),
    )(*lefts, *rights, *(() if got is None else (got,)))


EXPERT_JOBS = ((0, 0, 0), (0, 0, 1), (1, 1, 0), (2, 0, 2), (2, 0, 3), (3, 1, 1))


def flip(index, mask):
    for bit in (1, 2, 4):
        if mask & bit:
            index = index + bit - 2 * bit * (index // bit % 2)
    return index


def mix_kernel(
    dq_ref,
    o_ref,
    n_send,
    n_keep,
    d_send,
    d_keep,
    one_ref,
    two_ref,
    fa_keep,
    fa_got,
    fb_keep,
    fb_got,
    q_keep,
    q_send,
    o_keep,
    o_send,
    got_one,
    far_ref,
    got_two,
    both_ref,
    sent,
    got,
    halves,
    lasts,
    send,
    recv,
):
    d = lax.axis_index("dp")
    z = lax.axis_index("tensor")
    z_count = lax.axis_size("tensor")
    pairs = [{"dp": flip(d, bit)} for bit in (1, 2, 4)]
    others = [{"tensor": (z + m) % z_count} for m in range(1, z_count)]
    barrier = pltpu.get_barrier_semaphore()
    for peer in pairs + others:
        pl.semaphore_signal(barrier, inc=1, device_id=peer, device_id_type=pl.DeviceIdType.MESH)
    pl.semaphore_wait(barrier, len(pairs) + len(others))

    def start(src, dst, at, to):
        copy = pltpu.make_async_remote_copy(
            src_ref=src,
            dst_ref=dst,
            send_sem=send.at[at],
            recv_sem=recv.at[at],
            device_id=to,
            device_id_type=pl.DeviceIdType.MESH,
        )
        copy.start()
        return copy

    step_two = start(two_ref, got_two, 1, others[-1])
    rows = halves.shape[1]
    far_copies = []
    for side, (keep, arrived) in enumerate(((fa_keep, fa_got), (fb_keep, fb_got))):
        total = keep[rows:].astype(F32) + arrived[rows:].astype(F32)
        halves[side] = total.astype(BF16)
        far_copies.append(start(halves.at[side], lasts.at[side], 2 + side, pairs[2 - side]))

    columns = dq_ref.shape[1]
    chunk = columns // 4

    def at_chunk(i):
        return pl.ds(pl.multiple_of(i * chunk, chunk), chunk)

    sides = ((dq_ref, n_send, n_keep, q_keep, q_send), (o_ref, d_send, d_keep, o_keep, o_send))
    core_copies = []
    for side, (right, left, _, _, _) in enumerate(sides):

        def compute_send(i, carry, side=side, right=right, left=left):
            at = at_chunk(i)
            sent[side, :, at] = mm(left[...], right[:, at]).astype(BF16)
            return carry

        lax.fori_loop(0, 4, compute_send, 0)
        core_copies.append(start(sent.at[side], got.at[side], 4 + side, pairs[0]))
        if side == 0:
            step_two.wait()
            both_ref[...] = (one_ref[...].astype(F32) + got_two[...].astype(F32)).astype(BF16)
            step_one = start(both_ref, got_one, 0, others[-1])
    for side, (right, _, left, keep, away) in enumerate(sides):
        core_copies[side].wait()

        def compute_keep(i, carry, side=side, right=right, left=left, keep=keep, away=away):
            at = at_chunk(i)
            value = mm(left[...], right[:, at]) + got[side, :, at].astype(F32)
            half = value.shape[0] // 2
            keep[:, at] = value[:half].astype(BF16)
            away[:, at] = value[half:].astype(BF16)
            return carry

        lax.fori_loop(0, 4, compute_keep, 0)
    for side, (keep, arrived) in enumerate(((fa_keep, fa_got), (fb_keep, fb_got))):
        far_copies[side].wait()
        total = keep[:rows].astype(F32) + arrived[:rows].astype(F32) + lasts[side].astype(F32)
        far_ref[side] = total.astype(BF16)
    step_one.wait()


def mix(dq, o, lefts, dkv_one, dkv_two, far_parts):
    rows2, columns = far_parts[0].shape
    rows = rows2 // 2
    wide = dq.shape[1]
    vmem = pl.BlockSpec(memory_space=pltpu.VMEM)
    half = jax.ShapeDtypeStruct((rows2, wide), BF16)
    block = jax.ShapeDtypeStruct(dkv_one.shape, BF16)
    return pl.pallas_call(
        mix_kernel,
        in_specs=[vmem] * 12,
        out_specs=[vmem] * 6,
        out_shape=[half] * 4 + [block] + [jax.ShapeDtypeStruct((2, rows, columns), BF16)],
        scratch_shapes=[
            pltpu.VMEM(block.shape, BF16),
            pltpu.VMEM(block.shape, BF16),
            pltpu.VMEM((2, 2 * rows2, wide), BF16),
            pltpu.VMEM((2, 2 * rows2, wide), BF16),
            pltpu.VMEM((2, rows, columns), BF16),
            pltpu.VMEM((2, rows, columns), BF16),
            pltpu.SemaphoreType.DMA((6,)),
            pltpu.SemaphoreType.DMA((6,)),
        ],
        compiler_params=pltpu.CompilerParams(
            vmem_limit_bytes=56 * 2**20, collective_id=2, has_side_effects=True
        ),
        name="mix",
    )(dq, o, *lefts, dkv_one, dkv_two, *far_parts)


def finish_kernel(
    dx_ref,
    out_ref,
    q_keep,
    q_send,
    o_keep,
    o_send,
    s_send,
    s_keep,
    back_ref,
    back_out_ref,
    q_ref,
    o_ref,
    s_ref,
    q_got,
    o_got,
    q_half,
    o_half,
    q_last,
    o_last,
    s_got,
    s_half,
    s_got2,
    s_quarter,
    s_last,
    z_mine,
    z_got,
    k_mine,
    k_half,
    k_got,
    deal_send,
    deal_recv,
    send,
    recv,
):
    d = lax.axis_index("dp")
    z = lax.axis_index("tensor")
    count = dx_ref.shape[0]
    z_count = z_mine.shape[0]
    barrier = pltpu.get_barrier_semaphore()
    for p in range(1, count):
        pl.semaphore_signal(
            barrier, inc=1, device_id={"dp": flip(d, p)}, device_id_type=pl.DeviceIdType.MESH
        )
    for m in range(1, z_count):
        pl.semaphore_signal(
            barrier, inc=1, device_id={"tensor": flip(z, m)}, device_id_type=pl.DeviceIdType.MESH
        )
    pl.semaphore_wait(barrier, count - 1 + z_count - 1)

    def start(src, dst, at, to):
        copy = pltpu.make_async_remote_copy(
            src_ref=src,
            dst_ref=dst,
            send_sem=send.at[at],
            recv_sem=recv.at[at],
            device_id=to,
            device_id_type=pl.DeviceIdType.MESH,
        )
        copy.start()
        return copy

    one, two, four = [{"dp": flip(d, bit)} for bit in (1, 2, 4)]
    q_one = start(q_send, q_got, 1, two)
    o_one = start(o_send, o_got, 2, four)
    s_one = start(s_send, s_got, 0, one)
    back_ref[d] = dx_ref[d]
    back_out_ref[d] = out_ref[d]
    rows = q_last.shape[0]
    s_one.wait()
    total = s_keep[...].astype(F32) + s_got[...].astype(F32)
    s_keep2 = total[: 2 * rows]
    s_half[...] = total[2 * rows :].astype(BF16)
    s_two = start(s_half, s_got2, 3, four)
    q_one.wait()
    q_half[...] = (q_keep[rows:].astype(F32) + q_got[rows:].astype(F32)).astype(BF16)
    q_two = start(q_half, q_last, 4, four)
    o_one.wait()
    o_half[...] = (o_keep[rows:].astype(F32) + o_got[rows:].astype(F32)).astype(BF16)
    o_two = start(o_half, o_last, 5, two)
    s_two.wait()
    total = s_keep2 + s_got2[...].astype(F32)
    s_quarter[...] = total[rows:].astype(BF16)
    s_three = start(s_quarter, s_last, 6, two)
    deals = []
    for i, (src, dst) in enumerate(((dx_ref, back_ref), (out_ref, back_out_ref))):
        for p in range(1, count):
            copy = pltpu.make_async_remote_copy(
                src_ref=src.at[flip(d, p)],
                dst_ref=dst.at[d],
                send_sem=deal_send.at[i, p - 1],
                recv_sem=deal_recv.at[i, p - 1],
                device_id={"dp": flip(d, p)},
                device_id_type=pl.DeviceIdType.MESH,
            )
            copy.start()
            deals.append(copy)
    s_own = total[:rows]
    s_three.wait()
    s_own = s_own + s_last[...].astype(F32)
    k_mine[...] = s_own.astype(BF16)
    k_near = start(k_mine, k_got.at[0], 7, {"tensor": flip(z, 1)})
    finals = []
    part = q_ref.shape[1]
    for two_copy, keep, got, last, side in (
        (q_two, q_keep, q_got, q_last, 0),
        (o_two, o_keep, o_got, o_last, 1),
    ):
        two_copy.wait()
        total = (
            keep[:rows].astype(F32) + got[:rows].astype(F32) + last[...].astype(F32)
        )
        for i in range(z_count):
            block = total[:, i * part : (i + 1) * part]
            z_mine[i, :, side * part : (side + 1) * part] = block.astype(BF16)
    for m in range(1, z_count):
        finals.append(start(z_mine.at[flip(z, m)], z_got.at[m - 1], 8 + m, {"tensor": flip(z, m)}))
    k_near.wait()
    s_own = s_own + k_got[0].astype(F32)
    k_half[...] = s_own.astype(BF16)
    k_far = start(k_half, k_got.at[1], 8, {"tensor": flip(z, 2)})
    for copy in finals:
        copy.wait()
    total = z_mine[z].astype(F32)
    for m in range(z_count - 1):
        total = total + z_got[m].astype(F32)
    q_ref[...] = total[:, :part]
    o_ref[...] = total[:, part:]
    k_far.wait()
    s_ref[...] = s_own + k_got[1].astype(F32)
    for copy in deals:
        copy.wait()


def finish(dx, out, q_keep, q_send, o_keep, o_send, s_send, s_keep, z_count):
    count = dx.shape[0]
    rows = q_keep.shape[0] // 2
    columns = q_keep.shape[1]
    small = s_keep.shape[1]
    part = columns // z_count
    vmem = pl.BlockSpec(memory_space=pltpu.VMEM)
    dma = pltpu.SemaphoreType.DMA
    return pl.pallas_call(
        finish_kernel,
        in_specs=[vmem] * 8,
        out_specs=[vmem] * 5,
        out_shape=[
            jax.ShapeDtypeStruct(dx.shape, BF16),
            jax.ShapeDtypeStruct(dx.shape, BF16),
            jax.ShapeDtypeStruct((rows, part), F32),
            jax.ShapeDtypeStruct((rows, part), F32),
            jax.ShapeDtypeStruct((rows, small), F32),
        ],
        scratch_shapes=[
            pltpu.VMEM((2 * rows, columns), BF16),
            pltpu.VMEM((2 * rows, columns), BF16),
            pltpu.VMEM((rows, columns), BF16),
            pltpu.VMEM((rows, columns), BF16),
            pltpu.VMEM((rows, columns), BF16),
            pltpu.VMEM((rows, columns), BF16),
            pltpu.VMEM((4 * rows, small), BF16),
            pltpu.VMEM((2 * rows, small), BF16),
            pltpu.VMEM((2 * rows, small), BF16),
            pltpu.VMEM((rows, small), BF16),
            pltpu.VMEM((rows, small), BF16),
            pltpu.VMEM((z_count, rows, 2 * part), BF16),
            pltpu.VMEM((z_count - 1, rows, 2 * part), BF16),
            pltpu.VMEM((rows, small), BF16),
            pltpu.VMEM((rows, small), BF16),
            pltpu.VMEM((2, rows, small), BF16),
            dma((2, count - 1)),
            dma((2, count - 1)),
            dma((7 + 2 * z_count,)),
            dma((7 + 2 * z_count,)),
        ],
        compiler_params=pltpu.CompilerParams(
            vmem_limit_bytes=56 * 2**20, collective_id=0, has_side_effects=True
        ),
        name="finish",
    )(dx, out, q_keep, q_send, o_keep, o_send, s_send, s_keep)


def assemble_kernel(a_keep, a_got, b_keep, b_got, far_ref, gate_ref, up_ref, down_ref):
    count, rows, columns = gate_ref.shape
    a = a_keep[...] + a_got[...].astype(F32) + far_ref[0].astype(F32)
    b = b_keep[...] + b_got[...].astype(F32) + far_ref[1].astype(F32)
    gate = jnp.concatenate([a[:, :512], a[:, 1024:1536], b[:, 512:1024]], axis=1)
    up = jnp.concatenate([a[:, 512:1024], b[:, :512], b[:, 1024:1536]], axis=1)
    down = jnp.concatenate([a[:, 1536:], b[:, 1536:]], axis=1)
    pad = jnp.zeros((256 - rows, down.shape[1]), F32)
    down = jnp.concatenate([down, pad], axis=0).T[:, :rows]
    for e in range(count):
        at = slice(e * columns, (e + 1) * columns)
        gate_ref[e] = gate[:, at]
        up_ref[e] = up[:, at]
        down_ref[e] = down[at]


def assemble(own, far_sum, count):
    rows, columns = own[0].shape
    part = columns * 2 // (3 * count)
    vmem = pl.BlockSpec(memory_space=pltpu.VMEM)
    wide = jax.ShapeDtypeStruct((count, rows, part), F32)
    return pl.pallas_call(
        assemble_kernel,
        in_specs=[vmem] * 5,
        out_specs=[vmem] * 3,
        out_shape=[wide, wide, jax.ShapeDtypeStruct((count, part, rows), F32)],
        compiler_params=params(),
        name="assemble",
    )(*own, far_sum)


def turn_kernel(orders, d_ref, *refs):
    tiles = len(refs) - 1 - len(orders)
    scratch_ref = refs[-1]
    step = pl.program_id(0)
    for t in range(tiles):

        @pl.when(step == t)
        def _(t=t):
            scratch_ref[...] = refs[t][...].T

    for order, out_ref in zip(orders, refs[tiles:-1]):
        size = out_ref.shape[0] // len(order)
        for i, p in enumerate(order):
            block = jnp.bitwise_xor(d_ref[0], p)
            at = pl.multiple_of(block * size, size)
            out_ref[i * size : (i + 1) * size, :] = scratch_ref[pl.ds(at, size), :]


def turn(d, tiles, orders, blocks):
    rows, width = tiles[0].shape
    size = width // blocks
    return pl.pallas_call(
        functools.partial(turn_kernel, orders),
        grid_spec=pltpu.PrefetchScalarGridSpec(
            num_scalar_prefetch=1,
            grid=(len(tiles),),
            in_specs=[pl.BlockSpec((rows, width), lambda t, s: (0, 0))] * len(tiles),
            out_specs=[
                pl.BlockSpec((len(order) * size, rows), lambda t, s: (0, t)) for order in orders
            ],
            scratch_shapes=[pltpu.VMEM((width, rows), BF16)],
        ),
        out_shape=[
            jax.ShapeDtypeStruct((len(order) * size, rows * len(tiles)), BF16) for order in orders
        ],
        compiler_params=params(),
        name="turn",
        cost_estimate=pl.CostEstimate(
            flops=0, bytes_accessed=6 * rows * width * len(tiles), transcendentals=0
        ),
    )(d, *tiles)


def tie(*values):
    return lax.optimization_barrier(values)


def row_major(x):
    return with_layout_constraint(x, Layout(major_to_minor=tuple(range(x.ndim))))


def per_device(
    tokens,
    perm,
    routes,
    gates,
    lengths,
    cotangent,
    gain_attn,
    w_query,
    w_keyval,
    w_out,
    gain_moe,
    w_gate,
    w_up,
    w_down,
):
    dp_count = lax.axis_size("dp")
    tensor_count = lax.axis_size("tensor")
    d = lax.axis_index("dp")
    z = lax.axis_index("tensor")
    rows, width = tokens.shape
    group_rows = perm.shape[0]
    share = rows // dp_count
    top = routes.shape[1]
    experts_n, _, part_hidden = w_gate.shape
    hidden = experts_n * part_hidden
    capacity = 9 * group_rows * top // (8 * experts_n)
    kv_heads = w_keyval.shape[1] // (2 * HD)
    query_cols = w_query.shape[1]
    team = 8
    teams = [[t * team + i for i in range(team)] for t in range(dp_count // team)]
    teams = None if len(teams) == 1 else teams
    piece_rows = width // team
    member = d % team

    def z_move(x, pairs):
        return lax.ppermute(x, "tensor", pairs)

    def dp_move(x, bit):
        return lax.ppermute(x, "dp", [(i, i ^ bit) for i in range(dp_count)])

    near, far, across = [[(i, i ^ m) for i in range(tensor_count)] for m in (1, 2, 3)]
    up_one, up_two = [[(i, i + m) for i in range(tensor_count - m)] for m in (1, 2)]

    def deal(x):
        return lax.all_to_all(
            x.reshape(dp_count, share, x.shape[1]), "dp", split_axis=0, concat_axis=0, tiled=True
        ).reshape(rows, x.shape[1])

    def team_gather(x):
        return lax.all_gather(x, "dp", axis=0, tiled=True, axis_index_groups=teams)

    def flat(w):
        return w.transpose(0, 2, 1).reshape(hidden, w.shape[1])

    own_perm = lax.dynamic_slice_in_dim(perm, z * rows, rows, 0)
    own_routes = lax.dynamic_slice_in_dim(routes, z * rows, rows, 0)
    dest = own_perm // group_rows
    place = own_perm % rows
    row_index = jnp.arange(rows, dtype=jnp.int32)
    lower = (row_index[:, None] > row_index[None, :]).astype(BF16)
    dest_hot = (dest[:, None] == jnp.arange(dp_count, dtype=jnp.int32)[None, :]).astype(BF16)
    earlier = jnp.sum(mm(lower, dest_hot) * dest_hot.astype(F32), axis=1).astype(jnp.int32)
    slot = dest * share + earlier
    pack = (row_index[:, None] == slot[None, :]).astype(BF16)
    meta = jnp.concatenate(
        [
            (place // 16)[:, None].astype(BF16),
            (place % 16)[:, None].astype(BF16),
            own_routes.astype(BF16),
            gates,
            jnp.zeros((rows, META - 2 - 2 * top), BF16),
        ],
        axis=1,
    )
    packed = mm(pack, jnp.concatenate([tokens, meta], axis=1)).astype(BF16)
    wg_own, wu_own = flat(w_gate), flat(w_up)
    wd_own = w_down.reshape(hidden, width)
    out_rows = query_cols // team
    hidden_piece = hidden // team

    def piece(w, count):
        return lax.dynamic_slice_in_dim(w, member * count, count, 0)

    wg_piece, wu_piece, wd_piece = [piece(w, hidden_piece) for w in (wg_own, wu_own, wd_own)]
    packed_dy = mm(pack, cotangent).astype(BF16)
    packed, packed_dy = tie(packed, packed_dy)
    arrived, wq_z, wo_z = open_moves(
        packed.reshape(dp_count, share, width + META),
        piece(w_query, piece_rows),
        piece(w_out, out_rows),
        tensor_count,
    )
    arrived, wg_piece, wu_piece = tie(arrived.reshape(rows, width + META), wg_piece, wu_piece)
    wg_moved, wu_moved = z_move(wg_piece, far), z_move(wu_piece, far)
    wq_all = team_gather(wq_z).reshape(team, tensor_count, piece_rows, query_cols)
    wo_all = team_gather(wo_z).reshape(team, tensor_count, out_rows, width)
    wo = wo_all.transpose(1, 0, 2, 3).reshape(tensor_count * query_cols, width)

    meta_in = arrived[:, width:].astype(F32)
    place_in = (meta_in[:, 0] * 16.0 + meta_in[:, 1]).astype(jnp.int32)
    unpack = (row_index[:, None] == place_in[None, :]).astype(BF16)
    dealt = mm(unpack, arrived)
    x_rows = dealt[:, :width]
    meta_rows = dealt[:, width:]

    expert_ids = jnp.arange(experts_n, dtype=jnp.int32).astype(F32)
    route_rows = meta_rows[:, 2 : 2 + top]
    gate_rows = meta_rows[:, 2 + top : 2 + 2 * top]
    hot = route_rows[:, :, None] == expert_ids[None, None, :]
    routed = jnp.sum(hot.astype(F32), axis=1)
    counts = jnp.pad(jnp.sum(routed, axis=0)[None, :], ((0, 7), (0, HD - experts_n)))

    seq_lengths = lengths[0]
    seq_index = jnp.arange(seq_lengths.shape[0], dtype=jnp.int32)
    seq_ends = jnp.sum(
        jnp.where(seq_index[None, :] <= seq_index[:, None], seq_lengths[None, :], 0), axis=1
    ).astype(jnp.int32)
    global_row = z * rows + row_index
    start = jnp.max(
        jnp.where(global_row[:, None] >= seq_ends[None, :], seq_ends[None, :], 0), axis=1
    ).astype(jnp.int32)
    offset = (global_row - start).astype(F32)
    frequency = ROPE_BASE ** (-2.0 * jnp.arange(HD // 2, dtype=F32) / HD)
    angles = offset[:, None] * frequency[None, :]
    cosine, sine = jnp.cos(angles), jnp.sin(angles)
    cos_full = jnp.concatenate([cosine, cosine], axis=1)
    sin_full = jnp.concatenate([-sine, sine], axis=1)
    start = start[:, None]
    z_arg = z.astype(jnp.int32)[None]

    inv_one = lax.rsqrt(jnp.mean(x_rows * x_rows, axis=1, keepdims=True) + EPS)
    n1 = (x_rows * inv_one * gain_attn).astype(BF16)
    weight = jnp.sum(jnp.where(hot, gate_rows[:, :, None], 0.0), axis=1)
    marks = jnp.pad(
        jnp.concatenate([routed, weight], axis=1).astype(BF16), ((0, 0), (0, HD - 2 * experts_n))
    )
    kv, kv_one, kv_two, counts, marks_near, arrived_dy = keyval(
        n1,
        w_keyval,
        cos_full,
        sin_full,
        counts,
        marks,
        packed_dy.reshape(dp_count, share, width),
        tensor_count,
    )
    arrived_dy = arrived_dy.reshape(rows, width)
    kv, n1, wg_moved, wu_moved = tie(kv, n1, wg_moved, wu_moved)

    dy_rows = mm(unpack, arrived_dy).astype(BF16)
    n1, dy_rows = tie(n1, dy_rows)
    q = project_query(z_arg, n1, wq_all, cos_full, sin_full)
    dy_near = z_move(dy_rows, near)
    kvs = (kv_two, kv_one, kv)
    o, lse = attend(z_arg, start, q, kvs, kv_heads)
    o, wd_piece, dy_near, counts, weight, marks_near = tie(
        o, wd_piece, dy_near, counts, weight, marks_near
    )

    def kept_gates(routed, weight, at):
        block = (z - 1 - jnp.arange(tensor_count, dtype=jnp.int32)) % tensor_count
        base = jnp.sum(
            jnp.where((block < at)[:, None], counts[:, 0, :experts_n], 0.0), axis=0
        )
        position = mm(lower, routed.astype(BF16)) + base[None, :]
        weight = jnp.where(position < capacity, weight, 0.0).astype(BF16)
        return row_major(jnp.repeat(weight, part_hidden, axis=1))

    gate_own = kept_gates(routed, weight, z)
    marks_near = marks_near.astype(F32)
    gate_near = kept_gates(
        marks_near[:, :experts_n], marks_near[:, experts_n : 2 * experts_n], z + 1 - 2 * (z % 2)
    )
    wg_far = team_gather(wg_moved)
    wu_far = team_gather(wu_moved)
    h = x_rows + mm(o, wo)
    inv_two = lax.rsqrt(jnp.mean(h * h, axis=1, keepdims=True) + EPS)
    n2 = (h * inv_two * gain_moe).astype(BF16)

    halving = dp_count == 8
    d_arg = d.astype(jnp.int32)[None]
    out_w = width // dp_count
    orders_a = ((1, 5, 3, 7), (0, 4, 2, 6))
    orders_b = ((1, 3, 5, 7), (0, 2, 4, 6))

    def turned(tiles, *orders):
        if halving:
            return turn(d_arg, tiles, orders, dp_count)
        return [jnp.concatenate(tiles, axis=0).T] * len(orders)

    def dp_sum(x):
        return lax.psum_scatter(x, "dp", scatter_dimension=0, tiled=True)

    def first_moves(parts):
        return parts[0], dp_move(parts[1], xy[0]), parts[2], dp_move(parts[3], yx[0])

    def second_moves(moved):
        halves = []
        for keep, got, bit in ((*moved[:2], xy[1]), (*moved[2:], yx[1])):
            x = keep.astype(F32) + got.astype(F32)
            half = x.shape[0] // 2
            halves += [x[:half], dp_move(x[half:].astype(BF16), bit)]
        return halves

    def expert_lefts(n_a, d_a, keep):
        return n_a[keep], d_a[keep], n_a[2 + keep], d_a[2 + keep]

    xy, yx = (2, 4), (4, 2)
    n2_near = z_move(n2, near)
    y, dn2, *own_grads = experts(0, n2, dy_rows, gate_own, wg_own, wu_own, wd_own)
    n2_near, y, wd_piece = tie(n2_near, y, wd_piece)
    n2_a = turned((n2, n2_near), *orders_a, *orders_b)
    n1_t = turned((n1,), *orders_a, *orders_b)
    dy_near, *turns = tie(dy_near, *n2_a, *n1_t)
    n2_a, n1_t = turns[:4], turns[4:]
    wd_moved = z_move(wd_piece, far)
    yn, dnn, *own_grads = experts(
        1, n2_near, dy_near, gate_near, wg_own, wu_own, wd_own, filled=own_grads
    )
    yn, wd_moved, *own_grads = tie(yn, wd_moved, *own_grads)
    wd_far = team_gather(wd_moved)
    dy_a = turned((dy_rows, dy_near), *orders_a, *orders_b)
    if halving:
        own = gradients(
            EXPERT_JOBS,
            expert_lefts(n2_a, dy_a, 0),
            expert_lefts(n2_a, dy_a, 1),
            own_grads[::-1],
            3,
        )
        wg_far, *own = tie(wg_far, *own)
        own = first_moves(own)
    yn, dnn, *far_grads = experts(
        1, n2_near, dy_near, gate_near, wg_far, wu_far, wd_far, (yn, dnn), last=True
    )
    dnn_moved = z_move(dnn, near)
    y, dn2, *far_grads = experts(
        0, n2, dy_rows, gate_own, wg_far, wu_far, wd_far, (y, dn2), far_grads
    )
    if halving:
        far_grads = far_grads[::-1]
        far_sent = gradient_parts(EXPERT_JOBS, expert_lefts(n2_a, dy_a, 0), far_grads)
        dnn_moved, far_sent, *own = tie(dnn_moved, far_sent, *own)
        got = dp_move(far_sent, 1)
        own = second_moves(own)
    yn, dnn_moved = tie(yn, dnn_moved)
    yn_moved = z_move(yn, near)
    dn2 = dn2 + dnn_moved.astype(F32)

    gain_two_part = jnp.sum(dn2 * h * inv_two, axis=0)
    u2 = dn2 * gain_moe
    dh = dy_rows.astype(F32) + inv_two * (
        u2 - h * inv_two * inv_two * jnp.mean(u2 * h, axis=1, keepdims=True)
    )
    dhb = dh.astype(BF16)
    do = mm_nt(dhb, wo).astype(BF16)
    if halving:
        far_w = gradient_parts(EXPERT_JOBS, expert_lefts(n2_a, dy_a, 1), far_grads, got)
        do, *both = tie(do, *far_w, *own)
        far_w, own = both[:4], both[4:]
        far_w = first_moves(far_w)
    dq, dkv_two, dkv_one, dkv = attend_back(
        z_arg, start, q, o, do, lse, cos_full, sin_full, kvs, kv_heads
    )
    dhb_t = turned((dhb,), *orders_b)
    if halving:
        dq, *far_w = tie(dq, *far_w)
        *parts, dkv_sum, far_sum = mix(
            dq, o, (n1_t[0], n1_t[1], *dhb_t), dkv_one, dkv_two, far_w
        )
        far_sum = z_move(far_sum, far)
        dkv_sum, yn_moved = tie(dkv_sum, yn_moved)
    else:
        dkv_one = z_move(dkv_one, [(b, a) for a, b in up_one])
        dkv_two = z_move(dkv_two, [(b, a) for a, b in up_two])
        dkv_sum = dkv_one.astype(F32) + dkv_two.astype(F32)
        sum_q, sum_o = [
            dp_sum(mm_tn(a, b).astype(BF16)).astype(F32) for a, b in ((n1, dq), (dhb, o))
        ]
    dkv = dkv + dkv_sum.astype(F32)

    def unrotate(u):
        swapped = jnp.concatenate([u[:, HD // 2 :], u[:, : HD // 2]], axis=1)
        return u * cos_full - swapped * sin_full

    dkv = jnp.concatenate(
        [unrotate(dkv[:, i * HD : (i + 1) * HD]) for i in range(kv_heads)]
        + [dkv[:, kv_heads * HD :]],
        axis=1,
    ).astype(BF16)
    dn1 = project_back(z_arg, dq, wq_all, dkv, w_keyval)
    gain_one_part = jnp.sum(dn1 * x_rows * inv_one, axis=0)
    u1 = dn1 * gain_attn
    dx = dh + inv_one * (
        u1 - x_rows * inv_one * inv_one * jnp.mean(u1 * x_rows, axis=1, keepdims=True)
    )

    result = h + y + yn_moved.astype(F32)
    result_out = mm_tn(unpack, result.astype(BF16)).astype(BF16)

    if halving:
        sum_gate, sum_up, sum_down = assemble(own, far_sum, experts_n)
    else:
        lefts = (n2_a[0], dy_a[0])
        far_sums = [dp_sum(mm(a, b).astype(BF16)) for a, b in zip(lefts, far_grads[::-1])]
        own_sums = [dp_sum(mm(a, b).astype(BF16)) for a, b in zip(lefts, own_grads[::-1])]
        sum_gu, sum_down = [
            a.astype(F32) + z_move(b, far).astype(F32) for a, b in zip(own_sums, far_sums)
        ]
        sum_gu = sum_gu.reshape(out_w, hidden // 512, 2, 512)
        sum_gate, sum_up = [
            sum_gu[:, :, i].reshape(out_w, experts_n, part_hidden).transpose(1, 0, 2) for i in (0, 1)
        ]
        sum_down = sum_down.reshape(out_w, experts_n, part_hidden).transpose(1, 2, 0)

    gains = jnp.stack([gain_one_part, gain_two_part])

    def gain_columns(order):
        blocks = gains.reshape(2, dp_count, out_w)
        if halving:
            blocks = jnp.stack(
                [lax.dynamic_index_in_dim(blocks, d ^ p, 1, keepdims=False) for p in order], 1
            )
        return jnp.pad(blocks.reshape(2, -1).T, ((0, 0), (dkv.shape[1], HD - 2)))

    columns = [gain_columns(order) for order in orders_b]
    dkv_wide = jnp.pad(dkv, ((0, 0), (0, HD)))
    if halving:
        kv_send, kv_keep = [
            (mm(left, dkv_wide) + column).astype(BF16) for left, column in zip(n1_t[2:], columns)
        ]
        dx_out = mm_tn(unpack, dx.astype(BF16)).astype(BF16).reshape(dp_count, share, width)
        back, back_out, sum_query, sum_out, small = finish(
            dx_out,
            result_out.reshape(dp_count, share, width),
            *parts,
            kv_send,
            kv_keep,
            tensor_count,
        )
        grad_tokens = mm_tn(pack, back.reshape(rows, width)).astype(BF16)
        outputs = mm_tn(pack, back_out.reshape(rows, width)).astype(BF16)
    else:
        outputs = mm_tn(pack, deal(result_out)).astype(BF16)
        grad_tokens = mm_tn(pack, deal(mm_tn(unpack, dx.astype(BF16)).astype(BF16))).astype(BF16)
        small = dp_sum((mm(n1_t[3], dkv_wide) + columns[0]).astype(BF16))
        small = small.astype(F32) + sum(
            z_move(small, move).astype(F32) for move in (near, far, across)
        )

        def z_block(x, m):
            return lax.dynamic_slice_in_dim(x, (z ^ m) * query_cols, query_cols, 1)

        both = [jnp.concatenate([z_block(sum_q, m), z_block(sum_o, m)], axis=1) for m in range(4)]
        total = both[0] + sum(
            z_move(part.astype(BF16), move).astype(F32)
            for part, move in zip(both[1:], (near, far, across))
        )
        sum_query, sum_out = total[:, :query_cols], total[:, query_cols:]
    sum_out = sum_out.T
    kv_cols = w_keyval.shape[1]
    return (
        outputs,
        grad_tokens,
        small[:, kv_cols],
        sum_query,
        small[:, :kv_cols],
        sum_out,
        small[:, kv_cols + 1],
        sum_gate,
        sum_up,
        sum_down,
    )


def solution(mesh):
    in_specs = (
        P(("dp", "tensor"), None),
        P("dp"),
        P("dp", None),
        P(("dp", "tensor"), None),
        P("dp", None),
        P(("dp", "tensor"), None),
        P(),
        P(None, "tensor"),
        P(),
        P("tensor", None),
        P(),
        P(None, None, "tensor"),
        P(None, None, "tensor"),
        P(None, "tensor", None),
    )
    out_specs = (
        P(("dp", "tensor"), None),
        P(("dp", "tensor"), None),
        P("dp"),
        P("dp", "tensor"),
        P("dp", None),
        P("tensor", "dp"),
        P("dp"),
        P(None, "dp", "tensor"),
        P(None, "dp", "tensor"),
        P(None, "tensor", "dp"),
    )
    return jax.shard_map(
        per_device, mesh=mesh, in_specs=in_specs, out_specs=out_specs, check_vma=False
    )
```

```python
import functools

import jax
import jax.numpy as jnp
from jax import lax
from jax.experimental import pallas as pl
from jax.experimental.layout import Layout, with_layout_constraint
from jax.experimental.pallas import tpu as pltpu
from jax.sharding import PartitionSpec as P

HD = 128
EPS = 1e-06
ROPE_BASE = 1000000.0
MASKED = -1e30
LOG2E = 1.4426950408889634
F32 = jnp.float32
BF16 = jnp.bfloat16
META = 128


def mm(a, b):
    return lax.dot_general(a, b, (((1,), (0,)), ((), ())), preferred_element_type=F32)


def mm_nt(a, b):
    return lax.dot_general(a, b, (((1,), (1,)), ((), ())), preferred_element_type=F32)


def mm_tn(a, b):
    return lax.dot_general(a, b, (((0,), (0,)), ((), ())), preferred_element_type=F32)


def params(mb=56):
    return pltpu.CompilerParams(vmem_limit_bytes=mb * 2**20)


def swap_halves(u):
    return pltpu.roll(u, HD // 2, 1)


def open_kernel(
    deal_ref,
    q_ref,
    o_ref,
    dealt_ref,
    q_all,
    o_all,
    send,
    recv,
    deal_send,
    deal_recv,
):
    z = lax.axis_index("tensor")
    d = lax.axis_index("dp")
    d_count = deal_ref.shape[0]
    z_count = q_all.shape[0]
    others = [{"tensor": flip(z, m)} for m in range(1, z_count)]
    peers = [{"dp": (d + p) % d_count} for p in range(1, d_count)]
    barrier = pltpu.get_barrier_semaphore()
    for other in others + peers:
        pl.semaphore_signal(barrier, inc=1, device_id=other, device_id_type=pl.DeviceIdType.MESH)
    pl.semaphore_wait(barrier, len(others) + len(peers))
    moves = [(q_ref, q_all.at[m], others[m - 1]) for m in range(1, z_count)]
    moves += [(o_ref, o_all.at[z], other) for other in others]
    copies = []
    for p, peer in enumerate(peers):
        copy = pltpu.make_async_remote_copy(
            src_ref=deal_ref.at[(d + p + 1) % d_count],
            dst_ref=dealt_ref.at[d],
            send_sem=deal_send.at[p],
            recv_sem=deal_recv.at[p],
            device_id=peer,
            device_id_type=pl.DeviceIdType.MESH,
        )
        copy.start()
        copies.append(copy)
    for at, (src, dst, to) in enumerate(moves):
        copy = pltpu.make_async_remote_copy(
            src_ref=src,
            dst_ref=dst,
            send_sem=send.at[at],
            recv_sem=recv.at[at],
            device_id=to,
            device_id_type=pl.DeviceIdType.MESH,
        )
        copy.start()
        copies.append(copy)
    dealt_ref[d] = deal_ref[d]
    q_all[0] = q_ref[...]
    o_all[z] = o_ref[...]
    for copy in copies:
        copy.wait()


def open_moves(deals, q, o, z_count):
    vmem = pl.BlockSpec(memory_space=pltpu.VMEM)
    shapes = [deals.shape, (z_count, *q.shape), (z_count, *o.shape)]
    moves = 2 * (z_count - 1)
    return pl.pallas_call(
        open_kernel,
        in_specs=[vmem] * 3,
        out_specs=[vmem] * 3,
        out_shape=[jax.ShapeDtypeStruct(shape, BF16) for shape in shapes],
        scratch_shapes=[
            pltpu.SemaphoreType.DMA((moves,)),
            pltpu.SemaphoreType.DMA((moves,)),
            pltpu.SemaphoreType.DMA((deals.shape[0] - 1,)),
            pltpu.SemaphoreType.DMA((deals.shape[0] - 1,)),
        ],
        compiler_params=pltpu.CompilerParams(
            vmem_limit_bytes=40 * 2**20, collective_id=4, has_side_effects=True
        ),
        name="open_moves",
    )(deals, q, o)


def keyval_kernel(
    x_ref,
    w_ref,
    cos_ref,
    sin_ref,
    count_ref,
    mark_ref,
    deal_ref,
    kv_ref,
    one_ref,
    two_ref,
    counts_ref,
    near_ref,
    dealt_ref,
    send,
    recv,
    deal_send,
    deal_recv,
):
    z = lax.axis_index("tensor")
    d = lax.axis_index("dp")
    d_count = deal_ref.shape[0]
    z_count = counts_ref.shape[0]
    others = [{"tensor": (z + m) % z_count} for m in range(1, z_count)]
    barrier = pltpu.get_barrier_semaphore()
    peers = [{"dp": (d + p) % d_count} for p in range(1, d_count)]
    for other in others + peers:
        pl.semaphore_signal(barrier, inc=1, device_id=other, device_id_type=pl.DeviceIdType.MESH)
    raw = mm(x_ref[...], w_ref[...])
    turned = raw.shape[1] // 2
    for i in range(turned // HD):
        u = raw[:, i * HD : (i + 1) * HD]
        u = u * cos_ref[...] + swap_halves(u) * sin_ref[...]
        kv_ref[:, i * HD : (i + 1) * HD] = u.astype(BF16)
    kv_ref[:, turned:] = raw[:, turned:].astype(BF16)
    pl.semaphore_wait(barrier, z_count - 1 + d_count - 1)
    moves = [(count_ref, counts_ref.at[m], others[m]) for m in range(z_count - 1)]
    moves += [(mark_ref, near_ref, {"tensor": flip(z, 1)})]
    moves += [(kv_ref, one_ref, others[0]), (one_ref, two_ref, others[0])]
    copies = []
    for at, (src, dst, to) in enumerate(moves):
        copy = pltpu.make_async_remote_copy(
            src_ref=src,
            dst_ref=dst,
            send_sem=send.at[at],
            recv_sem=recv.at[at],
            device_id=to,
            device_id_type=pl.DeviceIdType.MESH,
        )
        copies.append(copy)
    for copy in copies[:-1]:
        copy.start()
    for p, peer in enumerate(peers):
        copy = pltpu.make_async_remote_copy(
            src_ref=deal_ref.at[(d + p + 1) % d_count],
            dst_ref=dealt_ref.at[d],
            send_sem=deal_send.at[p],
            recv_sem=deal_recv.at[p],
            device_id=peer,
            device_id_type=pl.DeviceIdType.MESH,
        )
        copy.start()
        copies.append(copy)
    counts_ref[z_count - 1] = count_ref[...]
    dealt_ref[d] = deal_ref[d]
    step_one, step_two = copies[z_count], copies[z_count + 1]
    step_one.wait()
    step_two.start()
    for copy in copies[:z_count] + copies[z_count + 1 :]:
        copy.wait()


def keyval(x, w, cos_full, sin_full, counts, marks, deals, z_count):
    rows = x.shape[0]
    columns = w.shape[1]
    vmem = pl.BlockSpec(memory_space=pltpu.VMEM)
    block = jax.ShapeDtypeStruct((rows, columns), BF16)
    return pl.pallas_call(
        keyval_kernel,
        in_specs=[vmem] * 7,
        out_specs=[vmem] * 6,
        out_shape=[block] * 3
        + [
            jax.ShapeDtypeStruct((z_count, *counts.shape), counts.dtype),
            jax.ShapeDtypeStruct(marks.shape, marks.dtype),
            jax.ShapeDtypeStruct(deals.shape, deals.dtype),
        ],
        scratch_shapes=[
            pltpu.SemaphoreType.DMA((z_count + 2,)),
            pltpu.SemaphoreType.DMA((z_count + 2,)),
            pltpu.SemaphoreType.DMA((deals.shape[0] - 1,)),
            pltpu.SemaphoreType.DMA((deals.shape[0] - 1,)),
        ],
        compiler_params=pltpu.CompilerParams(
            vmem_limit_bytes=40 * 2**20, collective_id=1, has_side_effects=True
        ),
        name="keyval",
    )(x, w, cos_full, sin_full, counts, marks, deals)


def project_query_kernel(z_ref, x_ref, w_ref, cos_ref, sin_ref, out_ref):
    raw = mm(x_ref[...], w_ref[...].reshape(x_ref.shape[1], out_ref.shape[1]))
    for i in range(raw.shape[1] // HD):
        u = raw[:, i * HD : (i + 1) * HD]
        turned = u * cos_ref[...] + swap_halves(u) * sin_ref[...]
        out_ref[:, i * HD : (i + 1) * HD] = (turned * SCALE).astype(BF16)


def project_query(z, x, w, cos_full, sin_full):
    rows, width = x.shape
    pieces, blocks, piece, columns = w.shape
    return pl.pallas_call(
        project_query_kernel,
        grid_spec=pltpu.PrefetchScalarGridSpec(
            num_scalar_prefetch=1,
            grid=(blocks,),
            in_specs=[
                pl.BlockSpec((rows, width), lambda i, s: (0, 0)),
                pl.BlockSpec(
                    (pieces, 1, piece, columns), lambda i, s: (0, jnp.bitwise_xor(i, s[0]), 0, 0)
                ),
                pl.BlockSpec((rows, HD), lambda i, s: (0, 0)),
                pl.BlockSpec((rows, HD), lambda i, s: (0, 0)),
            ],
            out_specs=pl.BlockSpec((rows, columns), lambda i, s: (0, i)),
        ),
        out_shape=jax.ShapeDtypeStruct((rows, blocks * columns), BF16),
        compiler_params=params(),
        name="project_query",
        cost_estimate=pl.CostEstimate(
            flops=2 * rows * width * blocks * columns,
            bytes_accessed=2 * (2 * rows * width + width * blocks * columns),
            transcendentals=0,
        ),
    )(z, x, w, cos_full, sin_full)


def project_back_kernel(z_ref, dq_ref, w_ref, dkv_ref, wkv_ref, out_ref):
    step = pl.program_id(0)
    width = out_ref.shape[1]
    part = mm_nt(dq_ref[...], w_ref[...].reshape(width, dq_ref.shape[1]))

    @pl.when(step == 0)
    def _():
        out_ref[...] = part + mm_nt(dkv_ref[...], wkv_ref[...])

    @pl.when(step > 0)
    def _():
        out_ref[...] += part


def project_back(z, dq, w, dkv, wkv):
    rows = dq.shape[0]
    pieces, blocks, piece, columns = w.shape
    width = pieces * piece
    return pl.pallas_call(
        project_back_kernel,
        grid_spec=pltpu.PrefetchScalarGridSpec(
            num_scalar_prefetch=1,
            grid=(blocks,),
            in_specs=[
                pl.BlockSpec((rows, columns), lambda i, s: (0, i)),
                pl.BlockSpec(
                    (pieces, 1, piece, columns), lambda i, s: (0, jnp.bitwise_xor(i, s[0]), 0, 0)
                ),
                pl.BlockSpec(dkv.shape, lambda i, s: (0, 0)),
                pl.BlockSpec(wkv.shape, lambda i, s: (0, 0)),
            ],
            out_specs=pl.BlockSpec((rows, width), lambda i, s: (0, 0)),
        ),
        out_shape=jax.ShapeDtypeStruct((rows, width), F32),
        compiler_params=params(),
        name="project_back",
        cost_estimate=pl.CostEstimate(
            flops=2 * rows * width * (blocks * columns + dkv.shape[1]),
            bytes_accessed=2 * width * (3 * rows + blocks * columns),
            transcendentals=0,
        ),
    )(z, dq, w, dkv, wkv)


ATTEND_TILE = 256
SCALE = HD**-0.5 * LOG2E


def make_bias(z, start_ref, bias_ref):
    tiles, tile, width = bias_ref.shape
    rows = tiles * tile
    for i in range(tiles):
        key = (z - 2) * rows + i * tile + lax.broadcasted_iota(jnp.int32, (tile, width), 1)
        query = z * rows + i * tile + lax.broadcasted_iota(jnp.int32, (tile, width), 0)
        allowed = (key >= start_ref[i * tile : (i + 1) * tile]) & (key <= query)
        bias_ref[i] = jnp.where(allowed, 0.0, MASKED)


def attend_kernel(
    kv_heads, z_ref, start_ref, q_ref, kv0_ref, kv1_ref, kv2_ref, o_ref, lse_ref, bias_ref, k_ref, v_ref
):
    head = pl.program_id(0)
    each = pl.num_programs(0) // kv_heads
    rows = q_ref.shape[0]
    tiles, tile, width = bias_ref.shape

    @pl.when(head == 0)
    def _():
        make_bias(z_ref[0], start_ref, bias_ref)
        v_ref[:, HD:] = jnp.ones((v_ref.shape[0], HD), BF16)

    @pl.when(head % each == 0)
    def _():
        kvh = head // each
        for j, ref in enumerate((kv0_ref, kv1_ref, kv2_ref)):
            at = slice(j * rows, (j + 1) * rows)
            k_ref[at] = ref[:, pl.ds(pl.multiple_of(kvh * HD, HD), HD)]
            v_ref[at, :HD] = ref[:, pl.ds(pl.multiple_of((kv_heads + kvh) * HD, HD), HD)]

    for i in range(tiles):
        at, window = slice(i * tile, (i + 1) * tile), slice(i * tile, i * tile + width)
        score = mm_nt(q_ref[at], k_ref[window]) + bias_ref[i]
        peak = jnp.max(score, axis=1, keepdims=True)
        mixed = mm(jnp.exp2(score - peak).astype(BF16), v_ref[window])
        total = mixed[:, HD : HD + 1]
        o_ref[at] = (mixed[:, :HD] / total).astype(BF16)
        lse_ref[0, at] = peak + jnp.log2(total)


def attend(z, start, q, kvs, kv_heads):
    rows, columns = q.shape
    heads = columns // HD
    tile = ATTEND_TILE
    kv_spec = pl.BlockSpec(kvs[0].shape, lambda h, s: (0, 0))
    return pl.pallas_call(
        functools.partial(attend_kernel, kv_heads),
        grid_spec=pltpu.PrefetchScalarGridSpec(
            num_scalar_prefetch=1,
            grid=(heads,),
            in_specs=[
                pl.BlockSpec((rows, 1), lambda h, s: (0, 0)),
                pl.BlockSpec((rows, HD), lambda h, s: (0, h)),
                *[kv_spec] * 3,
            ],
            out_specs=[
                pl.BlockSpec((rows, HD), lambda h, s: (0, h)),
                pl.BlockSpec((1, rows, 1), lambda h, s: (h, 0, 0)),
            ],
            scratch_shapes=[
                pltpu.VMEM((rows // tile, tile, 2 * rows + tile), F32),
                pltpu.VMEM((3 * rows, HD), BF16),
                pltpu.VMEM((3 * rows, 2 * HD), BF16),
            ],
        ),
        out_shape=[
            jax.ShapeDtypeStruct((rows, columns), BF16),
            jax.ShapeDtypeStruct((heads, rows, 1), F32),
        ],
        compiler_params=params(),
        name="attend",
        cost_estimate=pl.CostEstimate(
            flops=12 * rows * rows * columns,
            bytes_accessed=8 * rows * columns,
            transcendentals=rows * rows * 3 * heads,
        ),
    )(z, start, q, *kvs)


def attend_back_kernel(
    kv_heads,
    z_ref,
    start_ref,
    q_ref,
    o_ref,
    do_ref,
    lse_ref,
    cos_ref,
    sin_ref,
    kv0_ref,
    kv1_ref,
    kv2_ref,
    dq_ref,
    d0_ref,
    d1_ref,
    d2_ref,
    bias_ref,
    k_ref,
    v_ref,
    dk_ref,
    dv_ref,
):
    head = pl.program_id(0)
    each = pl.num_programs(0) // kv_heads
    rows = q_ref.shape[0]
    tiles, tile, width = bias_ref.shape
    kvh = head // each
    kcol = pl.ds(pl.multiple_of(kvh * HD, HD), HD)
    vcol = pl.ds(pl.multiple_of((kv_heads + kvh) * HD, HD), HD)

    @pl.when(head == 0)
    def _():
        make_bias(z_ref[0], start_ref, bias_ref)

    @pl.when(head % each == 0)
    def _():
        for j, ref in enumerate((kv0_ref, kv1_ref, kv2_ref)):
            k_ref[j * rows : (j + 1) * rows] = ref[:, kcol]
            v_ref[j * rows : (j + 1) * rows] = ref[:, vcol]
        dk_ref[...] = jnp.zeros_like(dk_ref)
        dv_ref[...] = jnp.zeros_like(dv_ref)

    for i in range(tiles):
        at, window = slice(i * tile, (i + 1) * tile), slice(i * tile, i * tile + width)
        q = q_ref[at]
        do = do_ref[at]
        centre = jnp.sum(do.astype(F32) * o_ref[at].astype(F32), axis=1, keepdims=True)
        soft = jnp.exp2(mm_nt(q, k_ref[window]) + (bias_ref[i] - lse_ref[0, at]))
        dv_ref[window] += mm_tn(soft.astype(BF16), do)
        dscore = (soft * (mm_nt(do, v_ref[window]) - centre)).astype(BF16)
        dk_ref[window] += mm_tn(dscore, q)
        dq = mm(dscore, k_ref[window]) * (HD**-0.5)
        dq_ref[at] = (dq * cos_ref[at] - swap_halves(dq) * sin_ref[at]).astype(BF16)

    @pl.when(head % each == each - 1)
    def _():
        for j, ref in enumerate((d0_ref, d1_ref, d2_ref)):
            at = slice(j * rows, (j + 1) * rows)
            ref[:, kcol] = (dk_ref[at] * (1 / LOG2E)).astype(ref.dtype)
            ref[:, vcol] = dv_ref[at].astype(ref.dtype)


def attend_back(z, start, q, o, do, lse, cos_full, sin_full, kvs, kv_heads):
    rows, columns = q.shape
    heads = columns // HD
    tile = ATTEND_TILE
    kv_columns = kvs[0].shape[1]
    kv_spec = pl.BlockSpec((rows, kv_columns), lambda h, s: (0, 0))
    head_spec = pl.BlockSpec((rows, HD), lambda h, s: (0, h))
    table_spec = pl.BlockSpec((rows, HD), lambda h, s: (0, 0))
    return pl.pallas_call(
        functools.partial(attend_back_kernel, kv_heads),
        grid_spec=pltpu.PrefetchScalarGridSpec(
            num_scalar_prefetch=1,
            grid=(heads,),
            in_specs=[
                pl.BlockSpec((rows, 1), lambda h, s: (0, 0)),
                head_spec,
                head_spec,
                head_spec,
                pl.BlockSpec((1, rows, 1), lambda h, s: (h, 0, 0)),
                table_spec,
                table_spec,
                *[kv_spec] * 3,
            ],
            out_specs=[head_spec, *[kv_spec] * 3],
            scratch_shapes=[
                pltpu.VMEM((rows // tile, tile, 2 * rows + tile), F32),
                pltpu.VMEM((3 * rows, HD), BF16),
                pltpu.VMEM((3 * rows, HD), BF16),
                pltpu.VMEM((3 * rows, HD), F32),
                pltpu.VMEM((3 * rows, HD), F32),
            ],
        ),
        out_shape=[
            jax.ShapeDtypeStruct((rows, columns), BF16),
            jax.ShapeDtypeStruct((rows, kv_columns), BF16),
            jax.ShapeDtypeStruct((rows, kv_columns), BF16),
            jax.ShapeDtypeStruct((rows, kv_columns), F32),
        ],
        compiler_params=params(),
        name="attend_back",
        cost_estimate=pl.CostEstimate(
            flops=30 * rows * rows * columns,
            bytes_accessed=12 * rows * columns,
            transcendentals=rows * rows * 3 * heads,
        ),
    )(z, start, q, o, do, lse, cos_full, sin_full, *kvs)


def expert_kernel(chunk, first, last, x_ref, dy_ref, gate_ref, wg_ref, wu_ref, wd_ref, *refs):
    if last:
        y_out, dn_out, hs_ref, dgu_ref, y_ref, dn_ref = refs[-6:]
    else:
        y_ref, dn_ref, hs_ref, dgu_ref = refs[-4:]
    step = pl.program_id(0)

    @pl.when(step == 0)
    def _():
        if first:
            y_ref[...] = jnp.zeros_like(y_ref)
            dn_ref[...] = jnp.zeros_like(dn_ref)
        else:
            y_ref[...] = refs[0][...]
            dn_ref[...] = refs[1][...]

    x = x_ref[...]
    gate = gate_ref[...].astype(F32)
    g = jnp.maximum(mm_nt(x, wg_ref[...]), 0.0)
    u = mm_nt(x, wu_ref[...])
    square = g * g
    hs = ((square * u).astype(BF16).astype(F32) * gate).astype(BF16)
    hs_ref[...] = hs
    dh = mm_nt(dy_ref[...], wd_ref[...]) * gate
    dg = (dh * u * (2.0 * g)).astype(BF16)
    du = (dh * square).astype(BF16)
    dgu_ref[:, :chunk] = dg
    dgu_ref[:, chunk:] = du
    dn_ref[...] += mm(dg, wg_ref[...]) + mm(du, wu_ref[...])
    y_ref[...] += mm(hs, wd_ref[...])
    if last:

        @pl.when(step == pl.num_programs(0) - 1)
        def _():
            y_out[...] = y_ref[...].astype(BF16)
            dn_out[...] = dn_ref[...].astype(BF16)


def experts(tile, x, dy, gate, wg, wu, wd, before=None, filled=None, last=False, chunk=512):
    rows, width = x.shape
    hidden = gate.shape[1]
    full = pl.BlockSpec((rows, width), lambda i: (0, 0))
    part = pl.BlockSpec((rows, chunk), lambda i: (0, i))
    operands = [x, dy, gate, wg, wu, wd]
    in_specs = [
        full,
        full,
        part,
        *[pl.BlockSpec((chunk, width), lambda i: (i, 0))] * 3,
    ]
    aliases = {}
    if before is not None:
        operands += list(before)
        in_specs += [full] * 2
    if filled is not None:
        aliases = {len(operands): 2, len(operands) + 1: 3}
        operands += list(filled)
        in_specs += [pl.BlockSpec(memory_space=pl.ANY)] * 2
    return pl.pallas_call(
        functools.partial(expert_kernel, chunk, before is None, last),
        grid=(hidden // chunk,),
        in_specs=in_specs,
        out_specs=[
            full,
            full,
            pl.BlockSpec((rows, chunk), lambda i: (tile, i)),
            pl.BlockSpec((rows, 2 * chunk), lambda i: (tile, i)),
        ],
        out_shape=[
            *[jax.ShapeDtypeStruct((rows, width), BF16 if last else F32)] * 2,
            jax.ShapeDtypeStruct((2 * rows, hidden), BF16),
            jax.ShapeDtypeStruct((2 * rows, 2 * hidden), BF16),
        ],
        scratch_shapes=[pltpu.VMEM((rows, width), F32)] * (2 if last else 0),
        input_output_aliases=aliases,
        compiler_params=params(),
        name="experts",
        cost_estimate=pl.CostEstimate(
            flops=12 * rows * width * hidden,
            bytes_accessed=6 * width * hidden + 16 * rows * width,
            transcendentals=0,
        ),
    )(*operands)


def pick(i, values):
    result = values[0]
    for at, value in enumerate(values):
        if at and value != values[at - 1]:
            result = jnp.where(i >= at, value, result)
    return result


def gradient_kernel(jobs, lefts, rights, *refs):
    send_refs, keep_refs, right_refs = refs[:lefts], refs[lefts : 2 * lefts], refs[2 * lefts :]
    outs, (sent, got, send, recv) = right_refs[rights:-4], refs[-4:]
    d = lax.axis_index("dp")
    step = pl.program_id(0)
    count = len(jobs)

    @pl.when(step == 0)
    def _():
        barrier = pltpu.get_barrier_semaphore()
        pl.semaphore_signal(
            barrier, inc=1, device_id={"dp": flip(d, 1)}, device_id_type=pl.DeviceIdType.MESH
        )
        pl.semaphore_wait(barrier, 1)

    def copy(i):
        return pltpu.make_async_remote_copy(
            src_ref=sent.at[i],
            dst_ref=got.at[i],
            send_sem=send.at[i],
            recv_sem=recv.at[i],
            device_id={"dp": flip(d, 1)},
            device_id_type=pl.DeviceIdType.MESH,
        )

    for i, (left, right, _) in enumerate(jobs):

        @pl.when(step == i)
        def _(i=i, left=left, right=right):
            sent[i] = mm(send_refs[left][...], right_refs[right][...]).astype(BF16)
            copy(i).start()

        @pl.when(step == count + i)
        def _(i=i, left=left, right=right):
            value = mm(keep_refs[left][...], right_refs[right][...])
            copy(i).wait()
            value = value + got[i].astype(F32)
            half = value.shape[0] // 2
            side = 2 * (i // (count // 2))
            outs[side][...] = value[:half].astype(BF16)
            outs[side + 1][...] = value[half:].astype(BF16)


def gradients(jobs, send_lefts, keep_lefts, rights, ident, chunk=768):
    rows, tokens = keep_lefts[0].shape
    count = len(jobs)
    each = count // 2
    first = lambda i: (0, jnp.clip(i - count, 0, each - 1))
    second = lambda i: (0, jnp.maximum(i - count - each, 0))
    right_specs = []
    for r in range(len(rights)):
        blocks, at = [], None
        for _, right, block in jobs + jobs:
            at = block if right == r else at
            blocks.append(at)
        known = next(block for block in blocks if block is not None)
        blocks = tuple(known if block is None else block for block in blocks)
        right_specs.append(
            pl.BlockSpec((tokens, chunk), lambda i, blocks=blocks: (0, pick(i, blocks)))
        )
    left = pl.BlockSpec((rows, tokens), lambda i: (0, 0), pipeline_mode=pl.Buffered(1))
    return pl.pallas_call(
        functools.partial(gradient_kernel, jobs, len(keep_lefts), len(rights)),
        grid=(2 * count,),
        in_specs=[*[left] * (2 * len(keep_lefts)), *right_specs],
        out_specs=[
            pl.BlockSpec((rows // 2, chunk), at) for at in (first, first, second, second)
        ],
        out_shape=[jax.ShapeDtypeStruct((rows // 2, each * chunk), BF16)] * 4,
        scratch_shapes=[
            pltpu.VMEM((count, rows, chunk), BF16),
            pltpu.VMEM((count, rows, chunk), BF16),
            pltpu.SemaphoreType.DMA((count,)),
            pltpu.SemaphoreType.DMA((count,)),
        ],
        compiler_params=pltpu.CompilerParams(
            vmem_limit_bytes=56 * 2**20, collective_id=ident, has_side_effects=True
        ),
        name="gradients",
        cost_estimate=pl.CostEstimate(flops=10**9, bytes_accessed=10**6, transcendentals=0),
    )(*send_lefts, *keep_lefts, *rights)


def part_kernel(jobs, lefts, rights, keep, *refs):
    left_refs, right_refs, rest = refs[:lefts], refs[lefts : lefts + rights], refs[lefts + rights :]
    step = pl.program_id(0)
    each = len(jobs) // 2
    for i, (left, right, _) in enumerate(jobs):

        @pl.when(step == i)
        def _(i=i, left=left, right=right):
            side = i // each
            value = mm(left_refs[left][...], right_refs[right][...])
            if keep:
                value = value + rest[0][0].astype(F32)
                half = value.shape[0] // 2
                rest[1 + 2 * side][...] = value[:half].astype(BF16)
                rest[2 + 2 * side][...] = value[half:].astype(BF16)
            else:
                rest[0][0] = value.astype(BF16)


def gradient_parts(jobs, lefts, rights, got=None, chunk=768):
    rows, tokens = lefts[0].shape
    each = len(jobs) // 2
    first = lambda i: (0, jnp.minimum(i, each - 1))
    second = lambda i: (0, jnp.maximum(i - each, 0))
    whole = [pl.BlockSpec((1, rows, chunk), lambda i: (i // each, 0, i % each))]
    if got is None:
        out_specs = whole[0]
        out_shape = jax.ShapeDtypeStruct((2, rows, each * chunk), BF16)
    else:
        out_specs = [pl.BlockSpec((rows // 2, chunk), at) for at in (first, first, second, second)]
        out_shape = [jax.ShapeDtypeStruct((rows // 2, each * chunk), BF16)] * 4
    right_specs = []
    for r in range(len(rights)):
        at, blocks = None, []
        for _, right, block in jobs:
            at = block if right == r else at
            blocks.append(at)
        known = next(block for block in blocks if block is not None)
        blocks = tuple(known if block is None else block for block in blocks)
        right_specs.append(
            pl.BlockSpec((tokens, chunk), lambda i, blocks=blocks: (0, pick(i, blocks)))
        )
    return pl.pallas_call(
        functools.partial(part_kernel, jobs, len(lefts), len(rights), got is not None),
        grid=(2 * each,),
        in_specs=[
            *[pl.BlockSpec((rows, tokens), lambda i: (0, 0))] * len(lefts),
            *right_specs,
            *(() if got is None else whole),
        ],
        out_specs=out_specs,
        out_shape=out_shape,
        compiler_params=params(),
        name="gradient_parts",
        cost_estimate=pl.CostEstimate(
            flops=4 * each * rows * tokens * chunk,
            bytes_accessed=4 * each * (rows + tokens) * chunk,
            transcendentals=0,
        ),
    )(*lefts, *rights, *(() if got is None else (got,)))


EXPERT_JOBS = ((0, 0, 0), (0, 0, 1), (1, 1, 0), (2, 0, 2), (2, 0, 3), (3, 1, 1))


def flip(index, mask):
    for bit in (1, 2, 4):
        if mask & bit:
            index = index + bit - 2 * bit * (index // bit % 2)
    return index


def mix_kernel(
    dq_ref,
    o_ref,
    n_send,
    n_keep,
    d_send,
    d_keep,
    one_ref,
    two_ref,
    fa_keep,
    fa_got,
    fb_keep,
    fb_got,
    q_keep,
    q_send,
    o_keep,
    o_send,
    got_one,
    far_ref,
    got_two,
    both_ref,
    sent,
    got,
    halves,
    lasts,
    send,
    recv,
):
    d = lax.axis_index("dp")
    z = lax.axis_index("tensor")
    z_count = lax.axis_size("tensor")
    pairs = [{"dp": flip(d, bit)} for bit in (1, 2, 4)]
    others = [{"tensor": (z + m) % z_count} for m in range(1, z_count)]
    barrier = pltpu.get_barrier_semaphore()
    for peer in pairs + others:
        pl.semaphore_signal(barrier, inc=1, device_id=peer, device_id_type=pl.DeviceIdType.MESH)
    pl.semaphore_wait(barrier, len(pairs) + len(others))

    def start(src, dst, at, to):
        copy = pltpu.make_async_remote_copy(
            src_ref=src,
            dst_ref=dst,
            send_sem=send.at[at],
            recv_sem=recv.at[at],
            device_id=to,
            device_id_type=pl.DeviceIdType.MESH,
        )
        copy.start()
        return copy

    step_two = start(two_ref, got_two, 1, others[-1])
    rows = halves.shape[1]
    far_copies = []
    for side, (keep, arrived) in enumerate(((fa_keep, fa_got), (fb_keep, fb_got))):
        total = keep[rows:].astype(F32) + arrived[rows:].astype(F32)
        halves[side] = total.astype(BF16)
        far_copies.append(start(halves.at[side], lasts.at[side], 2 + side, pairs[2 - side]))

    columns = dq_ref.shape[1]
    chunk = columns // 4

    def at_chunk(i):
        return pl.ds(pl.multiple_of(i * chunk, chunk), chunk)

    sides = ((dq_ref, n_send, n_keep, q_keep, q_send), (o_ref, d_send, d_keep, o_keep, o_send))
    core_copies = []
    for side, (right, left, _, _, _) in enumerate(sides):

        def compute_send(i, carry, side=side, right=right, left=left):
            at = at_chunk(i)
            sent[side, :, at] = mm(left[...], right[:, at]).astype(BF16)
            return carry

        lax.fori_loop(0, 4, compute_send, 0)
        core_copies.append(start(sent.at[side], got.at[side], 4 + side, pairs[0]))
        if side == 0:
            step_two.wait()
            both_ref[...] = (one_ref[...].astype(F32) + got_two[...].astype(F32)).astype(BF16)
            step_one = start(both_ref, got_one, 0, others[-1])
    for side, (right, _, left, keep, away) in enumerate(sides):
        core_copies[side].wait()

        def compute_keep(i, carry, side=side, right=right, left=left, keep=keep, away=away):
            at = at_chunk(i)
            value = mm(left[...], right[:, at]) + got[side, :, at].astype(F32)
            half = value.shape[0] // 2
            keep[:, at] = value[:half].astype(BF16)
            away[:, at] = value[half:].astype(BF16)
            return carry

        lax.fori_loop(0, 4, compute_keep, 0)
    for side, (keep, arrived) in enumerate(((fa_keep, fa_got), (fb_keep, fb_got))):
        far_copies[side].wait()
        total = keep[:rows].astype(F32) + arrived[:rows].astype(F32) + lasts[side].astype(F32)
        far_ref[side] = total.astype(BF16)
    step_one.wait()


def mix(dq, o, lefts, dkv_one, dkv_two, far_parts):
    rows2, columns = far_parts[0].shape
    rows = rows2 // 2
    wide = dq.shape[1]
    vmem = pl.BlockSpec(memory_space=pltpu.VMEM)
    half = jax.ShapeDtypeStruct((rows2, wide), BF16)
    block = jax.ShapeDtypeStruct(dkv_one.shape, BF16)
    return pl.pallas_call(
        mix_kernel,
        in_specs=[vmem] * 12,
        out_specs=[vmem] * 6,
        out_shape=[half] * 4 + [block] + [jax.ShapeDtypeStruct((2, rows, columns), BF16)],
        scratch_shapes=[
            pltpu.VMEM(block.shape, BF16),
            pltpu.VMEM(block.shape, BF16),
            pltpu.VMEM((2, 2 * rows2, wide), BF16),
            pltpu.VMEM((2, 2 * rows2, wide), BF16),
            pltpu.VMEM((2, rows, columns), BF16),
            pltpu.VMEM((2, rows, columns), BF16),
            pltpu.SemaphoreType.DMA((6,)),
            pltpu.SemaphoreType.DMA((6,)),
        ],
        compiler_params=pltpu.CompilerParams(
            vmem_limit_bytes=56 * 2**20, collective_id=2, has_side_effects=True
        ),
        name="mix",
    )(dq, o, *lefts, dkv_one, dkv_two, *far_parts)


def finish_kernel(
    dx_ref,
    out_ref,
    q_keep,
    q_send,
    o_keep,
    o_send,
    s_send,
    s_keep,
    back_ref,
    back_out_ref,
    q_ref,
    o_ref,
    s_ref,
    q_got,
    o_got,
    q_half,
    o_half,
    q_last,
    o_last,
    s_got,
    s_half,
    s_got2,
    s_quarter,
    s_last,
    z_mine,
    z_got,
    k_mine,
    k_half,
    k_got,
    deal_send,
    deal_recv,
    send,
    recv,
):
    d = lax.axis_index("dp")
    z = lax.axis_index("tensor")
    count = dx_ref.shape[0]
    z_count = z_mine.shape[0]
    barrier = pltpu.get_barrier_semaphore()
    for p in range(1, count):
        pl.semaphore_signal(
            barrier, inc=1, device_id={"dp": flip(d, p)}, device_id_type=pl.DeviceIdType.MESH
        )
    for m in range(1, z_count):
        pl.semaphore_signal(
            barrier, inc=1, device_id={"tensor": flip(z, m)}, device_id_type=pl.DeviceIdType.MESH
        )
    pl.semaphore_wait(barrier, count - 1 + z_count - 1)

    def start(src, dst, at, to):
        copy = pltpu.make_async_remote_copy(
            src_ref=src,
            dst_ref=dst,
            send_sem=send.at[at],
            recv_sem=recv.at[at],
            device_id=to,
            device_id_type=pl.DeviceIdType.MESH,
        )
        copy.start()
        return copy

    one, two, four = [{"dp": flip(d, bit)} for bit in (1, 2, 4)]
    q_one = start(q_send, q_got, 1, two)
    o_one = start(o_send, o_got, 2, four)
    s_one = start(s_send, s_got, 0, one)
    back_ref[d] = dx_ref[d]
    back_out_ref[d] = out_ref[d]
    rows = q_last.shape[0]
    s_one.wait()
    total = s_keep[...].astype(F32) + s_got[...].astype(F32)
    s_keep2 = total[: 2 * rows]
    s_half[...] = total[2 * rows :].astype(BF16)
    s_two = start(s_half, s_got2, 3, four)
    q_one.wait()
    q_half[...] = (q_keep[rows:].astype(F32) + q_got[rows:].astype(F32)).astype(BF16)
    q_two = start(q_half, q_last, 4, four)
    o_one.wait()
    o_half[...] = (o_keep[rows:].astype(F32) + o_got[rows:].astype(F32)).astype(BF16)
    o_two = start(o_half, o_last, 5, two)
    s_two.wait()
    total = s_keep2 + s_got2[...].astype(F32)
    s_quarter[...] = total[rows:].astype(BF16)
    s_three = start(s_quarter, s_last, 6, two)
    deals = []
    for i, (src, dst) in enumerate(((dx_ref, back_ref), (out_ref, back_out_ref))):
        for p in range(1, count):
            copy = pltpu.make_async_remote_copy(
                src_ref=src.at[flip(d, p)],
                dst_ref=dst.at[d],
                send_sem=deal_send.at[i, p - 1],
                recv_sem=deal_recv.at[i, p - 1],
                device_id={"dp": flip(d, p)},
                device_id_type=pl.DeviceIdType.MESH,
            )
            copy.start()
            deals.append(copy)
    s_own = total[:rows]
    s_three.wait()
    s_own = s_own + s_last[...].astype(F32)
    k_mine[...] = s_own.astype(BF16)
    k_near = start(k_mine, k_got.at[0], 7, {"tensor": flip(z, 1)})
    finals = []
    part = q_ref.shape[1]
    for two_copy, keep, got, last, side in (
        (q_two, q_keep, q_got, q_last, 0),
        (o_two, o_keep, o_got, o_last, 1),
    ):
        two_copy.wait()
        total = (
            keep[:rows].astype(F32) + got[:rows].astype(F32) + last[...].astype(F32)
        )
        for i in range(z_count):
            block = total[:, i * part : (i + 1) * part]
            z_mine[i, :, side * part : (side + 1) * part] = block.astype(BF16)
    for m in range(1, z_count):
        finals.append(start(z_mine.at[flip(z, m)], z_got.at[m - 1], 8 + m, {"tensor": flip(z, m)}))
    k_near.wait()
    s_own = s_own + k_got[0].astype(F32)
    k_half[...] = s_own.astype(BF16)
    k_far = start(k_half, k_got.at[1], 8, {"tensor": flip(z, 2)})
    for copy in finals:
        copy.wait()
    total = z_mine[z].astype(F32)
    for m in range(z_count - 1):
        total = total + z_got[m].astype(F32)
    q_ref[...] = total[:, :part]
    o_ref[...] = total[:, part:]
    k_far.wait()
    s_ref[...] = s_own + k_got[1].astype(F32)
    for copy in deals:
        copy.wait()


def finish(dx, out, q_keep, q_send, o_keep, o_send, s_send, s_keep, z_count):
    count = dx.shape[0]
    rows = q_keep.shape[0] // 2
    columns = q_keep.shape[1]
    small = s_keep.shape[1]
    part = columns // z_count
    vmem = pl.BlockSpec(memory_space=pltpu.VMEM)
    dma = pltpu.SemaphoreType.DMA
    return pl.pallas_call(
        finish_kernel,
        in_specs=[vmem] * 8,
        out_specs=[vmem] * 5,
        out_shape=[
            jax.ShapeDtypeStruct(dx.shape, BF16),
            jax.ShapeDtypeStruct(dx.shape, BF16),
            jax.ShapeDtypeStruct((rows, part), F32),
            jax.ShapeDtypeStruct((rows, part), F32),
            jax.ShapeDtypeStruct((rows, small), F32),
        ],
        scratch_shapes=[
            pltpu.VMEM((2 * rows, columns), BF16),
            pltpu.VMEM((2 * rows, columns), BF16),
            pltpu.VMEM((rows, columns), BF16),
            pltpu.VMEM((rows, columns), BF16),
            pltpu.VMEM((rows, columns), BF16),
            pltpu.VMEM((rows, columns), BF16),
            pltpu.VMEM((4 * rows, small), BF16),
            pltpu.VMEM((2 * rows, small), BF16),
            pltpu.VMEM((2 * rows, small), BF16),
            pltpu.VMEM((rows, small), BF16),
            pltpu.VMEM((rows, small), BF16),
            pltpu.VMEM((z_count, rows, 2 * part), BF16),
            pltpu.VMEM((z_count - 1, rows, 2 * part), BF16),
            pltpu.VMEM((rows, small), BF16),
            pltpu.VMEM((rows, small), BF16),
            pltpu.VMEM((2, rows, small), BF16),
            dma((2, count - 1)),
            dma((2, count - 1)),
            dma((7 + 2 * z_count,)),
            dma((7 + 2 * z_count,)),
        ],
        compiler_params=pltpu.CompilerParams(
            vmem_limit_bytes=56 * 2**20, collective_id=0, has_side_effects=True
        ),
        name="finish",
    )(dx, out, q_keep, q_send, o_keep, o_send, s_send, s_keep)


def assemble_kernel(a_keep, a_got, b_keep, b_got, far_ref, gate_ref, up_ref, down_ref):
    count, rows, columns = gate_ref.shape
    a = a_keep[...] + a_got[...].astype(F32) + far_ref[0].astype(F32)
    b = b_keep[...] + b_got[...].astype(F32) + far_ref[1].astype(F32)
    gate = jnp.concatenate([a[:, :512], a[:, 1024:1536], b[:, 512:1024]], axis=1)
    up = jnp.concatenate([a[:, 512:1024], b[:, :512], b[:, 1024:1536]], axis=1)
    down = jnp.concatenate([a[:, 1536:], b[:, 1536:]], axis=1)
    pad = jnp.zeros((256 - rows, down.shape[1]), F32)
    down = jnp.concatenate([down, pad], axis=0).T[:, :rows]
    for e in range(count):
        at = slice(e * columns, (e + 1) * columns)
        gate_ref[e] = gate[:, at]
        up_ref[e] = up[:, at]
        down_ref[e] = down[at]


def assemble(own, far_sum, count):
    rows, columns = own[0].shape
    part = columns * 2 // (3 * count)
    vmem = pl.BlockSpec(memory_space=pltpu.VMEM)
    wide = jax.ShapeDtypeStruct((count, rows, part), F32)
    return pl.pallas_call(
        assemble_kernel,
        in_specs=[vmem] * 5,
        out_specs=[vmem] * 3,
        out_shape=[wide, wide, jax.ShapeDtypeStruct((count, part, rows), F32)],
        compiler_params=params(),
        name="assemble",
    )(*own, far_sum)


def turn_kernel(orders, d_ref, *refs):
    tiles = len(refs) - 1 - len(orders)
    scratch_ref = refs[-1]
    step = pl.program_id(0)
    for t in range(tiles):

        @pl.when(step == t)
        def _(t=t):
            scratch_ref[...] = refs[t][...].T

    for order, out_ref in zip(orders, refs[tiles:-1]):
        size = out_ref.shape[0] // len(order)
        for i, p in enumerate(order):
            block = jnp.bitwise_xor(d_ref[0], p)
            at = pl.multiple_of(block * size, size)
            out_ref[i * size : (i + 1) * size, :] = scratch_ref[pl.ds(at, size), :]


def turn(d, tiles, orders, blocks):
    rows, width = tiles[0].shape
    size = width // blocks
    return pl.pallas_call(
        functools.partial(turn_kernel, orders),
        grid_spec=pltpu.PrefetchScalarGridSpec(
            num_scalar_prefetch=1,
            grid=(len(tiles),),
            in_specs=[pl.BlockSpec((rows, width), lambda t, s: (0, 0))] * len(tiles),
            out_specs=[
                pl.BlockSpec((len(order) * size, rows), lambda t, s: (0, t)) for order in orders
            ],
            scratch_shapes=[pltpu.VMEM((width, rows), BF16)],
        ),
        out_shape=[
            jax.ShapeDtypeStruct((len(order) * size, rows * len(tiles)), BF16) for order in orders
        ],
        compiler_params=params(),
        name="turn",
        cost_estimate=pl.CostEstimate(
            flops=0, bytes_accessed=6 * rows * width * len(tiles), transcendentals=0
        ),
    )(d, *tiles)


def tie(*values):
    return lax.optimization_barrier(values)


def row_major(x):
    return with_layout_constraint(x, Layout(major_to_minor=tuple(range(x.ndim))))


def per_device(
    tokens,
    perm,
    routes,
    gates,
    lengths,
    cotangent,
    gain_attn,
    w_query,
    w_keyval,
    w_out,
    gain_moe,
    w_gate,
    w_up,
    w_down,
):
    dp_count = lax.axis_size("dp")
    tensor_count = lax.axis_size("tensor")
    d = lax.axis_index("dp")
    z = lax.axis_index("tensor")
    rows, width = tokens.shape
    group_rows = perm.shape[0]
    share = rows // dp_count
    top = routes.shape[1]
    experts_n, _, part_hidden = w_gate.shape
    hidden = experts_n * part_hidden
    capacity = 9 * group_rows * top // (8 * experts_n)
    kv_heads = w_keyval.shape[1] // (2 * HD)
    query_cols = w_query.shape[1]
    team = 8
    teams = [[t * team + i for i in range(team)] for t in range(dp_count // team)]
    teams = None if len(teams) == 1 else teams
    piece_rows = width // team
    member = d % team

    def z_move(x, pairs):
        return lax.ppermute(x, "tensor", pairs)

    def dp_move(x, bit):
        return lax.ppermute(x, "dp", [(i, i ^ bit) for i in range(dp_count)])

    near, far, across = [[(i, i ^ m) for i in range(tensor_count)] for m in (1, 2, 3)]
    up_one, up_two = [[(i, i + m) for i in range(tensor_count - m)] for m in (1, 2)]

    def deal(x):
        return lax.all_to_all(
            x.reshape(dp_count, share, x.shape[1]), "dp", split_axis=0, concat_axis=0, tiled=True
        ).reshape(rows, x.shape[1])

    def team_gather(x):
        return lax.all_gather(x, "dp", axis=0, tiled=True, axis_index_groups=teams)

    def flat(w):
        return w.transpose(0, 2, 1).reshape(hidden, w.shape[1])

    own_perm = lax.dynamic_slice_in_dim(perm, z * rows, rows, 0)
    own_routes = lax.dynamic_slice_in_dim(routes, z * rows, rows, 0)
    dest = own_perm // group_rows
    place = own_perm % rows
    row_index = jnp.arange(rows, dtype=jnp.int32)
    lower = (row_index[:, None] > row_index[None, :]).astype(BF16)
    dest_hot = (dest[:, None] == jnp.arange(dp_count, dtype=jnp.int32)[None, :]).astype(BF16)
    earlier = jnp.sum(mm(lower, dest_hot) * dest_hot.astype(F32), axis=1).astype(jnp.int32)
    slot = dest * share + earlier
    pack = (row_index[:, None] == slot[None, :]).astype(BF16)
    meta = jnp.concatenate(
        [
            (place // 16)[:, None].astype(BF16),
            (place % 16)[:, None].astype(BF16),
            own_routes.astype(BF16),
            gates,
            jnp.zeros((rows, META - 2 - 2 * top), BF16),
        ],
        axis=1,
    )
    packed = mm(pack, jnp.concatenate([tokens, meta], axis=1)).astype(BF16)
    wg_own, wu_own = flat(w_gate), flat(w_up)
    wd_own = w_down.reshape(hidden, width)
    out_rows = query_cols // team
    hidden_piece = hidden // team

    def piece(w, count):
        return lax.dynamic_slice_in_dim(w, member * count, count, 0)

    wg_piece, wu_piece = [piece(w, hidden_piece) for w in (wg_own, wu_own)]
    packed_dy = mm(pack, cotangent).astype(BF16)
    packed, packed_dy = tie(packed, packed_dy)
    arrived, wq_z, wo_z = open_moves(
        packed.reshape(dp_count, share, width + META),
        piece(w_query, piece_rows),
        piece(w_out, out_rows),
        tensor_count,
    )
    arrived, wg_piece, wu_piece = tie(arrived.reshape(rows, width + META), wg_piece, wu_piece)
    wg_moved, wu_moved = z_move(wg_piece, far), z_move(wu_piece, far)
    wq_all = team_gather(wq_z).reshape(team, tensor_count, piece_rows, query_cols)
    wo_all = team_gather(wo_z).reshape(team, tensor_count, out_rows, width)
    wo = wo_all.transpose(1, 0, 2, 3).reshape(tensor_count * query_cols, width)

    meta_in = arrived[:, width:].astype(F32)
    place_in = (meta_in[:, 0] * 16.0 + meta_in[:, 1]).astype(jnp.int32)
    unpack = (row_index[:, None] == place_in[None, :]).astype(BF16)
    dealt = mm(unpack, arrived)
    x_rows = dealt[:, :width]
    meta_rows = dealt[:, width:]

    expert_ids = jnp.arange(experts_n, dtype=jnp.int32).astype(F32)
    route_rows = meta_rows[:, 2 : 2 + top]
    gate_rows = meta_rows[:, 2 + top : 2 + 2 * top]
    hot = route_rows[:, :, None] == expert_ids[None, None, :]
    routed = jnp.sum(hot.astype(F32), axis=1)
    counts = jnp.pad(jnp.sum(routed, axis=0)[None, :], ((0, 7), (0, HD - experts_n)))

    seq_lengths = lengths[0]
    seq_index = jnp.arange(seq_lengths.shape[0], dtype=jnp.int32)
    seq_ends = jnp.sum(
        jnp.where(seq_index[None, :] <= seq_index[:, None], seq_lengths[None, :], 0), axis=1
    ).astype(jnp.int32)
    global_row = z * rows + row_index
    start = jnp.max(
        jnp.where(global_row[:, None] >= seq_ends[None, :], seq_ends[None, :], 0), axis=1
    ).astype(jnp.int32)
    offset = (global_row - start).astype(F32)
    frequency = ROPE_BASE ** (-2.0 * jnp.arange(HD // 2, dtype=F32) / HD)
    angles = offset[:, None] * frequency[None, :]
    cosine, sine = jnp.cos(angles), jnp.sin(angles)
    cos_full = jnp.concatenate([cosine, cosine], axis=1)
    sin_full = jnp.concatenate([-sine, sine], axis=1)
    start = start[:, None]
    z_arg = z.astype(jnp.int32)[None]

    inv_one = lax.rsqrt(jnp.mean(x_rows * x_rows, axis=1, keepdims=True) + EPS)
    n1 = (x_rows * inv_one * gain_attn).astype(BF16)
    weight = jnp.sum(jnp.where(hot, gate_rows[:, :, None], 0.0), axis=1)
    marks = jnp.pad(
        jnp.concatenate([routed, weight], axis=1).astype(BF16), ((0, 0), (0, HD - 2 * experts_n))
    )
    kv, kv_one, kv_two, counts, marks_near, arrived_dy = keyval(
        n1,
        w_keyval,
        cos_full,
        sin_full,
        counts,
        marks,
        packed_dy.reshape(dp_count, share, width),
        tensor_count,
    )
    arrived_dy = arrived_dy.reshape(rows, width)
    kv, n1, wg_moved, wu_moved = tie(kv, n1, wg_moved, wu_moved)

    dy_rows = mm(unpack, arrived_dy).astype(BF16)
    n1, dy_rows = tie(n1, dy_rows)
    q = project_query(z_arg, n1, wq_all, cos_full, sin_full)
    dy_near = z_move(dy_rows, near)
    kvs = (kv_two, kv_one, kv)
    o, lse = attend(z_arg, start, q, kvs, kv_heads)
    o, dy_near = tie(o, dy_near)
    wg_far = team_gather(wg_moved)
    wu_far = team_gather(wu_moved)
    h = x_rows + mm(o, wo)
    inv_two = lax.rsqrt(jnp.mean(h * h, axis=1, keepdims=True) + EPS)
    n2 = (h * inv_two * gain_moe).astype(BF16)

    halving = dp_count == 8
    d_arg = d.astype(jnp.int32)[None]
    out_w = width // dp_count
    orders_a = ((1, 5, 3, 7), (0, 4, 2, 6))
    orders_b = ((1, 3, 5, 7), (0, 2, 4, 6))

    def turned(tiles, *orders):
        if halving:
            return turn(d_arg, tiles, orders, dp_count)
        return [jnp.concatenate(tiles, axis=0).T] * len(orders)

    def dp_sum(x):
        return lax.psum_scatter(x, "dp", scatter_dimension=0, tiled=True)

    def first_moves(parts):
        return parts[0], dp_move(parts[1], xy[0]), parts[2], dp_move(parts[3], yx[0])

    def second_moves(moved):
        halves = []
        for keep, got, bit in ((*moved[:2], xy[1]), (*moved[2:], yx[1])):
            x = keep.astype(F32) + got.astype(F32)
            half = x.shape[0] // 2
            halves += [x[:half], dp_move(x[half:].astype(BF16), bit)]
        return halves

    def expert_lefts(n_a, d_a, keep):
        return n_a[keep], d_a[keep], n_a[2 + keep], d_a[2 + keep]

    xy, yx = (2, 4), (4, 2)
    n2, counts, weight, marks_near = tie(n2, counts, weight, marks_near)
    n2_near = z_move(n2, near)

    def kept_gates(routed, weight, at):
        block = (z - 1 - jnp.arange(tensor_count, dtype=jnp.int32)) % tensor_count
        base = jnp.sum(
            jnp.where((block < at)[:, None], counts[:, 0, :experts_n], 0.0), axis=0
        )
        position = mm(lower, routed.astype(BF16)) + base[None, :]
        weight = jnp.where(position < capacity, weight, 0.0).astype(BF16)
        return row_major(jnp.repeat(weight, part_hidden, axis=1))

    gate_own = kept_gates(routed, weight, z)
    marks_near = marks_near.astype(F32)
    gate_near = kept_gates(
        marks_near[:, :experts_n], marks_near[:, experts_n : 2 * experts_n], z + 1 - 2 * (z % 2)
    )
    y, dn2, *own_grads = experts(0, n2, dy_rows, gate_own, wg_own, wu_own, wd_own)
    y, n1 = tie(y, n1)
    n1_t = turned((n1,), *orders_a, *orders_b)
    n2_near, y, wd_source = tie(n2_near, y, wd_own)
    wd_piece = piece(wd_source, hidden_piece)
    n2_a = turned((n2, n2_near), *orders_a, *orders_b)
    dy_near, *turns = tie(dy_near, *n2_a, *n1_t)
    n2_a, n1_t = turns[:4], turns[4:]
    wd_moved = z_move(wd_piece, far)
    yn, dnn, *own_grads = experts(
        1, n2_near, dy_near, gate_near, wg_own, wu_own, wd_own, filled=own_grads
    )
    yn, wd_moved, *own_grads = tie(yn, wd_moved, *own_grads)
    wd_far = team_gather(wd_moved)
    dy_a = turned((dy_rows, dy_near), *orders_a, *orders_b)
    if halving:
        own = gradients(
            EXPERT_JOBS,
            expert_lefts(n2_a, dy_a, 0),
            expert_lefts(n2_a, dy_a, 1),
            own_grads[::-1],
            3,
        )
        wg_far, *own = tie(wg_far, *own)
        own = first_moves(own)
    yn, dnn, *far_grads = experts(
        1, n2_near, dy_near, gate_near, wg_far, wu_far, wd_far, (yn, dnn), last=True
    )
    dnn_moved = z_move(dnn, near)
    y, dn2, *far_grads = experts(
        0, n2, dy_rows, gate_own, wg_far, wu_far, wd_far, (y, dn2), far_grads
    )
    if halving:
        far_grads = far_grads[::-1]
        far_sent = gradient_parts(EXPERT_JOBS, expert_lefts(n2_a, dy_a, 0), far_grads)
        dnn_moved, far_sent, *own = tie(dnn_moved, far_sent, *own)
        got = dp_move(far_sent, 1)
        own = second_moves(own)
    yn, dnn_moved = tie(yn, dnn_moved)
    yn_moved = z_move(yn, near)
    dn2 = dn2 + dnn_moved.astype(F32)

    gain_two_part = jnp.sum(dn2 * h * inv_two, axis=0)
    u2 = dn2 * gain_moe
    dh = dy_rows.astype(F32) + inv_two * (
        u2 - h * inv_two * inv_two * jnp.mean(u2 * h, axis=1, keepdims=True)
    )
    dhb = dh.astype(BF16)
    do = mm_nt(dhb, wo).astype(BF16)
    if halving:
        far_w = gradient_parts(EXPERT_JOBS, expert_lefts(n2_a, dy_a, 1), far_grads, got)
        do, *both = tie(do, *far_w, *own)
        far_w, own = both[:4], both[4:]
        far_w = first_moves(far_w)
    dq, dkv_two, dkv_one, dkv = attend_back(
        z_arg, start, q, o, do, lse, cos_full, sin_full, kvs, kv_heads
    )
    dhb_t = turned((dhb,), *orders_b)
    if halving:
        dq, *far_w = tie(dq, *far_w)
        *parts, dkv_sum, far_sum = mix(
            dq, o, (n1_t[0], n1_t[1], *dhb_t), dkv_one, dkv_two, far_w
        )
        far_sum = z_move(far_sum, far)
        dkv_sum, yn_moved = tie(dkv_sum, yn_moved)
    else:
        dkv_one = z_move(dkv_one, [(b, a) for a, b in up_one])
        dkv_two = z_move(dkv_two, [(b, a) for a, b in up_two])
        dkv_sum = dkv_one.astype(F32) + dkv_two.astype(F32)
        sum_q, sum_o = [
            dp_sum(mm_tn(a, b).astype(BF16)).astype(F32) for a, b in ((n1, dq), (dhb, o))
        ]
    dkv = dkv + dkv_sum.astype(F32)

    def unrotate(u):
        swapped = jnp.concatenate([u[:, HD // 2 :], u[:, : HD // 2]], axis=1)
        return u * cos_full - swapped * sin_full

    dkv = jnp.concatenate(
        [unrotate(dkv[:, i * HD : (i + 1) * HD]) for i in range(kv_heads)]
        + [dkv[:, kv_heads * HD :]],
        axis=1,
    ).astype(BF16)
    dn1 = project_back(z_arg, dq, wq_all, dkv, w_keyval)
    gain_one_part = jnp.sum(dn1 * x_rows * inv_one, axis=0)
    u1 = dn1 * gain_attn
    dx = dh + inv_one * (
        u1 - x_rows * inv_one * inv_one * jnp.mean(u1 * x_rows, axis=1, keepdims=True)
    )

    result = h + y + yn_moved.astype(F32)
    result_out = mm_tn(unpack, result.astype(BF16)).astype(BF16)

    if halving:
        sum_gate, sum_up, sum_down = assemble(own, far_sum, experts_n)
    else:
        lefts = (n2_a[0], dy_a[0])
        far_sums = [dp_sum(mm(a, b).astype(BF16)) for a, b in zip(lefts, far_grads[::-1])]
        own_sums = [dp_sum(mm(a, b).astype(BF16)) for a, b in zip(lefts, own_grads[::-1])]
        sum_gu, sum_down = [
            a.astype(F32) + z_move(b, far).astype(F32) for a, b in zip(own_sums, far_sums)
        ]
        sum_gu = sum_gu.reshape(out_w, hidden // 512, 2, 512)
        sum_gate, sum_up = [
            sum_gu[:, :, i].reshape(out_w, experts_n, part_hidden).transpose(1, 0, 2) for i in (0, 1)
        ]
        sum_down = sum_down.reshape(out_w, experts_n, part_hidden).transpose(1, 2, 0)

    gains = jnp.stack([gain_one_part, gain_two_part])

    def gain_columns(order):
        blocks = gains.reshape(2, dp_count, out_w)
        if halving:
            blocks = jnp.stack(
                [lax.dynamic_index_in_dim(blocks, d ^ p, 1, keepdims=False) for p in order], 1
            )
        return jnp.pad(blocks.reshape(2, -1).T, ((0, 0), (dkv.shape[1], HD - 2)))

    columns = [gain_columns(order) for order in orders_b]
    dkv_wide = jnp.pad(dkv, ((0, 0), (0, HD)))
    if halving:
        kv_send, kv_keep = [
            (mm(left, dkv_wide) + column).astype(BF16) for left, column in zip(n1_t[2:], columns)
        ]
        dx_out = mm_tn(unpack, dx.astype(BF16)).astype(BF16).reshape(dp_count, share, width)
        back, back_out, sum_query, sum_out, small = finish(
            dx_out,
            result_out.reshape(dp_count, share, width),
            *parts,
            kv_send,
            kv_keep,
            tensor_count,
        )
        grad_tokens = mm_tn(pack, back.reshape(rows, width)).astype(BF16)
        outputs = mm_tn(pack, back_out.reshape(rows, width)).astype(BF16)
    else:
        outputs = mm_tn(pack, deal(result_out)).astype(BF16)
        grad_tokens = mm_tn(pack, deal(mm_tn(unpack, dx.astype(BF16)).astype(BF16))).astype(BF16)
        small = dp_sum((mm(n1_t[3], dkv_wide) + columns[0]).astype(BF16))
        small = small.astype(F32) + sum(
            z_move(small, move).astype(F32) for move in (near, far, across)
        )

        def z_block(x, m):
            return lax.dynamic_slice_in_dim(x, (z ^ m) * query_cols, query_cols, 1)

        both = [jnp.concatenate([z_block(sum_q, m), z_block(sum_o, m)], axis=1) for m in range(4)]
        total = both[0] + sum(
            z_move(part.astype(BF16), move).astype(F32)
            for part, move in zip(both[1:], (near, far, across))
        )
        sum_query, sum_out = total[:, :query_cols], total[:, query_cols:]
    sum_out = sum_out.T
    kv_cols = w_keyval.shape[1]
    return (
        outputs,
        grad_tokens,
        small[:, kv_cols],
        sum_query,
        small[:, :kv_cols],
        sum_out,
        small[:, kv_cols + 1],
        sum_gate,
        sum_up,
        sum_down,
    )


def solution(mesh):
    in_specs = (
        P(("dp", "tensor"), None),
        P("dp"),
        P("dp", None),
        P(("dp", "tensor"), None),
        P("dp", None),
        P(("dp", "tensor"), None),
        P(),
        P(None, "tensor"),
        P(),
        P("tensor", None),
        P(),
        P(None, None, "tensor"),
        P(None, None, "tensor"),
        P(None, "tensor", None),
    )
    out_specs = (
        P(("dp", "tensor"), None),
        P(("dp", "tensor"), None),
        P("dp"),
        P("dp", "tensor"),
        P("dp", None),
        P("tensor", "dp"),
        P("dp"),
        P(None, "dp", "tensor"),
        P(None, "dp", "tensor"),
        P(None, "tensor", "dp"),
    )
    return jax.shard_map(
        per_device, mesh=mesh, in_specs=in_specs, out_specs=out_specs, check_vma=False
    )
```

```python
import functools

import jax
import jax.numpy as jnp
from jax import lax
from jax.experimental import pallas as pl
from jax.experimental.layout import Layout, with_layout_constraint
from jax.experimental.pallas import tpu as pltpu
from jax.sharding import PartitionSpec as P

HD = 128
EPS = 1e-06
ROPE_BASE = 1000000.0
MASKED = -1e30
LOG2E = 1.4426950408889634
F32 = jnp.float32
BF16 = jnp.bfloat16
META = 128


def mm(a, b):
    return lax.dot_general(a, b, (((1,), (0,)), ((), ())), preferred_element_type=F32)


def mm_nt(a, b):
    return lax.dot_general(a, b, (((1,), (1,)), ((), ())), preferred_element_type=F32)


def mm_tn(a, b):
    return lax.dot_general(a, b, (((0,), (0,)), ((), ())), preferred_element_type=F32)


def params(mb=56):
    return pltpu.CompilerParams(vmem_limit_bytes=mb * 2**20)


def swap_halves(u):
    return pltpu.roll(u, HD // 2, 1)


def open_kernel(
    deal_ref,
    q_ref,
    o_ref,
    dealt_ref,
    q_all,
    o_all,
    send,
    recv,
    deal_send,
    deal_recv,
):
    z = lax.axis_index("tensor")
    d = lax.axis_index("dp")
    d_count = deal_ref.shape[0]
    z_count = q_all.shape[0]
    others = [{"tensor": flip(z, m)} for m in range(1, z_count)]
    peers = [{"dp": (d + p) % d_count} for p in range(1, d_count)]
    barrier = pltpu.get_barrier_semaphore()
    for other in others + peers:
        pl.semaphore_signal(barrier, inc=1, device_id=other, device_id_type=pl.DeviceIdType.MESH)
    pl.semaphore_wait(barrier, len(others) + len(peers))
    moves = [(q_ref, q_all.at[m], others[m - 1]) for m in range(1, z_count)]
    moves += [(o_ref, o_all.at[z], other) for other in others]
    copies = []
    for p, peer in enumerate(peers):
        copy = pltpu.make_async_remote_copy(
            src_ref=deal_ref.at[(d + p + 1) % d_count],
            dst_ref=dealt_ref.at[d],
            send_sem=deal_send.at[p],
            recv_sem=deal_recv.at[p],
            device_id=peer,
            device_id_type=pl.DeviceIdType.MESH,
        )
        copy.start()
        copies.append(copy)
    for at, (src, dst, to) in enumerate(moves):
        copy = pltpu.make_async_remote_copy(
            src_ref=src,
            dst_ref=dst,
            send_sem=send.at[at],
            recv_sem=recv.at[at],
            device_id=to,
            device_id_type=pl.DeviceIdType.MESH,
        )
        copy.start()
        copies.append(copy)
    dealt_ref[d] = deal_ref[d]
    q_all[0] = q_ref[...]
    o_all[z] = o_ref[...]
    for copy in copies:
        copy.wait()


def open_moves(deals, q, o, z_count):
    vmem = pl.BlockSpec(memory_space=pltpu.VMEM)
    shapes = [deals.shape, (z_count, *q.shape), (z_count, *o.shape)]
    moves = 2 * (z_count - 1)
    return pl.pallas_call(
        open_kernel,
        in_specs=[vmem] * 3,
        out_specs=[vmem] * 3,
        out_shape=[jax.ShapeDtypeStruct(shape, BF16) for shape in shapes],
        scratch_shapes=[
            pltpu.SemaphoreType.DMA((moves,)),
            pltpu.SemaphoreType.DMA((moves,)),
            pltpu.SemaphoreType.DMA((deals.shape[0] - 1,)),
            pltpu.SemaphoreType.DMA((deals.shape[0] - 1,)),
        ],
        compiler_params=pltpu.CompilerParams(
            vmem_limit_bytes=40 * 2**20, collective_id=4, has_side_effects=True
        ),
        name="open_moves",
    )(deals, q, o)


def keyval_kernel(
    x_ref,
    w_ref,
    cos_ref,
    sin_ref,
    count_ref,
    mark_ref,
    deal_ref,
    kv_ref,
    one_ref,
    two_ref,
    counts_ref,
    near_ref,
    dealt_ref,
    send,
    recv,
    deal_send,
    deal_recv,
):
    z = lax.axis_index("tensor")
    d = lax.axis_index("dp")
    d_count = deal_ref.shape[0]
    z_count = counts_ref.shape[0]
    others = [{"tensor": (z + m) % z_count} for m in range(1, z_count)]
    barrier = pltpu.get_barrier_semaphore()
    peers = [{"dp": (d + p) % d_count} for p in range(1, d_count)]
    for other in others + peers:
        pl.semaphore_signal(barrier, inc=1, device_id=other, device_id_type=pl.DeviceIdType.MESH)
    raw = mm(x_ref[...], w_ref[...])
    turned = raw.shape[1] // 2
    for i in range(turned // HD):
        u = raw[:, i * HD : (i + 1) * HD]
        u = u * cos_ref[...] + swap_halves(u) * sin_ref[...]
        kv_ref[:, i * HD : (i + 1) * HD] = u.astype(BF16)
    kv_ref[:, turned:] = raw[:, turned:].astype(BF16)
    pl.semaphore_wait(barrier, z_count - 1 + d_count - 1)
    moves = [(count_ref, counts_ref.at[m], others[m]) for m in range(z_count - 1)]
    moves += [(mark_ref, near_ref, {"tensor": flip(z, 1)})]
    moves += [(kv_ref, one_ref, others[0]), (one_ref, two_ref, others[0])]
    copies = []
    for at, (src, dst, to) in enumerate(moves):
        copy = pltpu.make_async_remote_copy(
            src_ref=src,
            dst_ref=dst,
            send_sem=send.at[at],
            recv_sem=recv.at[at],
            device_id=to,
            device_id_type=pl.DeviceIdType.MESH,
        )
        copies.append(copy)
    for copy in copies[:-1]:
        copy.start()
    for p, peer in enumerate(peers):
        copy = pltpu.make_async_remote_copy(
            src_ref=deal_ref.at[(d + p + 1) % d_count],
            dst_ref=dealt_ref.at[d],
            send_sem=deal_send.at[p],
            recv_sem=deal_recv.at[p],
            device_id=peer,
            device_id_type=pl.DeviceIdType.MESH,
        )
        copy.start()
        copies.append(copy)
    counts_ref[z_count - 1] = count_ref[...]
    dealt_ref[d] = deal_ref[d]
    step_one, step_two = copies[z_count], copies[z_count + 1]
    step_one.wait()
    step_two.start()
    for copy in copies[:z_count] + copies[z_count + 1 :]:
        copy.wait()


def keyval(x, w, cos_full, sin_full, counts, marks, deals, z_count):
    rows = x.shape[0]
    columns = w.shape[1]
    vmem = pl.BlockSpec(memory_space=pltpu.VMEM)
    block = jax.ShapeDtypeStruct((rows, columns), BF16)
    return pl.pallas_call(
        keyval_kernel,
        in_specs=[vmem] * 7,
        out_specs=[vmem] * 6,
        out_shape=[block] * 3
        + [
            jax.ShapeDtypeStruct((z_count, *counts.shape), counts.dtype),
            jax.ShapeDtypeStruct(marks.shape, marks.dtype),
            jax.ShapeDtypeStruct(deals.shape, deals.dtype),
        ],
        scratch_shapes=[
            pltpu.SemaphoreType.DMA((z_count + 2,)),
            pltpu.SemaphoreType.DMA((z_count + 2,)),
            pltpu.SemaphoreType.DMA((deals.shape[0] - 1,)),
            pltpu.SemaphoreType.DMA((deals.shape[0] - 1,)),
        ],
        compiler_params=pltpu.CompilerParams(
            vmem_limit_bytes=40 * 2**20, collective_id=1, has_side_effects=True
        ),
        name="keyval",
    )(x, w, cos_full, sin_full, counts, marks, deals)


def project_query_kernel(z_ref, x_ref, w_ref, cos_ref, sin_ref, out_ref):
    raw = mm(x_ref[...], w_ref[...].reshape(x_ref.shape[1], out_ref.shape[1]))
    for i in range(raw.shape[1] // HD):
        u = raw[:, i * HD : (i + 1) * HD]
        turned = u * cos_ref[...] + swap_halves(u) * sin_ref[...]
        out_ref[:, i * HD : (i + 1) * HD] = (turned * SCALE).astype(BF16)


def project_query(z, x, w, cos_full, sin_full):
    rows, width = x.shape
    pieces, blocks, piece, columns = w.shape
    return pl.pallas_call(
        project_query_kernel,
        grid_spec=pltpu.PrefetchScalarGridSpec(
            num_scalar_prefetch=1,
            grid=(blocks,),
            in_specs=[
                pl.BlockSpec((rows, width), lambda i, s: (0, 0)),
                pl.BlockSpec(
                    (pieces, 1, piece, columns), lambda i, s: (0, jnp.bitwise_xor(i, s[0]), 0, 0)
                ),
                pl.BlockSpec((rows, HD), lambda i, s: (0, 0)),
                pl.BlockSpec((rows, HD), lambda i, s: (0, 0)),
            ],
            out_specs=pl.BlockSpec((rows, columns), lambda i, s: (0, i)),
        ),
        out_shape=jax.ShapeDtypeStruct((rows, blocks * columns), BF16),
        compiler_params=params(),
        name="project_query",
        cost_estimate=pl.CostEstimate(
            flops=2 * rows * width * blocks * columns,
            bytes_accessed=2 * (2 * rows * width + width * blocks * columns),
            transcendentals=0,
        ),
    )(z, x, w, cos_full, sin_full)


def project_back_kernel(z_ref, dq_ref, w_ref, dkv_ref, wkv_ref, out_ref):
    step = pl.program_id(0)
    width = out_ref.shape[1]
    part = mm_nt(dq_ref[...], w_ref[...].reshape(width, dq_ref.shape[1]))

    @pl.when(step == 0)
    def _():
        out_ref[...] = part + mm_nt(dkv_ref[...], wkv_ref[...])

    @pl.when(step > 0)
    def _():
        out_ref[...] += part


def project_back(z, dq, w, dkv, wkv):
    rows = dq.shape[0]
    pieces, blocks, piece, columns = w.shape
    width = pieces * piece
    return pl.pallas_call(
        project_back_kernel,
        grid_spec=pltpu.PrefetchScalarGridSpec(
            num_scalar_prefetch=1,
            grid=(blocks,),
            in_specs=[
                pl.BlockSpec((rows, columns), lambda i, s: (0, i)),
                pl.BlockSpec(
                    (pieces, 1, piece, columns), lambda i, s: (0, jnp.bitwise_xor(i, s[0]), 0, 0)
                ),
                pl.BlockSpec(dkv.shape, lambda i, s: (0, 0)),
                pl.BlockSpec(wkv.shape, lambda i, s: (0, 0)),
            ],
            out_specs=pl.BlockSpec((rows, width), lambda i, s: (0, 0)),
        ),
        out_shape=jax.ShapeDtypeStruct((rows, width), F32),
        compiler_params=params(),
        name="project_back",
        cost_estimate=pl.CostEstimate(
            flops=2 * rows * width * (blocks * columns + dkv.shape[1]),
            bytes_accessed=2 * width * (3 * rows + blocks * columns),
            transcendentals=0,
        ),
    )(z, dq, w, dkv, wkv)


ATTEND_TILE = 256
SCALE = HD**-0.5 * LOG2E


def make_bias(z, start_ref, bias_ref):
    tiles, tile, width = bias_ref.shape
    rows = tiles * tile
    for i in range(tiles):
        key = (z - 2) * rows + i * tile + lax.broadcasted_iota(jnp.int32, (tile, width), 1)
        query = z * rows + i * tile + lax.broadcasted_iota(jnp.int32, (tile, width), 0)
        allowed = (key >= start_ref[i * tile : (i + 1) * tile]) & (key <= query)
        bias_ref[i] = jnp.where(allowed, 0.0, MASKED)


def attend_kernel(
    kv_heads, z_ref, start_ref, q_ref, kv0_ref, kv1_ref, kv2_ref, o_ref, lse_ref, bias_ref, k_ref, v_ref
):
    head = pl.program_id(0)
    each = pl.num_programs(0) // kv_heads
    rows = q_ref.shape[0]
    tiles, tile, width = bias_ref.shape

    @pl.when(head == 0)
    def _():
        make_bias(z_ref[0], start_ref, bias_ref)
        v_ref[:, HD:] = jnp.ones((v_ref.shape[0], HD), BF16)

    @pl.when(head % each == 0)
    def _():
        kvh = head // each
        for j, ref in enumerate((kv0_ref, kv1_ref, kv2_ref)):
            at = slice(j * rows, (j + 1) * rows)
            k_ref[at] = ref[:, pl.ds(pl.multiple_of(kvh * HD, HD), HD)]
            v_ref[at, :HD] = ref[:, pl.ds(pl.multiple_of((kv_heads + kvh) * HD, HD), HD)]

    for i in range(tiles):
        at, window = slice(i * tile, (i + 1) * tile), slice(i * tile, i * tile + width)
        score = mm_nt(q_ref[at], k_ref[window]) + bias_ref[i]
        peak = jnp.max(score, axis=1, keepdims=True)
        mixed = mm(jnp.exp2(score - peak).astype(BF16), v_ref[window])
        total = mixed[:, HD : HD + 1]
        o_ref[at] = (mixed[:, :HD] / total).astype(BF16)
        lse_ref[0, at] = peak + jnp.log2(total)


def attend(z, start, q, kvs, kv_heads):
    rows, columns = q.shape
    heads = columns // HD
    tile = ATTEND_TILE
    kv_spec = pl.BlockSpec(kvs[0].shape, lambda h, s: (0, 0))
    return pl.pallas_call(
        functools.partial(attend_kernel, kv_heads),
        grid_spec=pltpu.PrefetchScalarGridSpec(
            num_scalar_prefetch=1,
            grid=(heads,),
            in_specs=[
                pl.BlockSpec((rows, 1), lambda h, s: (0, 0)),
                pl.BlockSpec((rows, HD), lambda h, s: (0, h)),
                *[kv_spec] * 3,
            ],
            out_specs=[
                pl.BlockSpec((rows, HD), lambda h, s: (0, h)),
                pl.BlockSpec((1, rows, 1), lambda h, s: (h, 0, 0)),
            ],
            scratch_shapes=[
                pltpu.VMEM((rows // tile, tile, 2 * rows + tile), F32),
                pltpu.VMEM((3 * rows, HD), BF16),
                pltpu.VMEM((3 * rows, 2 * HD), BF16),
            ],
        ),
        out_shape=[
            jax.ShapeDtypeStruct((rows, columns), BF16),
            jax.ShapeDtypeStruct((heads, rows, 1), F32),
        ],
        compiler_params=params(),
        name="attend",
        cost_estimate=pl.CostEstimate(
            flops=12 * rows * rows * columns,
            bytes_accessed=8 * rows * columns,
            transcendentals=rows * rows * 3 * heads,
        ),
    )(z, start, q, *kvs)


def attend_back_kernel(
    kv_heads,
    z_ref,
    start_ref,
    q_ref,
    o_ref,
    do_ref,
    lse_ref,
    cos_ref,
    sin_ref,
    kv0_ref,
    kv1_ref,
    kv2_ref,
    dq_ref,
    d0_ref,
    d1_ref,
    d2_ref,
    bias_ref,
    k_ref,
    v_ref,
    dk_ref,
    dv_ref,
):
    head = pl.program_id(0)
    each = pl.num_programs(0) // kv_heads
    rows = q_ref.shape[0]
    tiles, tile, width = bias_ref.shape
    kvh = head // each
    kcol = pl.ds(pl.multiple_of(kvh * HD, HD), HD)
    vcol = pl.ds(pl.multiple_of((kv_heads + kvh) * HD, HD), HD)

    @pl.when(head == 0)
    def _():
        make_bias(z_ref[0], start_ref, bias_ref)

    @pl.when(head % each == 0)
    def _():
        for j, ref in enumerate((kv0_ref, kv1_ref, kv2_ref)):
            k_ref[j * rows : (j + 1) * rows] = ref[:, kcol]
            v_ref[j * rows : (j + 1) * rows] = ref[:, vcol]
        dk_ref[...] = jnp.zeros_like(dk_ref)
        dv_ref[...] = jnp.zeros_like(dv_ref)

    for i in range(tiles):
        at, window = slice(i * tile, (i + 1) * tile), slice(i * tile, i * tile + width)
        q = q_ref[at]
        do = do_ref[at]
        centre = jnp.sum(do.astype(F32) * o_ref[at].astype(F32), axis=1, keepdims=True)
        soft = jnp.exp2(mm_nt(q, k_ref[window]) + (bias_ref[i] - lse_ref[0, at]))
        dv_ref[window] += mm_tn(soft.astype(BF16), do)
        dscore = (soft * (mm_nt(do, v_ref[window]) - centre)).astype(BF16)
        dk_ref[window] += mm_tn(dscore, q)
        dq = mm(dscore, k_ref[window]) * (HD**-0.5)
        dq_ref[at] = (dq * cos_ref[at] - swap_halves(dq) * sin_ref[at]).astype(BF16)

    @pl.when(head % each == each - 1)
    def _():
        for j, ref in enumerate((d0_ref, d1_ref, d2_ref)):
            at = slice(j * rows, (j + 1) * rows)
            ref[:, kcol] = (dk_ref[at] * (1 / LOG2E)).astype(ref.dtype)
            ref[:, vcol] = dv_ref[at].astype(ref.dtype)


def attend_back(z, start, q, o, do, lse, cos_full, sin_full, kvs, kv_heads):
    rows, columns = q.shape
    heads = columns // HD
    tile = ATTEND_TILE
    kv_columns = kvs[0].shape[1]
    kv_spec = pl.BlockSpec((rows, kv_columns), lambda h, s: (0, 0))
    head_spec = pl.BlockSpec((rows, HD), lambda h, s: (0, h))
    table_spec = pl.BlockSpec((rows, HD), lambda h, s: (0, 0))
    return pl.pallas_call(
        functools.partial(attend_back_kernel, kv_heads),
        grid_spec=pltpu.PrefetchScalarGridSpec(
            num_scalar_prefetch=1,
            grid=(heads,),
            in_specs=[
                pl.BlockSpec((rows, 1), lambda h, s: (0, 0)),
                head_spec,
                head_spec,
                head_spec,
                pl.BlockSpec((1, rows, 1), lambda h, s: (h, 0, 0)),
                table_spec,
                table_spec,
                *[kv_spec] * 3,
            ],
            out_specs=[head_spec, *[kv_spec] * 3],
            scratch_shapes=[
                pltpu.VMEM((rows // tile, tile, 2 * rows + tile), F32),
                pltpu.VMEM((3 * rows, HD), BF16),
                pltpu.VMEM((3 * rows, HD), BF16),
                pltpu.VMEM((3 * rows, HD), F32),
                pltpu.VMEM((3 * rows, HD), F32),
            ],
        ),
        out_shape=[
            jax.ShapeDtypeStruct((rows, columns), BF16),
            jax.ShapeDtypeStruct((rows, kv_columns), BF16),
            jax.ShapeDtypeStruct((rows, kv_columns), BF16),
            jax.ShapeDtypeStruct((rows, kv_columns), F32),
        ],
        compiler_params=params(),
        name="attend_back",
        cost_estimate=pl.CostEstimate(
            flops=30 * rows * rows * columns,
            bytes_accessed=12 * rows * columns,
            transcendentals=rows * rows * 3 * heads,
        ),
    )(z, start, q, o, do, lse, cos_full, sin_full, *kvs)


def expert_kernel(chunk, first, last, x_ref, dy_ref, gate_ref, wg_ref, wu_ref, wd_ref, *refs):
    if last:
        y_out, dn_out, hs_ref, dgu_ref, y_ref, dn_ref = refs[-6:]
    else:
        y_ref, dn_ref, hs_ref, dgu_ref = refs[-4:]
    step = pl.program_id(0)

    @pl.when(step == 0)
    def _():
        if first:
            y_ref[...] = jnp.zeros_like(y_ref)
            dn_ref[...] = jnp.zeros_like(dn_ref)
        else:
            y_ref[...] = refs[0][...]
            dn_ref[...] = refs[1][...]

    x = x_ref[...]
    gate = gate_ref[...].astype(F32)
    g = jnp.maximum(mm_nt(x, wg_ref[...]), 0.0)
    u = mm_nt(x, wu_ref[...])
    square = g * g
    hs = ((square * u).astype(BF16).astype(F32) * gate).astype(BF16)
    hs_ref[...] = hs
    dh = mm_nt(dy_ref[...], wd_ref[...]) * gate
    dg = (dh * u * (2.0 * g)).astype(BF16)
    du = (dh * square).astype(BF16)
    dgu_ref[:, :chunk] = dg
    dgu_ref[:, chunk:] = du
    dn_ref[...] += mm(dg, wg_ref[...]) + mm(du, wu_ref[...])
    y_ref[...] += mm(hs, wd_ref[...])
    if last:

        @pl.when(step == pl.num_programs(0) - 1)
        def _():
            y_out[...] = y_ref[...].astype(BF16)
            dn_out[...] = dn_ref[...].astype(BF16)


def experts(tile, x, dy, gate, wg, wu, wd, before=None, filled=None, last=False, chunk=512):
    rows, width = x.shape
    hidden = gate.shape[1]
    full = pl.BlockSpec((rows, width), lambda i: (0, 0))
    part = pl.BlockSpec((rows, chunk), lambda i: (0, i))
    operands = [x, dy, gate, wg, wu, wd]
    in_specs = [
        full,
        full,
        part,
        *[pl.BlockSpec((chunk, width), lambda i: (i, 0))] * 3,
    ]
    aliases = {}
    if before is not None:
        operands += list(before)
        in_specs += [full] * 2
    if filled is not None:
        aliases = {len(operands): 2, len(operands) + 1: 3}
        operands += list(filled)
        in_specs += [pl.BlockSpec(memory_space=pl.ANY)] * 2
    return pl.pallas_call(
        functools.partial(expert_kernel, chunk, before is None, last),
        grid=(hidden // chunk,),
        in_specs=in_specs,
        out_specs=[
            full,
            full,
            pl.BlockSpec((rows, chunk), lambda i: (tile, i)),
            pl.BlockSpec((rows, 2 * chunk), lambda i: (tile, i)),
        ],
        out_shape=[
            *[jax.ShapeDtypeStruct((rows, width), BF16 if last else F32)] * 2,
            jax.ShapeDtypeStruct((2 * rows, hidden), BF16),
            jax.ShapeDtypeStruct((2 * rows, 2 * hidden), BF16),
        ],
        scratch_shapes=[pltpu.VMEM((rows, width), F32)] * (2 if last else 0),
        input_output_aliases=aliases,
        compiler_params=params(),
        name="experts",
        cost_estimate=pl.CostEstimate(
            flops=12 * rows * width * hidden,
            bytes_accessed=6 * width * hidden + 16 * rows * width,
            transcendentals=0,
        ),
    )(*operands)


def pick(i, values):
    result = values[0]
    for at, value in enumerate(values):
        if at and value != values[at - 1]:
            result = jnp.where(i >= at, value, result)
    return result


def gradient_kernel(jobs, lefts, rights, *refs):
    send_refs, keep_refs, right_refs = refs[:lefts], refs[lefts : 2 * lefts], refs[2 * lefts :]
    outs, (sent, got, send, recv) = right_refs[rights:-4], refs[-4:]
    d = lax.axis_index("dp")
    step = pl.program_id(0)
    count = len(jobs)

    @pl.when(step == 0)
    def _():
        barrier = pltpu.get_barrier_semaphore()
        pl.semaphore_signal(
            barrier, inc=1, device_id={"dp": flip(d, 1)}, device_id_type=pl.DeviceIdType.MESH
        )
        pl.semaphore_wait(barrier, 1)

    def copy(i):
        return pltpu.make_async_remote_copy(
            src_ref=sent.at[i],
            dst_ref=got.at[i],
            send_sem=send.at[i],
            recv_sem=recv.at[i],
            device_id={"dp": flip(d, 1)},
            device_id_type=pl.DeviceIdType.MESH,
        )

    for i, (left, right, _) in enumerate(jobs):

        @pl.when(step == i)
        def _(i=i, left=left, right=right):
            sent[i] = mm(send_refs[left][...], right_refs[right][...]).astype(BF16)
            copy(i).start()

        @pl.when(step == count + i)
        def _(i=i, left=left, right=right):
            value = mm(keep_refs[left][...], right_refs[right][...])
            copy(i).wait()
            value = value + got[i].astype(F32)
            half = value.shape[0] // 2
            side = 2 * (i // (count // 2))
            outs[side][...] = value[:half].astype(BF16)
            outs[side + 1][...] = value[half:].astype(BF16)


def gradients(jobs, send_lefts, keep_lefts, rights, ident, chunk=768):
    rows, tokens = keep_lefts[0].shape
    count = len(jobs)
    each = count // 2
    first = lambda i: (0, jnp.clip(i - count, 0, each - 1))
    second = lambda i: (0, jnp.maximum(i - count - each, 0))
    right_specs = []
    for r in range(len(rights)):
        blocks, at = [], None
        for _, right, block in jobs + jobs:
            at = block if right == r else at
            blocks.append(at)
        known = next(block for block in blocks if block is not None)
        blocks = tuple(known if block is None else block for block in blocks)
        right_specs.append(
            pl.BlockSpec((tokens, chunk), lambda i, blocks=blocks: (0, pick(i, blocks)))
        )
    left = pl.BlockSpec((rows, tokens), lambda i: (0, 0), pipeline_mode=pl.Buffered(1))
    return pl.pallas_call(
        functools.partial(gradient_kernel, jobs, len(keep_lefts), len(rights)),
        grid=(2 * count,),
        in_specs=[*[left] * (2 * len(keep_lefts)), *right_specs],
        out_specs=[
            pl.BlockSpec((rows // 2, chunk), at) for at in (first, first, second, second)
        ],
        out_shape=[jax.ShapeDtypeStruct((rows // 2, each * chunk), BF16)] * 4,
        scratch_shapes=[
            pltpu.VMEM((count, rows, chunk), BF16),
            pltpu.VMEM((count, rows, chunk), BF16),
            pltpu.SemaphoreType.DMA((count,)),
            pltpu.SemaphoreType.DMA((count,)),
        ],
        compiler_params=pltpu.CompilerParams(
            vmem_limit_bytes=56 * 2**20, collective_id=ident, has_side_effects=True
        ),
        name="gradients",
        cost_estimate=pl.CostEstimate(flops=10**9, bytes_accessed=10**6, transcendentals=0),
    )(*send_lefts, *keep_lefts, *rights)


def part_kernel(jobs, lefts, rights, keep, *refs):
    left_refs, right_refs, rest = refs[:lefts], refs[lefts : lefts + rights], refs[lefts + rights :]
    step = pl.program_id(0)
    each = len(jobs) // 2
    for i, (left, right, _) in enumerate(jobs):

        @pl.when(step == i)
        def _(i=i, left=left, right=right):
            side = i // each
            value = mm(left_refs[left][...], right_refs[right][...])
            if keep:
                value = value + rest[0][0].astype(F32)
                half = value.shape[0] // 2
                rest[1 + 2 * side][...] = value[:half].astype(BF16)
                rest[2 + 2 * side][...] = value[half:].astype(BF16)
            else:
                rest[0][0] = value.astype(BF16)


def gradient_parts(jobs, lefts, rights, got=None, chunk=768):
    rows, tokens = lefts[0].shape
    each = len(jobs) // 2
    first = lambda i: (0, jnp.minimum(i, each - 1))
    second = lambda i: (0, jnp.maximum(i - each, 0))
    whole = [pl.BlockSpec((1, rows, chunk), lambda i: (i // each, 0, i % each))]
    if got is None:
        out_specs = whole[0]
        out_shape = jax.ShapeDtypeStruct((2, rows, each * chunk), BF16)
    else:
        out_specs = [pl.BlockSpec((rows // 2, chunk), at) for at in (first, first, second, second)]
        out_shape = [jax.ShapeDtypeStruct((rows // 2, each * chunk), BF16)] * 4
    right_specs = []
    for r in range(len(rights)):
        at, blocks = None, []
        for _, right, block in jobs:
            at = block if right == r else at
            blocks.append(at)
        known = next(block for block in blocks if block is not None)
        blocks = tuple(known if block is None else block for block in blocks)
        right_specs.append(
            pl.BlockSpec((tokens, chunk), lambda i, blocks=blocks: (0, pick(i, blocks)))
        )
    return pl.pallas_call(
        functools.partial(part_kernel, jobs, len(lefts), len(rights), got is not None),
        grid=(2 * each,),
        in_specs=[
            *[pl.BlockSpec((rows, tokens), lambda i: (0, 0))] * len(lefts),
            *right_specs,
            *(() if got is None else whole),
        ],
        out_specs=out_specs,
        out_shape=out_shape,
        compiler_params=params(),
        name="gradient_parts",
        cost_estimate=pl.CostEstimate(
            flops=4 * each * rows * tokens * chunk,
            bytes_accessed=4 * each * (rows + tokens) * chunk,
            transcendentals=0,
        ),
    )(*lefts, *rights, *(() if got is None else (got,)))


EXPERT_JOBS = ((0, 0, 0), (0, 0, 1), (1, 1, 0), (2, 0, 2), (2, 0, 3), (3, 1, 1))


def flip(index, mask):
    for bit in (1, 2, 4):
        if mask & bit:
            index = index + bit - 2 * bit * (index // bit % 2)
    return index


def mix_kernel(
    dq_ref,
    o_ref,
    n_send,
    n_keep,
    d_send,
    d_keep,
    one_ref,
    two_ref,
    fa_keep,
    fa_got,
    fb_keep,
    fb_got,
    q_keep,
    q_send,
    o_keep,
    o_send,
    got_one,
    far_ref,
    got_two,
    both_ref,
    sent,
    got,
    halves,
    lasts,
    send,
    recv,
):
    d = lax.axis_index("dp")
    z = lax.axis_index("tensor")
    z_count = lax.axis_size("tensor")
    pairs = [{"dp": flip(d, bit)} for bit in (1, 2, 4)]
    others = [{"tensor": (z + m) % z_count} for m in range(1, z_count)]
    barrier = pltpu.get_barrier_semaphore()
    for peer in pairs + others:
        pl.semaphore_signal(barrier, inc=1, device_id=peer, device_id_type=pl.DeviceIdType.MESH)
    pl.semaphore_wait(barrier, len(pairs) + len(others))

    def start(src, dst, at, to):
        copy = pltpu.make_async_remote_copy(
            src_ref=src,
            dst_ref=dst,
            send_sem=send.at[at],
            recv_sem=recv.at[at],
            device_id=to,
            device_id_type=pl.DeviceIdType.MESH,
        )
        copy.start()
        return copy

    step_two = start(two_ref, got_two, 1, others[-1])
    rows = halves.shape[1]
    far_copies = []
    for side, (keep, arrived) in enumerate(((fa_keep, fa_got), (fb_keep, fb_got))):
        total = keep[rows:].astype(F32) + arrived[rows:].astype(F32)
        halves[side] = total.astype(BF16)
        far_copies.append(start(halves.at[side], lasts.at[side], 2 + side, pairs[2 - side]))

    columns = dq_ref.shape[1]
    chunk = columns // 4

    def at_chunk(i):
        return pl.ds(pl.multiple_of(i * chunk, chunk), chunk)

    sides = ((dq_ref, n_send, n_keep, q_keep, q_send), (o_ref, d_send, d_keep, o_keep, o_send))
    core_copies = []
    for side, (right, left, _, _, _) in enumerate(sides):

        def compute_send(i, carry, side=side, right=right, left=left):
            at = at_chunk(i)
            sent[side, :, at] = mm(left[...], right[:, at]).astype(BF16)
            return carry

        lax.fori_loop(0, 4, compute_send, 0)
        core_copies.append(start(sent.at[side], got.at[side], 4 + side, pairs[0]))
        if side == 0:
            step_two.wait()
            both_ref[...] = (one_ref[...].astype(F32) + got_two[...].astype(F32)).astype(BF16)
            step_one = start(both_ref, got_one, 0, others[-1])
    for side, (right, _, left, keep, away) in enumerate(sides):
        core_copies[side].wait()

        def compute_keep(i, carry, side=side, right=right, left=left, keep=keep, away=away):
            at = at_chunk(i)
            value = mm(left[...], right[:, at]) + got[side, :, at].astype(F32)
            half = value.shape[0] // 2
            keep[:, at] = value[:half].astype(BF16)
            away[:, at] = value[half:].astype(BF16)
            return carry

        lax.fori_loop(0, 4, compute_keep, 0)
    for side, (keep, arrived) in enumerate(((fa_keep, fa_got), (fb_keep, fb_got))):
        far_copies[side].wait()
        total = keep[:rows].astype(F32) + arrived[:rows].astype(F32) + lasts[side].astype(F32)
        far_ref[side] = total.astype(BF16)
    step_one.wait()


def mix(dq, o, lefts, dkv_one, dkv_two, far_parts):
    rows2, columns = far_parts[0].shape
    rows = rows2 // 2
    wide = dq.shape[1]
    vmem = pl.BlockSpec(memory_space=pltpu.VMEM)
    half = jax.ShapeDtypeStruct((rows2, wide), BF16)
    block = jax.ShapeDtypeStruct(dkv_one.shape, BF16)
    return pl.pallas_call(
        mix_kernel,
        in_specs=[vmem] * 12,
        out_specs=[vmem] * 6,
        out_shape=[half] * 4 + [block] + [jax.ShapeDtypeStruct((2, rows, columns), BF16)],
        scratch_shapes=[
            pltpu.VMEM(block.shape, BF16),
            pltpu.VMEM(block.shape, BF16),
            pltpu.VMEM((2, 2 * rows2, wide), BF16),
            pltpu.VMEM((2, 2 * rows2, wide), BF16),
            pltpu.VMEM((2, rows, columns), BF16),
            pltpu.VMEM((2, rows, columns), BF16),
            pltpu.SemaphoreType.DMA((6,)),
            pltpu.SemaphoreType.DMA((6,)),
        ],
        compiler_params=pltpu.CompilerParams(
            vmem_limit_bytes=56 * 2**20, collective_id=2, has_side_effects=True
        ),
        name="mix",
    )(dq, o, *lefts, dkv_one, dkv_two, *far_parts)


def finish_kernel(
    dx_ref,
    out_ref,
    q_keep,
    q_send,
    o_keep,
    o_send,
    s_send,
    s_keep,
    back_ref,
    back_out_ref,
    q_ref,
    o_ref,
    s_ref,
    q_got,
    o_got,
    q_half,
    o_half,
    q_last,
    o_last,
    s_got,
    s_half,
    s_got2,
    s_quarter,
    s_last,
    z_mine,
    z_got,
    k_mine,
    k_half,
    k_got,
    deal_send,
    deal_recv,
    send,
    recv,
):
    d = lax.axis_index("dp")
    z = lax.axis_index("tensor")
    count = dx_ref.shape[0]
    z_count = z_mine.shape[0]
    barrier = pltpu.get_barrier_semaphore()
    for p in range(1, count):
        pl.semaphore_signal(
            barrier, inc=1, device_id={"dp": flip(d, p)}, device_id_type=pl.DeviceIdType.MESH
        )
    for m in range(1, z_count):
        pl.semaphore_signal(
            barrier, inc=1, device_id={"tensor": flip(z, m)}, device_id_type=pl.DeviceIdType.MESH
        )
    pl.semaphore_wait(barrier, count - 1 + z_count - 1)

    def start(src, dst, at, to):
        copy = pltpu.make_async_remote_copy(
            src_ref=src,
            dst_ref=dst,
            send_sem=send.at[at],
            recv_sem=recv.at[at],
            device_id=to,
            device_id_type=pl.DeviceIdType.MESH,
        )
        copy.start()
        return copy

    one, two, four = [{"dp": flip(d, bit)} for bit in (1, 2, 4)]
    q_one = start(q_send, q_got, 1, two)
    o_one = start(o_send, o_got, 2, four)
    s_one = start(s_send, s_got, 0, one)
    back_ref[d] = dx_ref[d]
    back_out_ref[d] = out_ref[d]
    rows = q_last.shape[0]
    s_one.wait()
    total = s_keep[...].astype(F32) + s_got[...].astype(F32)
    s_keep2 = total[: 2 * rows]
    s_half[...] = total[2 * rows :].astype(BF16)
    s_two = start(s_half, s_got2, 3, four)
    q_one.wait()
    q_half[...] = (q_keep[rows:].astype(F32) + q_got[rows:].astype(F32)).astype(BF16)
    q_two = start(q_half, q_last, 4, four)
    o_one.wait()
    o_half[...] = (o_keep[rows:].astype(F32) + o_got[rows:].astype(F32)).astype(BF16)
    o_two = start(o_half, o_last, 5, two)
    s_two.wait()
    total = s_keep2 + s_got2[...].astype(F32)
    s_quarter[...] = total[rows:].astype(BF16)
    s_three = start(s_quarter, s_last, 6, two)
    deals = []
    for i, (src, dst) in enumerate(((dx_ref, back_ref), (out_ref, back_out_ref))):
        for p in range(1, count):
            copy = pltpu.make_async_remote_copy(
                src_ref=src.at[flip(d, p)],
                dst_ref=dst.at[d],
                send_sem=deal_send.at[i, p - 1],
                recv_sem=deal_recv.at[i, p - 1],
                device_id={"dp": flip(d, p)},
                device_id_type=pl.DeviceIdType.MESH,
            )
            copy.start()
            deals.append(copy)
    s_own = total[:rows]
    s_three.wait()
    s_own = s_own + s_last[...].astype(F32)
    k_mine[...] = s_own.astype(BF16)
    k_near = start(k_mine, k_got.at[0], 7, {"tensor": flip(z, 1)})
    finals = []
    part = q_ref.shape[1]
    for two_copy, keep, got, last, side in (
        (q_two, q_keep, q_got, q_last, 0),
        (o_two, o_keep, o_got, o_last, 1),
    ):
        two_copy.wait()
        total = (
            keep[:rows].astype(F32) + got[:rows].astype(F32) + last[...].astype(F32)
        )
        for i in range(z_count):
            block = total[:, i * part : (i + 1) * part]
            z_mine[i, :, side * part : (side + 1) * part] = block.astype(BF16)
    for m in range(1, z_count):
        finals.append(start(z_mine.at[flip(z, m)], z_got.at[m - 1], 8 + m, {"tensor": flip(z, m)}))
    k_near.wait()
    s_own = s_own + k_got[0].astype(F32)
    k_half[...] = s_own.astype(BF16)
    k_far = start(k_half, k_got.at[1], 8, {"tensor": flip(z, 2)})
    for copy in finals:
        copy.wait()
    total = z_mine[z].astype(F32)
    for m in range(z_count - 1):
        total = total + z_got[m].astype(F32)
    q_ref[...] = total[:, :part]
    o_ref[...] = total[:, part:]
    k_far.wait()
    s_ref[...] = s_own + k_got[1].astype(F32)
    for copy in deals:
        copy.wait()


def finish(dx, out, q_keep, q_send, o_keep, o_send, s_send, s_keep, z_count):
    count = dx.shape[0]
    rows = q_keep.shape[0] // 2
    columns = q_keep.shape[1]
    small = s_keep.shape[1]
    part = columns // z_count
    vmem = pl.BlockSpec(memory_space=pltpu.VMEM)
    dma = pltpu.SemaphoreType.DMA
    return pl.pallas_call(
        finish_kernel,
        in_specs=[vmem] * 8,
        out_specs=[vmem] * 5,
        out_shape=[
            jax.ShapeDtypeStruct(dx.shape, BF16),
            jax.ShapeDtypeStruct(dx.shape, BF16),
            jax.ShapeDtypeStruct((rows, part), F32),
            jax.ShapeDtypeStruct((rows, part), F32),
            jax.ShapeDtypeStruct((rows, small), F32),
        ],
        scratch_shapes=[
            pltpu.VMEM((2 * rows, columns), BF16),
            pltpu.VMEM((2 * rows, columns), BF16),
            pltpu.VMEM((rows, columns), BF16),
            pltpu.VMEM((rows, columns), BF16),
            pltpu.VMEM((rows, columns), BF16),
            pltpu.VMEM((rows, columns), BF16),
            pltpu.VMEM((4 * rows, small), BF16),
            pltpu.VMEM((2 * rows, small), BF16),
            pltpu.VMEM((2 * rows, small), BF16),
            pltpu.VMEM((rows, small), BF16),
            pltpu.VMEM((rows, small), BF16),
            pltpu.VMEM((z_count, rows, 2 * part), BF16),
            pltpu.VMEM((z_count - 1, rows, 2 * part), BF16),
            pltpu.VMEM((rows, small), BF16),
            pltpu.VMEM((rows, small), BF16),
            pltpu.VMEM((2, rows, small), BF16),
            dma((2, count - 1)),
            dma((2, count - 1)),
            dma((7 + 2 * z_count,)),
            dma((7 + 2 * z_count,)),
        ],
        compiler_params=pltpu.CompilerParams(
            vmem_limit_bytes=56 * 2**20, collective_id=0, has_side_effects=True
        ),
        name="finish",
    )(dx, out, q_keep, q_send, o_keep, o_send, s_send, s_keep)


def assemble_kernel(a_keep, a_got, b_keep, b_got, far_ref, gate_ref, up_ref, down_ref):
    count, rows, columns = gate_ref.shape
    a = a_keep[...] + a_got[...].astype(F32) + far_ref[0].astype(F32)
    b = b_keep[...] + b_got[...].astype(F32) + far_ref[1].astype(F32)
    gate = jnp.concatenate([a[:, :512], a[:, 1024:1536], b[:, 512:1024]], axis=1)
    up = jnp.concatenate([a[:, 512:1024], b[:, :512], b[:, 1024:1536]], axis=1)
    down = jnp.concatenate([a[:, 1536:], b[:, 1536:]], axis=1)
    pad = jnp.zeros((256 - rows, down.shape[1]), F32)
    down = jnp.concatenate([down, pad], axis=0).T[:, :rows]
    for e in range(count):
        at = slice(e * columns, (e + 1) * columns)
        gate_ref[e] = gate[:, at]
        up_ref[e] = up[:, at]
        down_ref[e] = down[at]


def assemble(own, far_sum, count):
    rows, columns = own[0].shape
    part = columns * 2 // (3 * count)
    vmem = pl.BlockSpec(memory_space=pltpu.VMEM)
    wide = jax.ShapeDtypeStruct((count, rows, part), F32)
    return pl.pallas_call(
        assemble_kernel,
        in_specs=[vmem] * 5,
        out_specs=[vmem] * 3,
        out_shape=[wide, wide, jax.ShapeDtypeStruct((count, part, rows), F32)],
        compiler_params=params(),
        name="assemble",
    )(*own, far_sum)


def turn_kernel(orders, d_ref, *refs):
    tiles = len(refs) - 1 - len(orders)
    scratch_ref = refs[-1]
    step = pl.program_id(0)
    for t in range(tiles):

        @pl.when(step == t)
        def _(t=t):
            scratch_ref[...] = refs[t][...].T

    for order, out_ref in zip(orders, refs[tiles:-1]):
        size = out_ref.shape[0] // len(order)
        for i, p in enumerate(order):
            block = jnp.bitwise_xor(d_ref[0], p)
            at = pl.multiple_of(block * size, size)
            out_ref[i * size : (i + 1) * size, :] = scratch_ref[pl.ds(at, size), :]


def turn(d, tiles, orders, blocks):
    rows, width = tiles[0].shape
    size = width // blocks
    return pl.pallas_call(
        functools.partial(turn_kernel, orders),
        grid_spec=pltpu.PrefetchScalarGridSpec(
            num_scalar_prefetch=1,
            grid=(len(tiles),),
            in_specs=[pl.BlockSpec((rows, width), lambda t, s: (0, 0))] * len(tiles),
            out_specs=[
                pl.BlockSpec((len(order) * size, rows), lambda t, s: (0, t)) for order in orders
            ],
            scratch_shapes=[pltpu.VMEM((width, rows), BF16)],
        ),
        out_shape=[
            jax.ShapeDtypeStruct((len(order) * size, rows * len(tiles)), BF16) for order in orders
        ],
        compiler_params=params(),
        name="turn",
        cost_estimate=pl.CostEstimate(
            flops=0, bytes_accessed=6 * rows * width * len(tiles), transcendentals=0
        ),
    )(d, *tiles)


def tie(*values):
    return lax.optimization_barrier(values)


def row_major(x):
    return with_layout_constraint(x, Layout(major_to_minor=tuple(range(x.ndim))))


def per_device(
    tokens,
    perm,
    routes,
    gates,
    lengths,
    cotangent,
    gain_attn,
    w_query,
    w_keyval,
    w_out,
    gain_moe,
    w_gate,
    w_up,
    w_down,
):
    dp_count = lax.axis_size("dp")
    tensor_count = lax.axis_size("tensor")
    d = lax.axis_index("dp")
    z = lax.axis_index("tensor")
    rows, width = tokens.shape
    group_rows = perm.shape[0]
    share = rows // dp_count
    top = routes.shape[1]
    experts_n, _, part_hidden = w_gate.shape
    hidden = experts_n * part_hidden
    capacity = 9 * group_rows * top // (8 * experts_n)
    kv_heads = w_keyval.shape[1] // (2 * HD)
    query_cols = w_query.shape[1]
    team = 8
    teams = [[t * team + i for i in range(team)] for t in range(dp_count // team)]
    teams = None if len(teams) == 1 else teams
    piece_rows = width // team
    member = d % team

    def z_move(x, pairs):
        return lax.ppermute(x, "tensor", pairs)

    def dp_move(x, bit):
        return lax.ppermute(x, "dp", [(i, i ^ bit) for i in range(dp_count)])

    near, far, across = [[(i, i ^ m) for i in range(tensor_count)] for m in (1, 2, 3)]
    up_one, up_two = [[(i, i + m) for i in range(tensor_count - m)] for m in (1, 2)]

    def deal(x):
        return lax.all_to_all(
            x.reshape(dp_count, share, x.shape[1]), "dp", split_axis=0, concat_axis=0, tiled=True
        ).reshape(rows, x.shape[1])

    def team_gather(x):
        return lax.all_gather(x, "dp", axis=0, tiled=True, axis_index_groups=teams)

    def flat(w):
        return w.transpose(0, 2, 1).reshape(hidden, w.shape[1])

    own_perm = lax.dynamic_slice_in_dim(perm, z * rows, rows, 0)
    own_routes = lax.dynamic_slice_in_dim(routes, z * rows, rows, 0)
    dest = own_perm // group_rows
    place = own_perm % rows
    row_index = jnp.arange(rows, dtype=jnp.int32)
    lower = (row_index[:, None] > row_index[None, :]).astype(BF16)
    dest_hot = (dest[:, None] == jnp.arange(dp_count, dtype=jnp.int32)[None, :]).astype(BF16)
    earlier = jnp.sum(mm(lower, dest_hot) * dest_hot.astype(F32), axis=1).astype(jnp.int32)
    slot = dest * share + earlier
    pack = (row_index[:, None] == slot[None, :]).astype(BF16)
    meta = jnp.concatenate(
        [
            (place // 16)[:, None].astype(BF16),
            (place % 16)[:, None].astype(BF16),
            own_routes.astype(BF16),
            gates,
            jnp.zeros((rows, META - 2 - 2 * top), BF16),
        ],
        axis=1,
    )
    packed = mm(pack, jnp.concatenate([tokens, meta], axis=1)).astype(BF16)
    wg_own, wu_own = flat(w_gate), flat(w_up)
    wd_own = w_down.reshape(hidden, width)
    out_rows = query_cols // team
    hidden_piece = hidden // team

    def piece(w, count):
        return lax.dynamic_slice_in_dim(w, member * count, count, 0)

    wg_piece, wu_piece, wd_piece = [piece(w, hidden_piece) for w in (wg_own, wu_own, wd_own)]
    packed_dy = mm(pack, cotangent).astype(BF16)
    packed, packed_dy = tie(packed, packed_dy)
    arrived, wq_z, wo_z = open_moves(
        packed.reshape(dp_count, share, width + META),
        piece(w_query, piece_rows),
        piece(w_out, out_rows),
        tensor_count,
    )
    arrived, wg_piece, wu_piece = tie(arrived.reshape(rows, width + META), wg_piece, wu_piece)
    wg_moved, wu_moved = z_move(wg_piece, far), z_move(wu_piece, far)
    wq_all = team_gather(wq_z).reshape(team, tensor_count, piece_rows, query_cols)
    wo_all = team_gather(wo_z).reshape(team, tensor_count, out_rows, width)
    wo = wo_all.transpose(1, 0, 2, 3).reshape(tensor_count * query_cols, width)

    meta_in = arrived[:, width:].astype(F32)
    place_in = (meta_in[:, 0] * 16.0 + meta_in[:, 1]).astype(jnp.int32)
    unpack = (row_index[:, None] == place_in[None, :]).astype(BF16)
    dealt = mm(unpack, arrived)
    x_rows = dealt[:, :width]
    meta_rows = dealt[:, width:]

    expert_ids = jnp.arange(experts_n, dtype=jnp.int32).astype(F32)
    route_rows = meta_rows[:, 2 : 2 + top]
    gate_rows = meta_rows[:, 2 + top : 2 + 2 * top]
    hot = route_rows[:, :, None] == expert_ids[None, None, :]
    routed = jnp.sum(hot.astype(F32), axis=1)
    counts = jnp.pad(jnp.sum(routed, axis=0)[None, :], ((0, 7), (0, HD - experts_n)))

    seq_lengths = lengths[0]
    seq_index = jnp.arange(seq_lengths.shape[0], dtype=jnp.int32)
    seq_ends = jnp.sum(
        jnp.where(seq_index[None, :] <= seq_index[:, None], seq_lengths[None, :], 0), axis=1
    ).astype(jnp.int32)
    global_row = z * rows + row_index
    start = jnp.max(
        jnp.where(global_row[:, None] >= seq_ends[None, :], seq_ends[None, :], 0), axis=1
    ).astype(jnp.int32)
    offset = (global_row - start).astype(F32)
    frequency = ROPE_BASE ** (-2.0 * jnp.arange(HD // 2, dtype=F32) / HD)
    angles = offset[:, None] * frequency[None, :]
    cosine, sine = jnp.cos(angles), jnp.sin(angles)
    cos_full = jnp.concatenate([cosine, cosine], axis=1)
    sin_full = jnp.concatenate([-sine, sine], axis=1)
    start = start[:, None]
    z_arg = z.astype(jnp.int32)[None]

    inv_one = lax.rsqrt(jnp.mean(x_rows * x_rows, axis=1, keepdims=True) + EPS)
    n1 = (x_rows * inv_one * gain_attn).astype(BF16)
    weight = jnp.sum(jnp.where(hot, gate_rows[:, :, None], 0.0), axis=1)
    marks = jnp.pad(
        jnp.concatenate([routed, weight], axis=1).astype(BF16), ((0, 0), (0, HD - 2 * experts_n))
    )
    kv, kv_one, kv_two, counts, marks_near, arrived_dy = keyval(
        n1,
        w_keyval,
        cos_full,
        sin_full,
        counts,
        marks,
        packed_dy.reshape(dp_count, share, width),
        tensor_count,
    )
    arrived_dy = arrived_dy.reshape(rows, width)
    kv, n1, wg_moved, wu_moved = tie(kv, n1, wg_moved, wu_moved)

    dy_rows = mm(unpack, arrived_dy).astype(BF16)
    n1, dy_rows = tie(n1, dy_rows)
    q = project_query(z_arg, n1, wq_all, cos_full, sin_full)
    dy_near = z_move(dy_rows, near)
    kvs = (kv_two, kv_one, kv)
    o, lse = attend(z_arg, start, q, kvs, kv_heads)
    o, wd_piece, dy_near, counts, weight, marks_near = tie(
        o, wd_piece, dy_near, counts, weight, marks_near
    )

    def kept_gates(routed, weight, at):
        block = (z - 1 - jnp.arange(tensor_count, dtype=jnp.int32)) % tensor_count
        base = jnp.sum(
            jnp.where((block < at)[:, None], counts[:, 0, :experts_n], 0.0), axis=0
        )
        position = mm(lower, routed.astype(BF16)) + base[None, :]
        weight = jnp.where(position < capacity, weight, 0.0).astype(BF16)
        return row_major(jnp.repeat(weight, part_hidden, axis=1))

    gate_own = kept_gates(routed, weight, z)
    marks_near = marks_near.astype(F32)
    gate_near = kept_gates(
        marks_near[:, :experts_n], marks_near[:, experts_n : 2 * experts_n], z + 1 - 2 * (z % 2)
    )
    wg_far = team_gather(wg_moved)
    wu_far = team_gather(wu_moved)
    h = x_rows + mm(o, wo)
    inv_two = lax.rsqrt(jnp.mean(h * h, axis=1, keepdims=True) + EPS)
    n2 = (h * inv_two * gain_moe).astype(BF16)

    halving = dp_count == 8
    d_arg = d.astype(jnp.int32)[None]
    out_w = width // dp_count
    orders_a = ((1, 5, 3, 7), (0, 4, 2, 6))
    orders_b = ((1, 3, 5, 7), (0, 2, 4, 6))

    def turned(tiles, *orders):
        if halving:
            return turn(d_arg, tiles, orders, dp_count)
        return [jnp.concatenate(tiles, axis=0).T] * len(orders)

    def dp_sum(x):
        return lax.psum_scatter(x, "dp", scatter_dimension=0, tiled=True)

    def first_moves(parts):
        return parts[0], dp_move(parts[1], xy[0]), parts[2], dp_move(parts[3], yx[0])

    def second_moves(moved):
        halves = []
        for keep, got, bit in ((*moved[:2], xy[1]), (*moved[2:], yx[1])):
            x = keep.astype(F32) + got.astype(F32)
            half = x.shape[0] // 2
            halves += [x[:half], dp_move(x[half:].astype(BF16), bit)]
        return halves

    def expert_lefts(n_a, d_a, keep):
        return n_a[keep], d_a[keep], n_a[2 + keep], d_a[2 + keep]

    xy, yx = (2, 4), (4, 2)
    n2_near = z_move(n2, near)
    y, dn2, *own_grads = experts(0, n2, dy_rows, gate_own, wg_own, wu_own, wd_own)
    y, n1 = tie(y, n1)
    n1_t = turned((n1,), *orders_a, *orders_b)
    n2_near, y, wd_piece = tie(n2_near, y, wd_piece)
    n2_a = turned((n2, n2_near), *orders_a, *orders_b)
    dy_near, *turns = tie(dy_near, *n2_a, *n1_t)
    n2_a, n1_t = turns[:4], turns[4:]
    wd_moved = z_move(wd_piece, far)
    yn, dnn, *own_grads = experts(
        1, n2_near, dy_near, gate_near, wg_own, wu_own, wd_own, filled=own_grads
    )
    yn, wd_moved, *own_grads = tie(yn, wd_moved, *own_grads)
    wd_far = team_gather(wd_moved)
    dy_a = turned((dy_rows, dy_near), *orders_a, *orders_b)
    if halving:
        own = gradients(
            EXPERT_JOBS,
            expert_lefts(n2_a, dy_a, 0),
            expert_lefts(n2_a, dy_a, 1),
            own_grads[::-1],
            3,
        )
        wg_far, *own = tie(wg_far, *own)
        own = first_moves(own)
    yn, dnn, *far_grads = experts(
        1, n2_near, dy_near, gate_near, wg_far, wu_far, wd_far, (yn, dnn), last=True
    )
    dnn_moved = z_move(dnn, near)
    y, dn2, *far_grads = experts(
        0, n2, dy_rows, gate_own, wg_far, wu_far, wd_far, (y, dn2), far_grads
    )
    if halving:
        far_grads = far_grads[::-1]
        far_sent = gradient_parts(EXPERT_JOBS, expert_lefts(n2_a, dy_a, 0), far_grads)
        dnn_moved, far_sent, *own = tie(dnn_moved, far_sent, *own)
        got = dp_move(far_sent, 1)
        own = second_moves(own)
    yn, dnn_moved = tie(yn, dnn_moved)
    yn_moved = z_move(yn, near)
    dn2 = dn2 + dnn_moved.astype(F32)

    gain_two_part = jnp.sum(dn2 * h * inv_two, axis=0)
    u2 = dn2 * gain_moe
    dh = dy_rows.astype(F32) + inv_two * (
        u2 - h * inv_two * inv_two * jnp.mean(u2 * h, axis=1, keepdims=True)
    )
    dhb = dh.astype(BF16)
    do = mm_nt(dhb, wo).astype(BF16)
    if halving:
        far_w = gradient_parts(EXPERT_JOBS, expert_lefts(n2_a, dy_a, 1), far_grads, got)
        do, *both = tie(do, *far_w, *own)
        far_w, own = both[:4], both[4:]
        far_w = first_moves(far_w)
    dq, dkv_two, dkv_one, dkv = attend_back(
        z_arg, start, q, o, do, lse, cos_full, sin_full, kvs, kv_heads
    )
    dhb_t = turned((dhb,), *orders_b)
    if halving:
        dq, *far_w = tie(dq, *far_w)
        *parts, dkv_sum, far_sum = mix(
            dq, o, (n1_t[0], n1_t[1], *dhb_t), dkv_one, dkv_two, far_w
        )
        far_sum = z_move(far_sum, far)
        dkv_sum, yn_moved = tie(dkv_sum, yn_moved)
    else:
        dkv_one = z_move(dkv_one, [(b, a) for a, b in up_one])
        dkv_two = z_move(dkv_two, [(b, a) for a, b in up_two])
        dkv_sum = dkv_one.astype(F32) + dkv_two.astype(F32)
        sum_q, sum_o = [
            dp_sum(mm_tn(a, b).astype(BF16)).astype(F32) for a, b in ((n1, dq), (dhb, o))
        ]
    dkv = dkv + dkv_sum.astype(F32)

    def unrotate(u):
        swapped = jnp.concatenate([u[:, HD // 2 :], u[:, : HD // 2]], axis=1)
        return u * cos_full - swapped * sin_full

    dkv = jnp.concatenate(
        [unrotate(dkv[:, i * HD : (i + 1) * HD]) for i in range(kv_heads)]
        + [dkv[:, kv_heads * HD :]],
        axis=1,
    ).astype(BF16)
    dn1 = project_back(z_arg, dq, wq_all, dkv, w_keyval)
    gain_one_part = jnp.sum(dn1 * x_rows * inv_one, axis=0)
    u1 = dn1 * gain_attn
    dx = dh + inv_one * (
        u1 - x_rows * inv_one * inv_one * jnp.mean(u1 * x_rows, axis=1, keepdims=True)
    )

    result = h + y + yn_moved.astype(F32)
    result_out = mm_tn(unpack, result.astype(BF16)).astype(BF16)

    if halving:
        sum_gate, sum_up, sum_down = assemble(own, far_sum, experts_n)
    else:
        lefts = (n2_a[0], dy_a[0])
        far_sums = [dp_sum(mm(a, b).astype(BF16)) for a, b in zip(lefts, far_grads[::-1])]
        own_sums = [dp_sum(mm(a, b).astype(BF16)) for a, b in zip(lefts, own_grads[::-1])]
        sum_gu, sum_down = [
            a.astype(F32) + z_move(b, far).astype(F32) for a, b in zip(own_sums, far_sums)
        ]
        sum_gu = sum_gu.reshape(out_w, hidden // 512, 2, 512)
        sum_gate, sum_up = [
            sum_gu[:, :, i].reshape(out_w, experts_n, part_hidden).transpose(1, 0, 2) for i in (0, 1)
        ]
        sum_down = sum_down.reshape(out_w, experts_n, part_hidden).transpose(1, 2, 0)

    gains = jnp.stack([gain_one_part, gain_two_part])

    def gain_columns(order):
        blocks = gains.reshape(2, dp_count, out_w)
        if halving:
            blocks = jnp.stack(
                [lax.dynamic_index_in_dim(blocks, d ^ p, 1, keepdims=False) for p in order], 1
            )
        return jnp.pad(blocks.reshape(2, -1).T, ((0, 0), (dkv.shape[1], HD - 2)))

    columns = [gain_columns(order) for order in orders_b]
    dkv_wide = jnp.pad(dkv, ((0, 0), (0, HD)))
    if halving:
        kv_send, kv_keep = [
            (mm(left, dkv_wide) + column).astype(BF16) for left, column in zip(n1_t[2:], columns)
        ]
        dx_out = mm_tn(unpack, dx.astype(BF16)).astype(BF16).reshape(dp_count, share, width)
        back, back_out, sum_query, sum_out, small = finish(
            dx_out,
            result_out.reshape(dp_count, share, width),
            *parts,
            kv_send,
            kv_keep,
            tensor_count,
        )
        grad_tokens = mm_tn(pack, back.reshape(rows, width)).astype(BF16)
        outputs = mm_tn(pack, back_out.reshape(rows, width)).astype(BF16)
    else:
        outputs = mm_tn(pack, deal(result_out)).astype(BF16)
        grad_tokens = mm_tn(pack, deal(mm_tn(unpack, dx.astype(BF16)).astype(BF16))).astype(BF16)
        small = dp_sum((mm(n1_t[3], dkv_wide) + columns[0]).astype(BF16))
        small = small.astype(F32) + sum(
            z_move(small, move).astype(F32) for move in (near, far, across)
        )

        def z_block(x, m):
            return lax.dynamic_slice_in_dim(x, (z ^ m) * query_cols, query_cols, 1)

        both = [jnp.concatenate([z_block(sum_q, m), z_block(sum_o, m)], axis=1) for m in range(4)]
        total = both[0] + sum(
            z_move(part.astype(BF16), move).astype(F32)
            for part, move in zip(both[1:], (near, far, across))
        )
        sum_query, sum_out = total[:, :query_cols], total[:, query_cols:]
    sum_out = sum_out.T
    kv_cols = w_keyval.shape[1]
    return (
        outputs,
        grad_tokens,
        small[:, kv_cols],
        sum_query,
        small[:, :kv_cols],
        sum_out,
        small[:, kv_cols + 1],
        sum_gate,
        sum_up,
        sum_down,
    )


def solution(mesh):
    in_specs = (
        P(("dp", "tensor"), None),
        P("dp"),
        P("dp", None),
        P(("dp", "tensor"), None),
        P("dp", None),
        P(("dp", "tensor"), None),
        P(),
        P(None, "tensor"),
        P(),
        P("tensor", None),
        P(),
        P(None, None, "tensor"),
        P(None, None, "tensor"),
        P(None, "tensor", None),
    )
    out_specs = (
        P(("dp", "tensor"), None),
        P(("dp", "tensor"), None),
        P("dp"),
        P("dp", "tensor"),
        P("dp", None),
        P("tensor", "dp"),
        P("dp"),
        P(None, "dp", "tensor"),
        P(None, "dp", "tensor"),
        P(None, "tensor", "dp"),
    )
    return jax.shard_map(
        per_device, mesh=mesh, in_specs=in_specs, out_specs=out_specs, check_vma=False
    )
```
